128 devices in a mesh: aux: 8 (over y, x_lo), row: 8 (over z, core), col: 2 (over x_hi).
Axes of the slice: x: 4 (x_hi: 2, x_lo: 2; x = x_hi * 2 + x_lo), y: 4, z: 4, core: 2. Of those that a mesh axis runs over, the one named last changes fastest.
Arguments:
- b_tensor: bfloat16 [16, 6144, 1024], P('aux', 'row', 'col'), may hold values from -0.046875 to 0.046875
- hcore: float32 [6144, 6144], P('row', ('aux', 'col')), may hold values from -0.078125 to 0.078125
- c_occ: float32 [6144, 1024], P('row'), may hold values from -6 to 6
- c_virt: float32 [6144, 5120], P(('aux', 'col')), may hold values from -6 to 6
- eps_occ: float32 [1024], P('row'), may hold values from -3 to -0.5
- eps_virt: float32 [5120], P(('aux', 'col')), may hold values from 0.5 to 3
Outputs:
- c_new: float32 [6144, 1024], P(('aux', 'col'), 'row')
The draws below stay inside these ranges and needn't reach their ends.
All inputs are finite; a program needn't handle non-finite values.
Results may differ from the reference program's by a relative error of at most 0.0003.
Values may be sent and summed in bfloat16 or wider, within the bound.
A program may use at most 128 MiB of HBM per device.

```python
import jax
import jax.numpy as jnp
from jax import lax

N = 6144
O = 1024
TAYLOR = 8
V = 5120
AUXW = 16


def block_levels(key, extent, pieces, smallest, high):
    loudness = 1.0
    for dim, shards_of in pieces:
        steps = jax.random.uniform(jax.random.fold_in(jax.random.fold_in(key, 6), dim), (shards_of,), jnp.float32, smallest / len(pieces), high / len(pieces))
        loudness = loudness * jnp.repeat(jnp.exp(steps), extent[dim] // shards_of).reshape((-1,) + (1,) * (len(extent) - 1 - dim))
    return loudness


def noise(rng, extent, deviation, bound, shards=(), kind=jnp.bfloat16):
    values = jax.random.normal(rng, extent, jnp.float32) * deviation
    if len(shards) > 0:
        values = block_levels(rng, extent, shards, -0.22, 0.18) * values
    return jnp.clip(values, min=-bound, max=bound).astype(kind)


def setup_inputs(seed: int = 0) -> dict:
    key_list = jax.random.split(jax.random.key(seed), 7)
    b_tensor = noise(key_list[0], (AUXW, N, O), (AUXW * O) ** -0.5, 0.046875, ((0, 8), (1, 8), (2, 2)))
    hcore = noise(key_list[1], (N, N), N ** -0.5, 0.078125, ((0, 8), (1, 16)), jnp.float32)
    c_occ = noise(key_list[2], (N, O), 1.0, 6.0, ((0, 8),), jnp.float32)
    c_virt = noise(key_list[3], (N, V), 1.0, 6.0, ((0, 16),), jnp.float32)
    eps_occ = jnp.clip(-3.0 + 2.5 * jax.random.uniform(key_list[4], (O,), jnp.float32) ** block_levels(key_list[4], (O,), ((0, 8),), -0.2, 0.2), -3.0, -0.5)
    eps_virt = jnp.clip(0.5 + 2.5 * jax.random.uniform(key_list[5], (V,), jnp.float32) ** block_levels(key_list[5], (V,), ((0, 16),), -0.2, 0.2), 0.5, 3.0)
    return {"b_tensor": b_tensor, "hcore": hcore, "c_occ": c_occ, "c_virt": c_virt, "eps_occ": eps_occ, "eps_virt": eps_virt}


rotation_scale = 0.03

def reference(b_tensor, hcore, c_occ, c_virt, eps_occ, eps_virt):
    high = lax.Precision.HIGHEST

    def add_slab(total, slab):
        return (total + jnp.dot(slab, slab.T, preferred_element_type=jnp.float32), None)
    exchange, _ = lax.scan(add_slab, jnp.zeros((N, N), jnp.float32), b_tensor)
    fock = hcore - exchange
    occ_image = jnp.dot(fock.T, c_occ, precision=high)
    gradient = jnp.dot(c_virt.T, occ_image, precision=high)
    scaled = gradient / (eps_virt[:, None] - eps_occ[None, :])
    meansq = jnp.sum(scaled * scaled) / (V * O)
    kappa = rotation_scale * scaled / jnp.sqrt(meansq + 1e-06)
    occ_sum = jnp.eye(O, dtype=jnp.float32)
    virt_term = kappa
    virt_sum = kappa
    occ_term = occ_sum
    for order in range(2, TAYLOR + 1):
        if order % 2 == 0:
            occ_term = -jnp.dot(kappa.T, virt_term, precision=high) / float(order)
            occ_sum = occ_sum + occ_term
        else:
            virt_term = jnp.dot(kappa, occ_term, precision=high) / float(order)
            virt_sum = virt_sum + virt_term
    return jnp.dot(c_occ, occ_sum, precision=high) + jnp.dot(c_virt, virt_sum, precision=high)
```

```python
import functools

import jax
import jax.numpy as jnp
from jax import lax
from jax.experimental import pallas as pl
from jax.experimental.pallas import tpu as pltpu
from jax.sharding import PartitionSpec as P

ROTATION_SCALE = 0.03
MESH = pl.DeviceIdType.MESH
F32 = jnp.float32
BF16 = jnp.bfloat16
XY = ("xa", "xb", "ya", "yb")
ROW = ("za", "zb", "cc")
VMEM_LIMIT = 60 * 1024 * 1024


class Place:
    def __init__(self):
        aux, row, col = (lax.axis_index(n) for n in ("aux", "row", "col"))
        y, xl = aux // 2, aux % 2
        z, core = row // 2, row % 2
        self.aux, self.row, self.col = aux, row, col
        self.bit = {
            "xa": (xl + col) % 2, "xb": col,
            "ya": (y + y // 2) % 2, "yb": y // 2,
            "za": (z + z // 2) % 2, "zb": z // 2,
            "cc": core,
        }
        self.partner = {
            "xa": (aux + 1 - 2 * xl, row, col),
            "xb": (aux + 1 - 2 * xl, row, 1 - col),
            "ya": (aux + 2 - 4 * (y % 2), row, col),
            "yb": (2 * (3 - y) + xl, row, col),
            "za": (aux, row + 2 - 4 * (z % 2), col),
            "zb": (aux, 2 * (3 - z) + core, col),
            "cc": (aux, row + 1 - 2 * core, col),
        }

    def greet(self, dims, swap=False):
        barrier = pltpu.get_barrier_semaphore()
        for d in dims:
            pl.semaphore_signal(barrier, inc=1, device_id=self.partner[d], device_id_type=MESH)
        if not swap:
            pl.semaphore_wait(barrier, len(dims))
            return

        @pl.when(self.aux != self.row)
        def _():
            pl.semaphore_signal(
                barrier, inc=1, device_id=(self.row, self.aux, self.col), device_id_type=MESH
            )
            pl.semaphore_wait(barrier, len(dims) + 1)

        @pl.when(self.aux == self.row)
        def _():
            pl.semaphore_wait(barrier, len(dims))


def xy_bits(aux, col):
    y, xl = aux // 2, aux % 2
    return ((xl + col) % 2, col, (y + y // 2) % 2, y // 2)


def row_bits(row):
    z, core = row // 2, row % 2
    return ((z + z // 2) % 2, z // 2, core)


class Sems:
    def __init__(self, send, recv):
        self.send, self.recv, self.n = send, recv, 0

    def take(self):
        n = self.n
        self.n += 1
        return self.send.at[n], self.recv.at[n]


def scatter_stream(place, work, axes, order, tail, recvs, sems):
    done = []
    for step, d in enumerate(order):
        def index(bit_of_d):
            return tuple(
                place.bit[a] if a in done else (bit_of_d if a == d else slice(None)) for a in axes
            ) + tail
        mine, theirs = index(place.bit[d]), index(1 - place.bit[d])
        s, r = sems.take()
        copy = pltpu.make_async_remote_copy(
            src_ref=work.at[theirs], dst_ref=recvs[step], send_sem=s, recv_sem=r,
            device_id=place.partner[d], device_id_type=MESH,
        )
        copy.start()
        yield
        copy.wait()
        work[mine] = work[mine] + recvs[step][...]
        done.append(d)


def gather_stream(place, full, axes, order, tail, sems):
    done = []
    for d in order:
        sl = tuple(slice(None) if a in done else place.bit[a] for a in axes) + tail
        s, r = sems.take()
        copy = pltpu.make_async_remote_copy(
            src_ref=full.at[sl], dst_ref=full.at[sl], send_sem=s, recv_sem=r,
            device_id=place.partner[d], device_id_type=MESH,
        )
        copy.start()
        yield
        copy.wait()
        done.append(d)


def drive(streams):
    streams = list(streams)
    while streams:
        alive = []
        for g in streams:
            try:
                next(g)
                alive.append(g)
            except StopIteration:
                pass
        streams = alive


def rotate(dims, k):
    return tuple(dims[k:]) + tuple(dims[:k])


XY_ORDERS = [("xa", "ya", "xb", "yb"), ("xb", "yb", "xa", "ya"),
             ("ya", "xa", "yb", "xb"), ("yb", "xb", "ya", "xa")]
ROW_ORDERS = [("cc", "za", "zb"), ("cc", "zb", "za")]


def recv_shapes(n, block):
    return [pltpu.VMEM((2,) * (n - 1 - t) + block, F32) for t in range(n)]


def dma(n):
    return pltpu.SemaphoreType.DMA((n,))


ANY = pl.BlockSpec(memory_space=pl.ANY)
VM = pl.BlockSpec(memory_space=pltpu.VMEM)


def call(kernel, outs, in_specs, scratch, cid, *args):
    return pl.pallas_call(
        kernel,
        out_shape=outs,
        in_specs=in_specs,
        out_specs=jax.tree.map(lambda _: VM, outs),
        scratch_shapes=scratch,
        compiler_params=pltpu.CompilerParams(
            collective_id=cid, has_side_effects=True, vmem_limit_bytes=VMEM_LIMIT
        ),
    )(*args)


def split(x):
    hi = x.astype(BF16)
    return hi, (x - hi.astype(F32)).astype(BF16)


def x_kernel(x_in, hi_ref, lo_ref, work, full, r0, r1, local, send, recv):
    place = Place()
    sems = Sems(send, recv)
    load = pltpu.make_async_copy(x_in, work, local)
    load.start()
    place.greet(ROW)
    load.wait()
    rec = [r0, r1]
    axes = ROW
    drive(
        scatter_stream(place, work, axes, ROW_ORDERS[s], (pl.ds(64 * s, 64),),
                       rec[s], sems)
        for s in range(2)
    )
    mine = tuple(place.bit[d] for d in axes)
    full[mine] = work[mine]
    drive(
        gather_stream(place, full, axes, ROW_ORDERS[s][::-1], (pl.ds(64 * s, 64),), sems)
        for s in range(2)
    )
    for i in range(8):
        bits = (i // 4, (i // 2) % 2, i % 2)
        hi, lo = split(full[bits])
        hi_ref[pl.ds(128 * i, 128)] = hi
        lo_ref[pl.ds(128 * i, 128)] = lo


def x_all_reduce(x):
    n = x.shape[0]
    outs = (jax.ShapeDtypeStruct((n, n), BF16),) * 2
    rec = recv_shapes(3, (64, n))
    return call(
        lambda x_in, hi, lo, work, full, a0, a1, a2, b0, b1, b2, local, send, recv: x_kernel(
            x_in, hi, lo, work, full, [a0, a1, a2], [b0, b1, b2], local, send, recv),
        outs, [ANY],
        [pltpu.VMEM((2, 2, 2, 128, n), F32)] * 2 + rec + rec
        + [pltpu.SemaphoreType.DMA, dma(12), dma(12)],
        0, x.reshape(2, 2, 2, 128, n),
    )


def image_kernel(y_in, h_in, out, yw, hw, ybuf, *rest):
    yrec = [rest[4 * s: 4 * s + 4] for s in range(4)]
    hrec = [rest[16 + 3 * s: 19 + 3 * s] for s in range(2)]
    ylocal, hlocal, send, recv = rest[22:]
    place = Place()
    sems = Sems(send, recv)
    loads = []
    for aux in range(8):
        for half in range(2):
            loads.append(pltpu.make_async_copy(
                y_in.at[pl.ds(384 * half, 384), pl.ds(128 * aux, 128)],
                yw.at[xy_bits(aux, half)], ylocal.at[2 * aux + half]))
    for row in range(8):
        loads.append(pltpu.make_async_copy(
            h_in.at[:, pl.ds(128 * row, 128)], hw.at[row_bits(row)], hlocal.at[row]))
    for c in loads:
        c.start()
    place.greet(XY + ROW, swap=True)
    for c in loads:
        c.wait()
    drive(
        [scatter_stream(place, yw, XY, XY_ORDERS[s], (pl.ds(96 * s, 96),), yrec[s], sems)
         for s in range(4)]
        + [scatter_stream(place, hw, ROW, ROW_ORDERS[s], (pl.ds(192 * s, 192),), hrec[s], sems)
           for s in range(2)]
    )
    mine = tuple(place.bit[d] for d in XY)
    hmine = tuple(place.bit[d] for d in ROW)
    s, r = sems.take()
    swap = pltpu.make_async_remote_copy(
        src_ref=yw.at[mine], dst_ref=ybuf, send_sem=s, recv_sem=r,
        device_id=(place.row, place.aux, place.col), device_id_type=MESH)

    @pl.when(place.aux != place.row)
    def _():
        swap.start()
        swap.wait()
        out[...] = hw[hmine] - ybuf[...]

    @pl.when(place.aux == place.row)
    def _():
        out[...] = hw[hmine] - yw[mine]


def image_block(y, h):
    rows = h.shape[0]
    outs = jax.ShapeDtypeStruct((rows, 128), F32)
    scratch = [pltpu.VMEM((2, 2, 2, 2, rows, 128), F32), pltpu.VMEM((2, 2, 2, rows, 128), F32),
               pltpu.VMEM((rows, 128), F32)]
    for s in range(4):
        scratch += recv_shapes(4, (96, 128))
    for s in range(2):
        scratch += recv_shapes(3, (192, 128))
    scratch += [dma(16), dma(8), dma(23), dma(23)]
    return call(image_kernel, outs, [ANY, ANY], scratch, 1, y, h)


def scaled_kernel(g_in, ev, eo, own, rows_out, cols_out, gw, gr, gc, *rest):
    rec = [rest[4 * s: 4 * s + 4] for s in range(4)]
    local, send, recv = rest[16:]
    place = Place()
    sems = Sems(send, recv)
    loads = []
    for aux in range(8):
        for col in range(2):
            g = 2 * aux + col
            loads.append(pltpu.make_async_copy(
                g_in.at[pl.ds(320 * g, 320)], gw.at[xy_bits(aux, col)], local.at[g]))
    for c in loads:
        c.start()
    place.greet(XY + ROW)
    for c in loads:
        c.wait()
    drive(scatter_stream(place, gw, XY, XY_ORDERS[s], (pl.ds(80 * s, 80),), rec[s], sems)
          for s in range(4))
    mine = tuple(place.bit[d] for d in XY)
    rmine = tuple(place.bit[d] for d in ROW)
    scaled = gw[mine] / (ev[...] - eo[...])
    own[...] = scaled
    gr[rmine] = scaled
    gc[mine] = scaled
    drive(
        [gather_stream(place, gr, ROW, ROW_ORDERS[s][::-1], (pl.ds(160 * s, 160),), sems)
         for s in range(2)]
        + [gather_stream(place, gc, XY, XY_ORDERS[s][::-1], (pl.ds(80 * s, 80),), sems)
           for s in range(4)]
    )
    for aux in range(8):
        for col in range(2):
            cols_out[pl.ds(320 * (2 * aux + col), 320)] = gc[xy_bits(aux, col)]
    for row in range(8):
        rows_out[:, pl.ds(128 * row, 128)] = gr[row_bits(row)]


def scaled_gradient(g, ev, eo):
    outs = (jax.ShapeDtypeStruct((320, 128), F32), jax.ShapeDtypeStruct((320, 1024), F32),
            jax.ShapeDtypeStruct((5120, 128), F32))
    scratch = [pltpu.VMEM((2, 2, 2, 2, 320, 128), F32), pltpu.VMEM((2, 2, 2, 320, 128), F32),
               pltpu.VMEM((2, 2, 2, 2, 320, 128), F32)]
    for s in range(4):
        scratch += recv_shapes(4, (80, 128))
    scratch += [dma(16), dma(38), dma(38)]
    return call(scaled_kernel, outs, [ANY, VM, VM], scratch, 2, g, ev, eo)


def rotate_kernel(entries, g_in, w_in, c_in, out, gw, gfull, wfull, chalf, ghi, glo, thi, tlo,
                  tacc, whi, wlo, chi, clo, eacc, sacc, part, pbuf, *rest):
    rec = [rest[4 * s: 4 * s + 4] for s in range(4)]
    local, send, recv = rest[16:]
    place = Place()
    sems = Sems(send, recv)
    xmine = tuple(place.bit[d] for d in XY)
    rmine = tuple(place.bit[d] for d in ROW)
    loads = [
        pltpu.make_async_copy(g_in, gw, local.at[0]),
        pltpu.make_async_copy(w_in, wfull.at[rmine], local.at[1]),
        pltpu.make_async_copy(c_in.at[pl.ds(384 * place.col, 384)], chalf, local.at[2]),
    ]
    for c in loads:
        c.start()
    place.greet(XY + ROW, swap=True)
    for c in loads:
        c.wait()
    drive(scatter_stream(place, gw, XY, XY_ORDERS[s], (pl.ds(16 * s, 16),), rec[s], sems)
          for s in range(4))
    gfull[xmine + rmine] = gw[xmine]
    drive(
        [gather_stream(place, gfull, XY + ROW, ("za", "zb") + XY_ORDERS[s][::-1] + ("cc",),
                       (pl.ds(16 * s, 16),), sems) for s in range(4)]
        + [gather_stream(place, wfull, ROW, (("za", "zb", "cc"), ("zb", "za", "cc"))[s],
                         (pl.ds(192 * s, 192),), sems) for s in range(2)]
    )
    total = jnp.zeros((64, 128), F32)
    r64 = lax.broadcasted_iota(jnp.int32, (64, 128), 0)
    l128 = lax.broadcasted_iota(jnp.int32, (64, 128), 1)
    for i in range(16):
        xb = (i // 8, (i // 4) % 2, (i // 2) % 2, i % 2)
        block = gfull[xb + row_bits(i // 2)]
        total = total + jnp.where(l128 == r64 + 64 * (i % 2), block, 0.0)
    meansq = jnp.sum(total, axis=(0, 1), keepdims=True) / entries
    s1 = ROTATION_SCALE / jnp.sqrt(meansq + 1e-06)
    s2 = s1 * s1
    arow = row_bits(place.aux)
    rowl = lax.broadcasted_iota(jnp.int32, (64, 128), 0)
    for i in range(16):
        xb = (i // 8, (i // 4) % 2, (i // 2) % 2, i % 2)
        rs = pl.ds(64 * i, 64)
        for row in range(8):
            hi, lo = split(gfull[xb + row_bits(row)] * s2)
            ghi[rs, pl.ds(128 * row, 128)] = hi
            glo[rs, pl.ds(128 * row, 128)] = lo
        t_r = gfull[xb + rmine] * s2
        t_a = gfull[xb + arow] * s2
        hi, lo = split(t_r)
        thi[0, rs, pl.ds(0, 128)] = hi
        tlo[0, rs, pl.ds(0, 128)] = lo
        hi, lo = split(t_a)
        thi[0, rs, pl.ds(128, 128)] = hi
        tlo[0, rs, pl.ds(128, 128)] = lo
        eye_r = jnp.where(rowl + 64 * i == l128 + 128 * place.row, 1.0, 0.0)
        eye_a = jnp.where(rowl + 64 * i == l128 + 128 * place.aux, 1.0, 0.0)
        sacc[rs] = eye_r - t_r * (1.0 / 6.0)
        eacc[rs] = eye_a - t_a * 0.5
    coeff = [(1.0 / 120.0, 1.0 / 24.0), (-1.0 / 5040.0, -1.0 / 720.0), (0.0, 1.0 / 40320.0)]
    for k, (cs, ce) in enumerate(coeff):
        now, later = k % 2, (k + 1) % 2

        @pl.loop(0, 4)
        def _(t):
            rs = pl.ds(pl.multiple_of(t * 256, 256), 256)
            acc = jnp.dot(ghi[rs], thi[now], preferred_element_type=F32)
            acc += jnp.dot(ghi[rs], tlo[now], preferred_element_type=F32)
            acc += jnp.dot(glo[rs], thi[now], preferred_element_type=F32)
            if k < 2:
                hi, lo = split(acc)
                thi[later, rs] = hi
                tlo[later, rs] = lo
                sacc[rs] = sacc[rs] + acc[:, :128] * cs
            eacc[rs] = eacc[rs] + acc[:, 128:] * ce

    hi, lo = split(eacc[...])
    thi[0, :, pl.ds(128, 128)] = hi
    tlo[0, :, pl.ds(128, 128)] = lo
    hi, lo = split(sacc[...])
    thi[0, :, pl.ds(0, 128)] = hi
    tlo[0, :, pl.ds(0, 128)] = lo
    hi, lo = split(chalf[...])
    chi[...] = hi
    clo[...] = lo
    e_hi, e_lo = thi[0, :, pl.ds(128, 128)], tlo[0, :, pl.ds(128, 128)]
    part[...] = (jnp.dot(chi[...], e_hi, preferred_element_type=F32)
                 + jnp.dot(chi[...], e_lo, preferred_element_type=F32)
                 + jnp.dot(clo[...], e_hi, preferred_element_type=F32))
    s, r = sems.take()
    swap = pltpu.make_async_remote_copy(
        src_ref=part, dst_ref=pbuf, send_sem=s, recv_sem=r,
        device_id=(place.row, place.aux, place.col), device_id_type=MESH)

    @pl.when(place.aux != place.row)
    def _():
        swap.start()

    for row in range(8):
        hi, lo = split(wfull[row_bits(row)] * s1)
        whi[:, pl.ds(128 * row, 128)] = hi
        wlo[:, pl.ds(128 * row, 128)] = lo
    s_hi, s_lo = thi[0, :, pl.ds(0, 128)], tlo[0, :, pl.ds(0, 128)]
    out[...] = (jnp.dot(whi[...], s_hi, preferred_element_type=F32)
                + jnp.dot(whi[...], s_lo, preferred_element_type=F32)
                + jnp.dot(wlo[...], s_hi, preferred_element_type=F32))

    @pl.when(place.aux != place.row)
    def _():
        swap.wait()
        out[...] = out[...] + pbuf[...]

    @pl.when(place.aux == place.row)
    def _():
        out[...] = out[...] + part[...]


def rotate_block(entries, g, w, c_occ):
    outs = jax.ShapeDtypeStruct((384, 128), F32)
    vm = pltpu.VMEM
    scratch = [
        vm((2,) * 4 + (64, 128), F32), vm((2,) * 7 + (64, 128), F32),
        vm((2,) * 3 + (384, 128), F32), vm((384, 1024), F32),
        vm((1024, 1024), BF16), vm((1024, 1024), BF16),
        vm((2, 1024, 256), BF16), vm((2, 1024, 256), BF16), vm((1024, 256), F32),
        vm((384, 1024), BF16), vm((384, 1024), BF16),
        vm((384, 1024), BF16), vm((384, 1024), BF16),
        vm((1024, 128), F32), vm((1024, 128), F32), vm((384, 128), F32), vm((384, 128), F32),
    ]
    for s in range(4):
        scratch += recv_shapes(4, (16, 128))
    scratch += [dma(3), dma(51), dma(51)]
    return call(functools.partial(rotate_kernel, entries), outs, [ANY, ANY, ANY], scratch, 3,
                g.reshape(2, 2, 2, 2, 64, 128), w, c_occ)


def on_device(b_tensor, hcore, c_occ, c_virt, eps_occ, eps_virt):
    high = lax.Precision.HIGH
    naux, _, nocc = b_tensor.shape
    entries = float(c_virt.shape[1] * c_occ.shape[1])
    c_hi32 = lax.reduce_precision(c_occ, 8, 7)
    c_hi = c_hi32.astype(BF16)
    c_lo = (c_occ - c_hi32).astype(BF16)

    def xdot(c):
        return jnp.einsum("pmi,mj->pij", b_tensor, c, preferred_element_type=F32)

    x = (xdot(c_hi) + xdot(c_lo)).reshape(naux * nocc, -1)
    x_hi, x_lo = x_all_reduce(x)

    def ydot(v):
        return jnp.einsum("pni,pij->nj", b_tensor, v.reshape(naux, nocc, -1),
                          preferred_element_type=F32)

    y = ydot(x_hi) + ydot(x_lo)
    h = jnp.dot(hcore.T, c_occ, precision=high)
    image = image_block(y, h)
    grad = jnp.dot(c_virt.T, image, precision=high)
    own, rows, cols = scaled_gradient(grad, eps_virt[:, None], eps_occ[None, :])
    g = jnp.dot(rows.T, own, precision=high)
    w = jnp.dot(c_virt, cols, precision=high)
    return rotate_block(entries, g, w, c_occ)


def solution(mesh):
    placed = (
        P("aux", "row", "col"),
        P("row", ("aux", "col")),
        P("row", None),
        P(("aux", "col"), None),
        P("row"),
        P(("aux", "col")),
    )
    return jax.shard_map(
        on_device, mesh=mesh, in_specs=placed, out_specs=P(("aux", "col"), "row"), check_vma=False
    )
```

```python
import functools

import jax
import jax.numpy as jnp
from jax import lax
from jax.experimental import pallas as pl
from jax.experimental.pallas import tpu as pltpu
from jax.sharding import PartitionSpec as P

ROTATION_SCALE = 0.03
MESH = pl.DeviceIdType.MESH
F32 = jnp.float32
BF16 = jnp.bfloat16
XY = ("xa", "xb", "ya", "yb")
ROW = ("za", "zb", "cc")
VMEM_LIMIT = 60 * 1024 * 1024


class Place:
    def __init__(self):
        aux, row, col = (lax.axis_index(n) for n in ("aux", "row", "col"))
        y, xl = aux // 2, aux % 2
        z, core = row // 2, row % 2
        self.aux, self.row, self.col = aux, row, col
        self.bit = {
            "xa": (xl + col) % 2, "xb": col,
            "ya": (y + y // 2) % 2, "yb": y // 2,
            "za": (z + z // 2) % 2, "zb": z // 2,
            "cc": core,
        }
        self.partner = {
            "xa": (aux + 1 - 2 * xl, row, col),
            "xb": (aux + 1 - 2 * xl, row, 1 - col),
            "ya": (aux + 2 - 4 * (y % 2), row, col),
            "yb": (2 * (3 - y) + xl, row, col),
            "za": (aux, row + 2 - 4 * (z % 2), col),
            "zb": (aux, 2 * (3 - z) + core, col),
            "cc": (aux, row + 1 - 2 * core, col),
        }

    def greet(self, dims, swap=False):
        barrier = pltpu.get_barrier_semaphore()
        for d in dims:
            pl.semaphore_signal(barrier, inc=1, device_id=self.partner[d], device_id_type=MESH)
        if not swap:
            pl.semaphore_wait(barrier, len(dims))
            return

        @pl.when(self.aux != self.row)
        def _():
            pl.semaphore_signal(
                barrier, inc=1, device_id=(self.row, self.aux, self.col), device_id_type=MESH
            )
            pl.semaphore_wait(barrier, len(dims) + 1)

        @pl.when(self.aux == self.row)
        def _():
            pl.semaphore_wait(barrier, len(dims))


def xy_bits(aux, col):
    y, xl = aux // 2, aux % 2
    return ((xl + col) % 2, col, (y + y // 2) % 2, y // 2)


def row_bits(row):
    z, core = row // 2, row % 2
    return ((z + z // 2) % 2, z // 2, core)


class Sems:
    def __init__(self, send, recv):
        self.send, self.recv, self.n = send, recv, 0

    def take(self):
        n = self.n
        self.n += 1
        assert self.n <= self.send.shape[0]
        return self.send.at[n], self.recv.at[n]


def scatter_stream(place, work, axes, order, tail, recvs, sems):
    done = []
    for step, d in enumerate(order):
        def index(bit_of_d):
            return tuple(
                place.bit[a] if a in done else (bit_of_d if a == d else slice(None)) for a in axes
            ) + tail
        mine, theirs = index(place.bit[d]), index(1 - place.bit[d])
        s, r = sems.take()
        copy = pltpu.make_async_remote_copy(
            src_ref=work.at[theirs], dst_ref=recvs[step], send_sem=s, recv_sem=r,
            device_id=place.partner[d], device_id_type=MESH,
        )
        copy.start()
        yield
        copy.wait()
        work[mine] = work[mine] + recvs[step][...]
        done.append(d)


def gather_stream(place, full, axes, order, tail, sems):
    done = []
    for d in order:
        sl = tuple(slice(None) if a in done else place.bit[a] for a in axes) + tail
        s, r = sems.take()
        copy = pltpu.make_async_remote_copy(
            src_ref=full.at[sl], dst_ref=full.at[sl], send_sem=s, recv_sem=r,
            device_id=place.partner[d], device_id_type=MESH,
        )
        copy.start()
        yield
        copy.wait()
        done.append(d)


def drive(streams):
    streams = list(streams)
    while streams:
        alive = []
        for g in streams:
            try:
                next(g)
                alive.append(g)
            except StopIteration:
                pass
        streams = alive


def rotate(dims, k):
    return tuple(dims[k:]) + tuple(dims[:k])


XY_ORDERS = [("xa", "ya", "xb", "yb"), ("xb", "yb", "xa", "ya"),
             ("ya", "xa", "yb", "xb"), ("yb", "xb", "ya", "xa")]
ROW_ORDERS = [("cc", "za", "zb"), ("cc", "zb", "za")]


def recv_shapes(n, block):
    return [pltpu.VMEM((2,) * (n - 1 - t) + block, F32) for t in range(n)]


def dma(n):
    return pltpu.SemaphoreType.DMA((n,))


ANY = pl.BlockSpec(memory_space=pl.ANY)
VM = pl.BlockSpec(memory_space=pltpu.VMEM)


def call(kernel, outs, in_specs, scratch, cid, *args):
    return pl.pallas_call(
        kernel,
        out_shape=outs,
        in_specs=in_specs,
        out_specs=jax.tree.map(lambda _: VM, outs),
        scratch_shapes=scratch,
        compiler_params=pltpu.CompilerParams(
            collective_id=cid, has_side_effects=True, vmem_limit_bytes=VMEM_LIMIT
        ),
    )(*args)


def split(x):
    hi = x.astype(BF16)
    return hi, (x - hi.astype(F32)).astype(BF16)


PIECES = 2


def start_all(streams):
    for g in streams:
        next(g)
    return streams


def nt(a, b):
    return lax.dot_general(a, b, (((1,), (1,)), ((), ())), preferred_element_type=F32)


def nn(a, b):
    return jnp.dot(a, b, preferred_element_type=F32)


class Bag:
    def __init__(self):
        self.names, self.shapes = [], []

    def add(self, name, shape):
        self.names.append(name)
        self.shapes.append(shape)

    def recvs(self, name, n, block):
        for t, s in enumerate(recv_shapes(n, block)):
            self.add((name, t), s)

    def bind(self, refs):
        return dict(zip(self.names, refs))


def gradient_scratch():
    bag, vm = Bag(), pltpu.VMEM
    bag.add("b", vm((2, 2, 768, 512), BF16))
    bag.add("c", vm((768, 1024), F32))
    bag.add("hc", vm((768, 384), F32))
    bag.add("cth", vm((4, 2, 2, 64, 768), BF16))
    bag.add("ctl", vm((4, 2, 2, 64, 768), BF16))
    bag.add("hch", vm((768, 384), BF16))
    bag.add("hcl", vm((768, 384), BF16))
    bag.add("cv", vm((2, 384, 640), F32))
    bag.add("cvh", vm((384, 5120), BF16))
    bag.add("cvl", vm((384, 5120), BF16))
    bag.add("ev", vm((8, 640), F32))
    for p in range(PIECES):
        bag.add(("xs", p), vm((4, 64, 1024), F32))
        bag.add(("xr", p), vm((4, 64, 1024), F32))
        bag.add(("xw", p), vm((2, 2, 64, 1024), F32))
        bag.add(("xf", p), vm((2, 2, 64, 1024), F32))
        bag.add(("yw", p), vm((2, 2, 2, 2, 64, 384), F32))
        bag.add(("yb", p), vm((64, 384), F32))
        bag.add(("gw", p), vm((2, 2, 2, 2, 32, 640), F32))
        for s in range(2):
            bag.recvs(("xrec", p, s), 2, (32, 1024))
            bag.recvs(("hrec", p, s), 3, (32, 384))
        for s in range(4):
            bag.recvs(("yrec", p, s), 4, (16, 384))
            bag.recvs(("grec", p, s), 4, (8, 640))
    bag.add("hw", vm((2, 2, 2, 128, 384), F32))
    bag.add("local", dma(6))
    bag.add("send", dma(112))
    bag.add("recv", dma(112))
    return bag


def gradient_kernel(bag, b_in, h_in, c_in, cv_in, ev_in, eo, own, *refs):
    m = bag.bind(refs)
    place = Place()
    sems = Sems(m["send"], m["recv"])
    core = place.row % 2
    y, z = place.aux // 2, place.row // 2
    across = (place.aux, place.row, 1 - place.col)
    swapped = (2 * z + place.aux % 2, 2 * y + core, place.col)

    def remote(src, dst, device):
        s, r = sems.take()
        return pltpu.make_async_remote_copy(
            src_ref=src, dst_ref=dst, send_sem=s, recv_sem=r,
            device_id=device, device_id_type=MESH)

    load_c = pltpu.make_async_copy(c_in, m["c"], m["local"].at[0])
    load_b = pltpu.make_async_copy(b_in, m["b"].at[0], m["local"].at[1])
    load_h = pltpu.make_async_copy(h_in, m["hc"], m["local"].at[2])

    def load_cv(k):
        return pltpu.make_async_copy(
            cv_in.at[:, pl.ds(640 * k, 640)], m["cv"].at[k % 2], m["local"].at[3 + k % 2])

    for c in (load_c, load_b, load_h, load_cv(0), load_cv(1)):
        c.start()
    barrier = pltpu.get_barrier_semaphore()
    dims = XY + ROW
    for d in dims:
        pl.semaphore_signal(barrier, inc=1, device_id=place.partner[d], device_id_type=MESH)
    pl.semaphore_signal(barrier, inc=1, device_id=across, device_id_type=MESH)

    @pl.when(y != z)
    def _():
        pl.semaphore_signal(barrier, inc=1, device_id=swapped, device_id_type=MESH)
        pl.semaphore_wait(barrier, len(dims) + 2)

    @pl.when(y == z)
    def _():
        pl.semaphore_wait(barrier, len(dims) + 1)

    ev_copy = remote(ev_in, m["ev"], across)
    ev_copy.start()
    load_c.wait()
    for r in range(8):
        hi, lo = split(m["c"][:, pl.ds(128 * r, 128)].T)
        m["cth"][r // 2, r % 2] = hi.reshape(2, 64, 768)
        m["ctl"][r // 2, r % 2] = lo.reshape(2, 64, 768)
    load_b.wait()
    b_copy = remote(m["b"].at[0], m["b"].at[1], place.partner["cc"])

    def x_part(p, k, out):
        hi = m["cth"][:, k, p].reshape(256, 768)
        lo = m["ctl"][:, k, p].reshape(256, 768)
        for q in range(2):
            b = m["b"][0, q]
            out[..., pl.ds(512 * q, 512)] = (nn(hi, b) + nn(lo, b)).reshape(
                out.shape[:-1] + (512,))

    xc = []
    for p in range(PIECES):
        x_part(p, 1 - core, m["xs", p])
        xc.append(remote(m["xs", p], m["xr", p], place.partner["cc"]))
        xc[p].start()
        x_part(p, core, m["xw", p])
    b_copy.start()
    zaxes = ("za", "zb")
    zorders = (("za", "zb"), ("zb", "za"))
    xrs = []
    for p in range(PIECES):
        xc[p].wait()
        m["xw", p][...] = m["xw", p][...] + m["xr", p][...].reshape(2, 2, 64, 1024)
        xrs.append(start_all([
            scatter_stream(place, m["xw", p], zaxes, zorders[s], (pl.ds(32 * s, 32),),
                           [m[("xrec", p, s), t] for t in range(2)], sems)
            for s in range(2)]))

    load_h.wait()
    hi, lo = split(m["hc"][...])
    m["hch"][...] = hi
    m["hcl"][...] = lo
    for r in range(8):
        chi = m["cth"][r // 2, r % 2].reshape(128, 768)
        clo = m["ctl"][r // 2, r % 2].reshape(128, 768)
        m["hw"][row_bits(r)] = (
            nn(chi, m["hch"][...]) + nn(clo, m["hch"][...]) + nn(chi, m["hcl"][...]))
    hrs = [
        scatter_stream(place, m["hw"], ROW, ROW_ORDERS[s], (pl.ds(64 * p + 32 * s, 32),),
                       [m[("hrec", p, s), t] for t in range(3)], sems)
        for p in range(PIECES) for s in range(2)]
    start_all(hrs)

    def split_cv(k):
        load_cv(k).wait()
        hi, lo = split(m["cv"][k % 2])
        m["cvh"][:, pl.ds(640 * k, 640)] = hi
        m["cvl"][:, pl.ds(640 * k, 640)] = lo
        if k + 2 < 8:
            load_cv(k + 2).start()

    for k in range(4):
        split_cv(k)
    mine = tuple(place.bit[d] for d in zaxes)
    xag = []
    for step in range(2):
        for p in range(PIECES):
            if step == 0:
                for g in xrs[p]:
                    next(g)
            else:
                drive(xrs[p])
                m["xf", p][mine] = m["xw", p][mine]
                xag.append(start_all([
                    gather_stream(place, m["xf", p], zaxes, zorders[s][::-1],
                                  (pl.ds(32 * s, 32),), sems)
                    for s in range(2)]))
        if step == 0:
            for k in range(4, 8):
                split_cv(k)
    for p in range(PIECES):
        for g in xag[p]:
            next(g)
    yrs = []
    for p in range(PIECES):
        drive(xag[p])
        if p == 0:
            b_copy.wait()
        else:
            for g in hrs:
                next(g)
        hi, lo = split(m["xf", p][...].reshape(256, 1024))
        for side in range(2):
            xlo = core if side == 0 else 1 - core
            for half in range(2):
                rows = pl.ds(384 * half, 384)
                acc = 0.0
                for q in range(2):
                    b = m["b"][side, q, rows]
                    sl = slice(512 * q, 512 * q + 512)
                    acc = acc + nt(hi[:, sl], b) + nt(lo[:, sl], b)
                for zz in range(4):
                    m["yw", p][(xlo + half) % 2, half, (zz + zz // 2) % 2, zz // 2] = (
                        acc[64 * zz: 64 * zz + 64])
        yrs.append(start_all([
            scatter_stream(place, m["yw", p], XY, XY_ORDERS[s], (pl.ds(16 * s, 16),),
                           [m[("yrec", p, s), t] for t in range(4)], sems)
            for s in range(4)]))
    drive(hrs)
    xmine = tuple(place.bit[d] for d in XY)
    hmine = tuple(place.bit[d] for d in ROW)
    for step in range(3):
        for p in range(PIECES):
            for g in yrs[p]:
                next(g)
    swaps = []
    for p in range(PIECES):
        drive(yrs[p])
        swaps.append(remote(m["yw", p].at[xmine], m["yb", p], swapped))

        @pl.when(y != z)
        def _():
            swaps[p].start()

        @pl.when(y == z)
        def _():
            m["yb", p][...] = m["yw", p][xmine]

    grs = []
    for p in range(PIECES):
        @pl.when(y != z)
        def _():
            swaps[p].wait()

        image = m["hw"][hmine + (pl.ds(64 * p, 64),)] - m["yb", p][...]
        hi, lo = split(image)
        both = jnp.concatenate([hi, lo], axis=0)
        for aux in range(8):
            sl = pl.ds(640 * aux, 640)
            acc = nn(both, m["cvh"][:, sl])
            acc = acc[:64] + acc[64:] + nn(hi, m["cvl"][:, sl])
            for col in range(2):
                m["gw", p][xy_bits(aux, col)] = acc[32 * col: 32 * col + 32]
        grs.append(start_all([
            scatter_stream(place, m["gw", p], XY, XY_ORDERS[s], (pl.ds(8 * s, 8),),
                           [m[("grec", p, s), t] for t in range(4)], sems)
            for s in range(4)]))
    ev_copy.wait()
    for step in range(3):
        for p in range(PIECES):
            for g in grs[p]:
                next(g)
    ev = ev_in[0:1] + m["ev"][0:1]
    for p in range(PIECES):
        drive(grs[p])
        e = eo[pl.ds(64 * p + 32 * place.col, 32)]
        own[pl.ds(32 * p, 32)] = m["gw", p][xmine] / (ev - e)


def gradient_block(b, hcore, c_occ, c_virt, ev, eo):
    bag = gradient_scratch()
    return call(functools.partial(gradient_kernel, bag), jax.ShapeDtypeStruct((64, 640), F32),
                [ANY, ANY, ANY, ANY, VM, VM], bag.shapes, 0, b, hcore, c_occ, c_virt, ev, eo)


def rotate_scratch():
    bag, vm = Bag(), pltpu.VMEM
    bag.add("cv", vm((2, 384, 640), F32))
    bag.add("cvh", vm((384, 5120), BF16))
    bag.add("cvl", vm((384, 5120), BF16))
    bag.add("kc", vm((2, 2, 2, 2, 64, 640), F32))
    bag.add("kg", vm((2, 2, 2, 2, 2, 32, 384), F32))
    bag.add("win", vm((2, 32, 384), F32))
    bag.add("gw", vm((2, 2, 2, 2, 64, 128), F32))
    bag.add("gfull", vm((2,) * 7 + (64, 128), F32))
    bag.add("wfull", vm((2, 2, 2, 384, 128), F32))
    bag.add("chalf", vm((384, 1024), F32))
    for n, s in (("ghi", (1024, 1024)), ("glo", (1024, 1024)), ("thi", (2, 1024, 256)),
                 ("tlo", (2, 1024, 256)), ("whi", (384, 1024)), ("wlo", (384, 1024)),
                 ("chi", (384, 1024)), ("clo", (384, 1024))):
        bag.add(n, vm(s, BF16))
    for n, s in (("eacc", (1024, 128)), ("sacc", (1024, 128)), ("part", (384, 128)),
                 ("pbuf", (384, 128))):
        bag.add(n, vm(s, F32))
    for s in range(4):
        bag.recvs(("grec", s), 4, (16, 128))
    bag.add("local", dma(3))
    bag.add("send", dma(80))
    bag.add("recv", dma(80))
    return bag


def rotate_kernel(bag, entries, own, cv_in, c_in, out, *refs):
    m = bag.bind(refs)
    place = Place()
    sems = Sems(m["send"], m["recv"])
    col = place.col
    xmine = tuple(place.bit[d] for d in XY)
    rmine = tuple(place.bit[d] for d in ROW)
    across = (place.aux, place.row, 1 - col)
    other = (place.row, place.aux, col)

    def remote(src, dst, device):
        s, r = sems.take()
        return pltpu.make_async_remote_copy(
            src_ref=src, dst_ref=dst, send_sem=s, recv_sem=r,
            device_id=device, device_id_type=MESH)

    def load_cv(k):
        return pltpu.make_async_copy(
            cv_in.at[:, pl.ds(640 * k, 640)], m["cv"].at[k % 2], m["local"].at[k % 2])

    load_c = pltpu.make_async_copy(
        c_in.at[pl.ds(384 * col, 384)], m["chalf"], m["local"].at[2])
    for c in (load_cv(0), load_cv(1), load_c):
        c.start()
    barrier = pltpu.get_barrier_semaphore()
    dims = XY + ROW
    for d in dims:
        pl.semaphore_signal(barrier, inc=1, device_id=place.partner[d], device_id_type=MESH)
    pl.semaphore_signal(barrier, inc=1, device_id=across, device_id_type=MESH)
    m["kc"][xmine] = own[...]
    m["kg"][rmine + (slice(None), col)] = own[:, pl.ds(pl.multiple_of(256 * col, 128), 384)].reshape(2, 32, 384)
    m["win"][...] = own[:, pl.ds(pl.multiple_of(256 - 256 * col, 128), 384)].reshape(2, 32, 384)

    @pl.when(place.aux != place.row)
    def _():
        pl.semaphore_signal(barrier, inc=1, device_id=other, device_id_type=MESH)
        pl.semaphore_wait(barrier, len(dims) + 2)

    @pl.when(place.aux == place.row)
    def _():
        pl.semaphore_wait(barrier, len(dims) + 1)

    window = remote(m["win"], m["kg"].at[rmine + (slice(None), col)], across)
    window.start()
    kag = start_all([
        gather_stream(place, m["kc"], XY, XY_ORDERS[s][::-1], (pl.ds(16 * s, 16),), sems)
        for s in range(4)])

    def split_cv(k):
        load_cv(k).wait()
        hi, lo = split(m["cv"][k % 2])
        m["cvh"][:, pl.ds(640 * k, 640)] = hi
        m["cvl"][:, pl.ds(640 * k, 640)] = lo
        if k + 2 < 8:
            load_cv(k + 2).start()

    for k in range(3):
        split_cv(k)
    window.wait()
    zag = start_all([
        gather_stream(place, m["kg"], ROW, (("za", "zb", "cc"), ("zb", "za", "cc"))[s],
                      (s,), sems) for s in range(2)])
    for k in range(3, 6):
        split_cv(k)
    for step in range(2):
        for g in zag:
            next(g)
        for g in kag:
            next(g)
    for k in range(6, 8):
        split_cv(k)
    load_c.wait()
    hi, lo = split(m["chalf"][...])
    m["chi"][...] = hi
    m["clo"][...] = lo
    drive(zag)
    lanes = lax.broadcasted_iota(jnp.int32, (128, 384), 1)
    rhs = m["kg"][rmine].reshape(128, 384)
    rhs = jnp.where(lanes >= 128 * col, rhs, 0.0)
    rh, rl = split(rhs)
    for row in range(8):
        lh, ll = split(m["kg"][row_bits(row)].reshape(128, 384))
        acc = nt(lh, rh) + nt(lh, rl) + nt(ll, rh)
        for i in range(2):
            k = 2 * row + i
            m["gw"][k // 8, (k // 4) % 2, (k // 2) % 2, k % 2] = acc[64 * i: 64 * i + 64]
    grs = start_all([
        scatter_stream(place, m["gw"], XY, XY_ORDERS[s], (pl.ds(16 * s, 16),),
                       [m[("grec", s), t] for t in range(4)], sems) for s in range(4)])
    drive(grs)
    m["gfull"][xmine + rmine] = m["gw"][xmine]
    gag = start_all([
        gather_stream(place, m["gfull"], XY + ROW, ("za", "zb") + XY_ORDERS[s][::-1] + ("cc",),
                      (pl.ds(16 * s, 16),), sems) for s in range(4)])
    for g in kag:
        next(g)
    for step in range(2):
        for g in gag:
            next(g)
    drive(kag)
    w = 0.0
    for aux in range(8):
        k0 = m["kc"][xy_bits(aux, 0)]
        k1 = m["kc"][xy_bits(aux, 1)]
        kt = jnp.concatenate([k0[:32], k1[:32], k0[32:], k1[32:]], axis=0)
        kh, kl = split(kt)
        ch, cl = m["cvh"][:, pl.ds(640 * aux, 640)], m["cvl"][:, pl.ds(640 * aux, 640)]
        w = w + nt(ch, kh) + nt(ch, kl) + nt(cl, kh)
    m["wfull"][rmine] = w
    wag = start_all([
        gather_stream(place, m["wfull"], ROW, (("za", "zb", "cc"), ("zb", "za", "cc"))[s],
                      (pl.ds(192 * s, 192),), sems) for s in range(2)])
    for step in range(2):
        for g in gag:
            next(g)
        for g in wag:
            next(g)
    drive(gag)

    gfull, thi, tlo, eacc, sacc = m["gfull"], m["thi"], m["tlo"], m["eacc"], m["sacc"]
    total = jnp.zeros((64, 128), F32)
    r64 = lax.broadcasted_iota(jnp.int32, (64, 128), 0)
    l128 = lax.broadcasted_iota(jnp.int32, (64, 128), 1)
    for i in range(16):
        xb = (i // 8, (i // 4) % 2, (i // 2) % 2, i % 2)
        block = gfull[xb + row_bits(i // 2)]
        total = total + jnp.where(l128 == r64 + 64 * (i % 2), block, 0.0)
    meansq = jnp.sum(total, axis=(0, 1), keepdims=True) / entries
    s1 = ROTATION_SCALE / jnp.sqrt(meansq + 1e-06)
    s2 = s1 * s1
    arow = row_bits(place.aux)
    for i in range(16):
        xb = (i // 8, (i // 4) % 2, (i // 2) % 2, i % 2)
        rs = pl.ds(64 * i, 64)
        for row in range(8):
            hi, lo = split(gfull[xb + row_bits(row)] * s2)
            m["ghi"][rs, pl.ds(128 * row, 128)] = hi
            m["glo"][rs, pl.ds(128 * row, 128)] = lo
        t_r = gfull[xb + rmine] * s2
        t_a = gfull[xb + arow] * s2
        hi, lo = split(t_r)
        thi[0, rs, pl.ds(0, 128)] = hi
        tlo[0, rs, pl.ds(0, 128)] = lo
        hi, lo = split(t_a)
        thi[0, rs, pl.ds(128, 128)] = hi
        tlo[0, rs, pl.ds(128, 128)] = lo
        eye_r = jnp.where(r64 + 64 * i == l128 + 128 * place.row, 1.0, 0.0)
        eye_a = jnp.where(r64 + 64 * i == l128 + 128 * place.aux, 1.0, 0.0)
        sacc[rs] = eye_r - t_r * (1.0 / 6.0)
        eacc[rs] = eye_a - t_a * 0.5
    coeff = [(1.0 / 120.0, 1.0 / 24.0), (-1.0 / 5040.0, -1.0 / 720.0), (0.0, 1.0 / 40320.0)]
    for k, (cs, ce) in enumerate(coeff):
        now, later = k % 2, (k + 1) % 2

        @pl.loop(0, 4)
        def _(t):
            rs = pl.ds(pl.multiple_of(t * 256, 256), 256)
            acc = (nn(m["ghi"][rs], thi[now]) + nn(m["ghi"][rs], tlo[now])
                   + nn(m["glo"][rs], thi[now]))
            if k < 2:
                hi, lo = split(acc)
                thi[later, rs] = hi
                tlo[later, rs] = lo
                sacc[rs] = sacc[rs] + acc[:, :128] * cs
            eacc[rs] = eacc[rs] + acc[:, 128:] * ce

    e_hi, e_lo = split(eacc[...])
    m["part"][...] = nn(m["chi"][...], e_hi) + nn(m["chi"][...], e_lo) + nn(m["clo"][...], e_hi)
    swap = remote(m["part"], m["pbuf"], other)

    @pl.when(place.aux != place.row)
    def _():
        swap.start()

    drive(wag)
    for row in range(8):
        hi, lo = split(m["wfull"][row_bits(row)] * s1)
        m["whi"][:, pl.ds(128 * row, 128)] = hi
        m["wlo"][:, pl.ds(128 * row, 128)] = lo
    s_hi, s_lo = split(sacc[...])
    result = nn(m["whi"][...], s_hi) + nn(m["whi"][...], s_lo) + nn(m["wlo"][...], s_hi)

    @pl.when(place.aux != place.row)
    def _():
        swap.wait()
        out[...] = result + m["pbuf"][...]

    @pl.when(place.aux == place.row)
    def _():
        out[...] = result + m["part"][...]


def rotate_block(entries, own, c_virt, c_occ):
    bag = rotate_scratch()
    return call(functools.partial(rotate_kernel, bag, entries),
                jax.ShapeDtypeStruct((384, 128), F32), [VM, ANY, ANY], bag.shapes, 1,
                own, c_virt, c_occ)


def on_device(b_tensor, hcore, c_occ, c_virt, eps_occ, eps_virt):
    entries = float(c_virt.shape[1] * c_occ.shape[1])
    width = eps_virt.shape[0]
    ev = lax.dynamic_update_slice(
        jnp.zeros((8, 2 * width), F32), jnp.broadcast_to(eps_virt, (8, width)),
        (0, lax.axis_index("col") * width))
    own = gradient_block(b_tensor, hcore, c_occ, c_virt, ev, eps_occ[:, None])
    return rotate_block(entries, own, c_virt, c_occ)


def solution(mesh):
    placed = (
        P("aux", "row", "col"),
        P("row", ("aux", "col")),
        P("row", None),
        P(("aux", "col"), None),
        P("row"),
        P(("aux", "col")),
    )
    return jax.shard_map(
        on_device, mesh=mesh, in_specs=placed, out_specs=P(("aux", "col"), "row"), check_vma=False
    )
```

```python
import functools

import jax
import jax.numpy as jnp
from jax import lax
from jax.experimental import pallas as pl
from jax.experimental.pallas import tpu as pltpu
from jax.sharding import PartitionSpec as P

ROTATION_SCALE = 0.03
MESH = pl.DeviceIdType.MESH
F32 = jnp.float32
BF16 = jnp.bfloat16
XY = ("xa", "xb", "ya", "yb")
ROW = ("za", "zb", "cc")
VMEM_LIMIT = 62 * 1024 * 1024


class Place:
    def __init__(self):
        aux, row, col = (lax.axis_index(n) for n in ("aux", "row", "col"))
        y, xl = aux // 2, aux % 2
        z, core = row // 2, row % 2
        self.aux, self.row, self.col = aux, row, col
        self.bit = {
            "xa": (xl + col) % 2, "xb": col,
            "ya": (y + y // 2) % 2, "yb": y // 2,
            "za": (z + z // 2) % 2, "zb": z // 2,
            "cc": core,
        }
        self.partner = {
            "xa": (aux + 1 - 2 * xl, row, col),
            "xb": (aux + 1 - 2 * xl, row, 1 - col),
            "ya": (aux + 2 - 4 * (y % 2), row, col),
            "yb": (2 * (3 - y) + xl, row, col),
            "za": (aux, row + 2 - 4 * (z % 2), col),
            "zb": (aux, 2 * (3 - z) + core, col),
            "cc": (aux, row + 1 - 2 * core, col),
        }

    def greet(self, dims, swap=False):
        barrier = pltpu.get_barrier_semaphore()
        for d in dims:
            pl.semaphore_signal(barrier, inc=1, device_id=self.partner[d], device_id_type=MESH)
        if not swap:
            pl.semaphore_wait(barrier, len(dims))
            return

        @pl.when(self.aux != self.row)
        def _():
            pl.semaphore_signal(
                barrier, inc=1, device_id=(self.row, self.aux, self.col), device_id_type=MESH
            )
            pl.semaphore_wait(barrier, len(dims) + 1)

        @pl.when(self.aux == self.row)
        def _():
            pl.semaphore_wait(barrier, len(dims))


def xy_bits(aux, col):
    y, xl = aux // 2, aux % 2
    return ((xl + col) % 2, col, (y + y // 2) % 2, y // 2)


def row_bits(row):
    z, core = row // 2, row % 2
    return ((z + z // 2) % 2, z // 2, core)


class Sems:
    def __init__(self, send, recv):
        self.send, self.recv, self.n = send, recv, 0

    def take(self):
        n = self.n
        self.n += 1
        assert self.n <= self.send.shape[0]
        return self.send.at[n], self.recv.at[n]


def scatter_stream(place, work, axes, order, tail, recvs, sems):
    done = []
    for step, d in enumerate(order):
        def index(bit_of_d):
            return tuple(
                place.bit[a] if a in done else (bit_of_d if a == d else slice(None)) for a in axes
            ) + tail
        mine, theirs = index(place.bit[d]), index(1 - place.bit[d])
        s, r = sems.take()
        copy = pltpu.make_async_remote_copy(
            src_ref=work.at[theirs], dst_ref=recvs[step], send_sem=s, recv_sem=r,
            device_id=place.partner[d], device_id_type=MESH,
        )
        copy.start()
        yield
        copy.wait()
        work[mine] = work[mine] + recvs[step][...]
        done.append(d)


def gather_stream(place, full, axes, order, tail, sems):
    done = []
    for d in order:
        sl = tuple(slice(None) if a in done else place.bit[a] for a in axes) + tail
        s, r = sems.take()
        copy = pltpu.make_async_remote_copy(
            src_ref=full.at[sl], dst_ref=full.at[sl], send_sem=s, recv_sem=r,
            device_id=place.partner[d], device_id_type=MESH,
        )
        copy.start()
        yield
        copy.wait()
        done.append(d)


def drive(streams):
    streams = list(streams)
    while streams:
        alive = []
        for g in streams:
            try:
                next(g)
                alive.append(g)
            except StopIteration:
                pass
        streams = alive


def rotate(dims, k):
    return tuple(dims[k:]) + tuple(dims[:k])


XY_ORDERS = [("xa", "ya", "xb", "yb"), ("xb", "yb", "xa", "ya"),
             ("ya", "xa", "yb", "xb"), ("yb", "xb", "ya", "xa")]
ROW_ORDERS = [("cc", "za", "zb"), ("cc", "zb", "za")]


def recv_shapes(n, block):
    return [pltpu.VMEM((2,) * (n - 1 - t) + block, F32) for t in range(n)]


def dma(n):
    return pltpu.SemaphoreType.DMA((n,))


ANY = pl.BlockSpec(memory_space=pl.ANY)
VM = pl.BlockSpec(memory_space=pltpu.VMEM)


def call(kernel, outs, in_specs, scratch, cid, *args):
    return pl.pallas_call(
        kernel,
        out_shape=outs,
        in_specs=in_specs,
        out_specs=jax.tree.map(lambda _: VM, outs),
        scratch_shapes=scratch,
        compiler_params=pltpu.CompilerParams(
            collective_id=cid, has_side_effects=True, vmem_limit_bytes=VMEM_LIMIT
        ),
    )(*args)


def split(x):
    hi = x.astype(BF16)
    return hi, (x - hi.astype(F32)).astype(BF16)


def start_all(streams):
    for g in streams:
        next(g)
    return streams


def nt(a, b):
    return lax.dot_general(a, b, (((1,), (1,)), ((), ())), preferred_element_type=F32)


def nn(a, b):
    return jnp.dot(a, b, preferred_element_type=F32)


class Bag:
    def __init__(self):
        self.names, self.shapes = [], []

    def add(self, name, shape):
        self.names.append(name)
        self.shapes.append(shape)

    def recvs(self, name, n, block):
        for t, s in enumerate(recv_shapes(n, block)):
            self.add((name, t), s)

    def bind(self, refs):
        return dict(zip(self.names, refs))


PIECES = 4
R = 128 // PIECES
Q = R // 2
G_CUTS = ((0, 16), (16, 8), (24, 8), (32, 8))
G_ORDERS = [("za", "zb") + o[::-1] + ("cc",) for o in XY_ORDERS] + [XY_ORDERS[0] + ("za", "zb", "cc")]
Z_ORDERS = (("za", "zb"), ("zb", "za"))
SCHEDULE = [
    1, 2, 4, 3, 4, 6, 6, 6, 0, 1, 6, 6, 2, 3, 0, 1, 2, 3, 0, 1, 2, 3, 0, 1,
    2, 3, 1, 4, 0, 2, 5, 3, 1, 0, 4, 2, 3, 1, 0, 2, 3, 1, 0, 2, 5, 3, 0, 4,
    1, 2, 3, 0, 1, 5, 2, 3, 5, 0, 1, 2, 3, 0, 1, 2, 3, 0, 1, 2, 3, 0, 8, 9,
    1, 2, 10, 3, 7, 0, 1, 8, 2, 9, 3, 10, 0, 7, 1, 2, 1, 3, 2, 0, 3, 0, 8, 7,
    9, 10, 12, 12, 12, 12, 12, 12, 8, 7, 9, 10, 11, 11, 11, 11, 12, 12, 11, 12, 11, 12, 11, 12,
]


def grad_cuts(p):
    return [((slice(None), pl.ds(128 * s, 128)), XY_ORDERS[s if s < 4 else p]) for s in range(5)]


def scratch():
    bag, vm = Bag(), pltpu.VMEM
    bag.add("b", vm((2, 2, 768, 512), BF16))
    bag.add("c", vm((768, 1024), F32))
    bag.add("cg", vm((384, 1024), F32))
    bag.add("hc", vm((768, 384), F32))
    bag.add("ct", vm((2, PIECES, 2, 4, R, 768), BF16))
    bag.add("hch", vm((768, 384), BF16))
    bag.add("hcl", vm((768, 384), BF16))
    bag.add("cv", vm((2, 384, 256), F32))
    bag.add("cvh", vm((384, 5120), BF16))
    bag.add("cvl", vm((384, 5120), BF16))
    bag.add("ev", vm((2, 8, 640), F32))
    bag.add("eo", vm((128, 8), F32))
    for p in range(PIECES):
        bag.add(("xs", p), vm((4, R, 1024), F32))
        bag.add(("xr", p), vm((4, R, 1024), F32))
        bag.add(("xw", p), vm((2, 2, R, 1024), F32))
        bag.add(("xf", p), vm((2, 2, R, 1024), F32))
        bag.add(("yw", p), vm((2, 2, 2, 2, R, 384), F32))
        bag.add(("yb", p), vm((R, 384), F32))
        bag.add(("gw", p), vm((2, 2, 2, 2, Q, 640), F32))
        for s in range(2):
            bag.recvs(("xrec", p, s), 2, (R // 2, 1024))
        for s in range(4):
            bag.recvs(("yrec", p, s), 4, (R // 4, 384))
        for s in range(5):
            bag.recvs(("grec", p, s), 4, (Q, 128))
    for s in range(2):
        bag.recvs(("hrec", s), 3, (64, 384))
    bag.add("hw", vm((2, 2, 2, 128, 384), F32))
    bag.add("kc", vm((2, 2, 2, 2, PIECES, Q, 640), F32))
    bag.add("kg", vm((2, 2, 2, PIECES, 2, Q, 384), F32))
    bag.add("win", vm((PIECES, Q, 384), F32))
    bag.add("gs", vm((2, 2, 2, 2, 40, 128), F32))
    for s, (_, n) in enumerate(G_CUTS):
        bag.recvs(("gsrec", s), 4, (n, 128))
    bag.add("gfull", vm((2,) * 7 + (40, 128), F32))
    bag.add("wfull", vm((2, 2, 2, 384, 128), F32))
    bag.add("ghi", vm((1024, 1024), BF16))
    bag.add("glo", vm((1024, 1024), BF16))
    bag.add("t", vm((2, 1024, 256), BF16))
    bag.add("acc", vm((2, 1024, 128), F32))
    bag.add("local", dma(12))
    bag.add("send", dma(320))
    bag.add("recv", dma(320))
    return bag


def kernel(bag, entries, b_in, h_in, c_in, cv_in, ev_in, eo_in, out, *refs):
    m = bag.bind(refs)
    place = Place()
    sems = Sems(m["send"], m["recv"])
    core, col = place.row % 2, place.col
    other = 1 - core
    y, z = place.aux // 2, place.row // 2
    across = (place.aux, place.row, 1 - col)
    swapped = (2 * z + place.aux % 2, 2 * y + core, col)
    xmine = tuple(place.bit[d] for d in XY)
    rmine = tuple(place.bit[d] for d in ROW)
    zmine = rmine[:2]

    def remote(src, dst, device):
        s, r = sems.take()
        return pltpu.make_async_remote_copy(
            src_ref=src, dst_ref=dst, send_sem=s, recv_sem=r,
            device_id=device, device_id_type=MESH)

    def load_c(k, zz):
        sl = pl.ds(pl.multiple_of(128 * (2 * zz + k), 128), 128)
        which = zz if k is core else 4 + zz
        return pltpu.make_async_copy(c_in.at[:, sl], m["c"].at[:, sl], m["local"].at[which])

    load_b = pltpu.make_async_copy(b_in, m["b"].at[0], m["local"].at[8])
    load_h = pltpu.make_async_copy(h_in, m["hc"], m["local"].at[9])

    def load_cv(k):
        return pltpu.make_async_copy(
            cv_in.at[:, pl.ds(256 * k, 256)], m["cv"].at[k % 2], m["local"].at[10 + k % 2])

    for zz in range(4):
        load_c(other, zz).start()
    load_b.start()
    for zz in range(4):
        load_c(core, zz).start()
    barrier = pltpu.get_barrier_semaphore()
    dims = XY + ROW
    for d in dims:
        pl.semaphore_signal(barrier, inc=1, device_id=place.partner[d], device_id_type=MESH)
    pl.semaphore_signal(barrier, inc=1, device_id=across, device_id_type=MESH)

    @pl.when(y != z)
    def _():
        pl.semaphore_signal(barrier, inc=1, device_id=swapped, device_id_type=MESH)

    def turn_c(k, zz):
        load_c(k, zz).wait()
        sl = pl.ds(pl.multiple_of(128 * (2 * zz + k), 128), 128)
        hi, lo = split(m["c"][:, sl].T)
        m["ct"][k, :, 0, zz] = hi.reshape(PIECES, R, 768)
        m["ct"][k, :, 1, zz] = lo.reshape(PIECES, R, 768)

    def x_part(p, k, out_ref):
        both = m["ct"][k, p].reshape(8 * R, 768)
        for q in range(2):
            acc = nn(both, m["b"][0, q])
            out_ref[..., pl.ds(512 * q, 512)] = (acc[:4 * R] + acc[4 * R:]).reshape(
                out_ref.shape[:-1] + (512,))

    for zz in range(4):
        turn_c(other, zz)
    load_b.wait()
    x_part(0, other, m["xs", 0])

    @pl.when(y != z)
    def _():
        pl.semaphore_wait(barrier, len(dims) + 2)

    @pl.when(y == z)
    def _():
        pl.semaphore_wait(barrier, len(dims) + 1)

    xc = [remote(m["xs", p], m["xr", p], place.partner["cc"]) for p in range(PIECES)]
    xc[0].start()
    load_h.start()
    load_cv(0).start()
    load_cv(1).start()
    for zz in range(4):
        turn_c(core, zz)
    b_copy = remote(m["b"].at[0], m["b"].at[1], place.partner["cc"])
    ev_copy = remote(m["ev"].at[0], m["ev"].at[1], across)
    for p in range(PIECES):
        x_part(p, core, m["xw", p])
        if p + 1 < PIECES:
            x_part(p + 1, other, m["xs", p + 1])
            xc[p + 1].start()
    b_copy.start()

    tasks, finished, have_b = {}, set(), []

    def advance(n):
        if n in tasks:
            try:
                next(tasks[n])
            except StopIteration:
                del tasks[n]
                finished.add(n)

    def complete(n):
        while n in tasks:
            advance(n)

    def launch(n, g):
        tasks[n] = g
        advance(n)

    def steps(streams, n):
        for _ in range(n - 1):
            yield
            for g in streams:
                next(g)
        yield
        drive(streams)

    def piece(p):
        yield
        xc[p].wait()
        m["xw", p][...] = m["xw", p][...] + m["xr", p][...].reshape(2, 2, R, 1024)
        streams = start_all([
            scatter_stream(place, m["xw", p], ("za", "zb"), Z_ORDERS[s],
                           (pl.ds(R // 2 * s, R // 2),),
                           [m[("xrec", p, s), t] for t in range(2)], sems) for s in range(2)])
        yield from steps(streams, 2)
        m["xf", p][zmine] = m["xw", p][zmine]
        streams = start_all([
            gather_stream(place, m["xf", p], ("za", "zb"), Z_ORDERS[s][::-1],
                          (pl.ds(R // 2 * s, R // 2),), sems) for s in range(2)])
        yield from steps(streams, 2)
        if not have_b:
            b_copy.wait()
            have_b.append(p)
        hi, lo = split(m["xf", p][...].reshape(4 * R, 1024))
        both = jnp.concatenate([hi, lo], axis=0)
        for side in range(2):
            xlo = core if side == 0 else other
            for half in range(2):
                rows = pl.ds(384 * half, 384)
                acc = nt(both[:, :512], m["b"][side, 0, rows])
                acc += nt(both[:, 512:], m["b"][side, 1, rows])
                acc = acc[:4 * R] + acc[4 * R:]
                for zz in range(4):
                    m["yw", p][(xlo + half) % 2, half, (zz + zz // 2) % 2, zz // 2] = (
                        acc[R * zz: R * zz + R])
        streams = start_all([
            scatter_stream(place, m["yw", p], XY, XY_ORDERS[s], (pl.ds(R // 4 * s, R // 4),),
                           [m[("yrec", p, s), t] for t in range(4)], sems) for s in range(4)])
        yield from steps(streams, 4)
        swap = remote(m["yw", p].at[xmine], m["yb", p], swapped)

        @pl.when(y != z)
        def _():
            swap.start()

        @pl.when(y == z)
        def _():
            m["yb", p][...] = m["yw", p][xmine]

        yield
        complete(4)
        complete(6)

        @pl.when(y != z)
        def _():
            swap.wait()

        image = m["hw"][rmine + (pl.ds(R * p, R),)] - m["yb", p][...]
        hi, lo = split(image)
        both = jnp.concatenate([hi, lo], axis=0)
        for aux in range(8):
            sl = pl.ds(640 * aux, 640)
            acc = nn(both, m["cvh"][:, sl])
            acc = acc[:R] + acc[R:] + nn(hi, m["cvl"][:, sl])
            for c in range(2):
                m["gw", p][xy_bits(aux, c)] = acc[Q * c: Q * c + Q]
        streams = start_all([
            scatter_stream(place, m["gw", p], XY, order, tail,
                           [m[("grec", p, s), t] for t in range(4)], sems)
            for s, (tail, order) in enumerate(grad_cuts(p))])
        yield from steps(streams, 4)
        ev = m["ev"][0, 0:1] + m["ev"][1, 0:1]
        eo = m["eo"][pl.ds(R * p + Q * col, Q), 0:1]
        m["kc"][xmine + (p,)] = m["gw", p][xmine] / (ev - eo)
        mine = pl.ds(pl.multiple_of(256 * col, 128), 384)
        theirs = pl.ds(pl.multiple_of(256 - 256 * col, 128), 384)
        m["kg"][rmine + (p, col)] = m["kc"][xmine + (p, slice(None), mine)]
        m["win"][p] = m["kc"][xmine + (p, slice(None), theirs)]
        window = remote(m["win"].at[p], m["kg"].at[rmine + (p, col)], across)
        window.start()
        launch(7 + p, gather_piece(p))
        yield
        window.wait()
        streams = start_all([
            gather_stream(place, m["kg"], ROW, Z_ORDERS[s] + ("cc",), (p, s), sems)
            for s in range(2)])
        yield from steps(streams, 3)

    def gather_piece(p):
        yield from steps(start_all([
            gather_stream(place, m["kc"], XY, XY_ORDERS[p][::-1], (p,), sems)]), 4)

    def h_task():
        yield
        load_h.wait()
        hi, lo = split(m["hc"][...])
        m["hch"][...] = hi
        m["hcl"][...] = lo
        for r in range(8):
            chi = m["ct"][r % 2, :, 0, r // 2].reshape(128, 768)
            clo = m["ct"][r % 2, :, 1, r // 2].reshape(128, 768)
            m["hw"][row_bits(r)] = (
                nn(chi, m["hch"][...]) + nn(clo, m["hch"][...]) + nn(chi, m["hcl"][...]))
            if r == 3:
                yield
        yield from steps(start_all([
            scatter_stream(place, m["hw"], ROW, ROW_ORDERS[s], (pl.ds(64 * s, 64),),
                           [m[("hrec", s), t] for t in range(3)], sems) for s in range(2)]), 3)

    def c_rows():
        source = row_bits(place.aux)
        yield

        @pl.when(place.aux == place.row)
        def _():
            m["cg"][...] = m["c"][pl.ds(pl.multiple_of(384 * col, 384), 384)]

        differs = {d: (place.bit[d] - source[ROW.index(d)]) * (place.bit[d] - source[ROW.index(d)])
                   for d in ROW}
        for k in range(3):
            copies = []
            for s in range(2):
                order = Z_ORDERS[s] + ("cc",)
                later = sum((differs[d] for d in order[k + 1:]), 0)
                at = m["cg"].at[pl.ds(192 * s, 192)]
                copy = remote(at, at, place.partner[order[k]])
                sends = later + differs[order[k]] == 0
                takes = later + (1 - differs[order[k]]) == 0
                copies.append((copy, sends, takes))

                @pl.when(sends)
                def _():
                    copy.start()

            yield
            for copy, sends, takes in copies:
                @pl.when(sends)
                def _():
                    copy.wait_send()

                @pl.when(takes)
                def _():
                    copy.wait_recv()

    def cv_task():
        m["ev"][0] = jnp.zeros((8, 640), F32)
        value = jnp.broadcast_to(ev_in[...], (8, 320))

        @pl.when(col == 0)
        def _():
            m["ev"][0, :, :320] = value

        @pl.when(col == 1)
        def _():
            m["ev"][0, :, 320:] = value

        ev_copy.start()
        m["eo"][...] = jnp.broadcast_to(eo_in[...], (8, 128)).T
        for k in range(20):
            if k % 4 == 0:
                yield
            load_cv(k).wait()
            hi, lo = split(m["cv"][k % 2])
            m["cvh"][:, pl.ds(256 * k, 256)] = hi
            m["cvl"][:, pl.ds(256 * k, 256)] = lo
            if k + 2 < 20:
                load_cv(k + 2).start()
        ev_copy.wait()

    def w_task():
        w = 0.0
        for aux in range(8):
            if aux % 2 == 0:
                yield
            k0 = m["kc"][xy_bits(aux, 0)]
            k1 = m["kc"][xy_bits(aux, 1)]
            kh, kl = split(jnp.concatenate([k0[:, None], k1[:, None]], axis=1).reshape(128, 640))
            ch, cl = m["cvh"][:, pl.ds(640 * aux, 640)], m["cvl"][:, pl.ds(640 * aux, 640)]
            both = nt(ch, jnp.concatenate([kh, kl], axis=0))
            w = w + both[:, :128] + both[:, 128:] + nt(cl, kh)
        m["wfull"][rmine] = w
        yield from steps(start_all([
            gather_stream(place, m["wfull"], ROW, Z_ORDERS[s] + ("cc",),
                          (pl.ds(192 * s, 192),), sems) for s in range(2)]), 3)

    def place_blocks(r):
        chunks = [m["gfull"][(i // 8, (i // 4) % 2, (i // 2) % 2, i % 2) + row_bits(r)]
                  for i in range(16)]
        column = jnp.concatenate(chunks, axis=0)
        for k in range(5):
            block = column[128 * k: 128 * k + 128]
            i = (r + k) % 8
            hi, lo = split(block)
            m["ghi"][pl.ds(128 * i, 128), pl.ds(128 * r, 128)] = hi
            m["glo"][pl.ds(128 * i, 128), pl.ds(128 * r, 128)] = lo
            if 0 < k < 4:
                hi, lo = split(block.T)
                m["ghi"][pl.ds(128 * r, 128), pl.ds(128 * i, 128)] = hi
                m["glo"][pl.ds(128 * r, 128), pl.ds(128 * i, 128)] = lo
        return column[:128]

    def g_task():
        lanes = lax.broadcasted_iota(jnp.int32, (128, 384), 1)
        rhs = m["kg"][rmine].reshape(128, 384)
        rh, rl = split(jnp.where(lanes >= 128 * col, rhs, 0.0))
        accs = []
        for k in range(5):
            lh, ll = split(m["kg"][row_bits((place.row + k) % 8)].reshape(128, 384))
            accs.append(nt(lh, rh) + nt(lh, rl) + nt(ll, rh))
        acc = jnp.concatenate(accs, axis=0)
        for k in range(16):
            m["gs"][k // 8, (k // 4) % 2, (k // 2) % 2, k % 2] = acc[40 * k: 40 * k + 40]
        yield from steps(start_all([
            scatter_stream(place, m["gs"], XY, XY_ORDERS[s], (pl.ds(*cut),),
                           [m[("gsrec", s), t] for t in range(4)], sems)
            for s, cut in enumerate(G_CUTS)]), 4)
        m["gfull"][xmine + rmine] = m["gs"][xmine]
        yield from steps(start_all([
            gather_stream(place, m["gfull"], XY + ROW, G_ORDERS[s], (pl.ds(8 * s, 8),), sems)
            for s in range(5)]), 7)

    for p in range(PIECES):
        launch(p, piece(p))
    launch(4, h_task())
    launch(5, c_rows())
    launch(6, cv_task())

    def follow():
        if 12 not in tasks and 12 not in finished and finished.issuperset(range(PIECES)):
            launch(12, g_task())
        if 11 not in tasks and 11 not in finished and finished.issuperset(range(7, 7 + PIECES)):
            launch(11, w_task())

    for n in SCHEDULE:
        advance(n)
        follow()
    while tasks:
        for n in sorted(tasks):
            advance(n)
        follow()

    ghi, glo, t, acc_ref = m["ghi"], m["glo"], m["t"], m["acc"]
    r128 = lax.broadcasted_iota(jnp.int32, (128, 128), 0)
    l128 = lax.broadcasted_iota(jnp.int32, (128, 128), 1)
    total = jnp.zeros((128, 128), F32)
    for r in range(8):
        total = total + jnp.where(r128 == l128, place_blocks(r), 0.0)
    meansq = jnp.sum(total, axis=(0, 1), keepdims=True) / entries
    s1 = ROTATION_SCALE / jnp.sqrt(meansq + 1e-06)
    s2 = s1 * s1
    at = pl.ds(pl.multiple_of(128 * place.row, 128), 128)
    t[0, :, :128] = ghi[:, at]
    t[0, :, 128:] = glo[:, at]
    rows8 = lax.broadcasted_iota(jnp.int32, (1024, 128), 0)
    lanes8 = lax.broadcasted_iota(jnp.int32, (1024, 128), 1)
    g1 = (ghi[:, at].astype(F32) + glo[:, at].astype(F32)) * s2
    eye = jnp.where(rows8 == lanes8 + 128 * place.row, 1.0, 0.0)
    acc_ref[0] = eye - g1 * 0.5
    acc_ref[1] = eye - g1 * (1.0 / 6.0)
    coeff = [(1.0 / 24.0, 1.0 / 120.0), (-1.0 / 720.0, -1.0 / 5040.0), (1.0 / 40320.0, 0.0)]
    for k, (ce, cs) in enumerate(coeff):
        now, later = k % 2, (k + 1) % 2
        scale = s2 * s2 if k == 0 else s2

        @pl.loop(0, 4)
        def _(i):
            rs = pl.ds(pl.multiple_of(i * 256, 256), 256)
            high = nn(ghi[rs], t[now])
            power = (high[:, :128] + high[:, 128:] + nn(glo[rs], t[now, :, :128])) * scale
            if k < 2:
                hi, lo = split(power)
                t[later, rs, :128] = hi
                t[later, rs, 128:] = lo
                acc_ref[1, rs] = acc_ref[1, rs] + power * cs
            acc_ref[0, rs] = acc_ref[0, rs] + power * ce

    e_hi, e_lo = split(acc_ref[0])
    c_hi, c_lo = split(m["cg"][...])
    both = nn(c_hi, jnp.concatenate([e_hi, e_lo], axis=1))
    result = both[:, :128] + both[:, 128:] + nn(c_lo, e_hi)
    s_hi, s_lo = split(acc_ref[1] * s1)
    w_all = jnp.concatenate([m["wfull"][row_bits(r)] for r in range(8)], axis=1)
    w_hi, w_lo = split(w_all)
    both = nn(w_hi, jnp.concatenate([s_hi, s_lo], axis=1))
    out[...] = result + both[:, :128] + both[:, 128:] + nn(w_lo, s_hi)


def on_device(b_tensor, hcore, c_occ, c_virt, eps_occ, eps_virt):
    entries = float(c_virt.shape[1] * c_occ.shape[1])
    bag = scratch()
    return call(functools.partial(kernel, bag, entries), jax.ShapeDtypeStruct((384, 128), F32),
                [ANY, ANY, ANY, ANY, VM, VM], bag.shapes, 0,
                b_tensor, hcore, c_occ, c_virt, eps_virt[None, :], eps_occ[None, :])


def solution(mesh):
    placed = (
        P("aux", "row", "col"),
        P("row", ("aux", "col")),
        P("row", None),
        P(("aux", "col"), None),
        P("row"),
        P(("aux", "col")),
    )
    return jax.shard_map(
        on_device, mesh=mesh, in_specs=placed, out_specs=P(("aux", "col"), "row"), check_vma=False
    )
```

```python
import functools

import jax
import jax.numpy as jnp
from jax import lax
from jax.experimental import pallas as pl
from jax.experimental.pallas import tpu as pltpu
from jax.sharding import PartitionSpec as P

ROTATION_SCALE = 0.03
MESH = pl.DeviceIdType.MESH
F32 = jnp.float32
BF16 = jnp.bfloat16
XY = ("xa", "xb", "ya", "yb")
ROW = ("za", "zb", "cc")
VMEM_LIMIT = 62 * 1024 * 1024


class Place:
    def __init__(self):
        aux, row, col = (lax.axis_index(n) for n in ("aux", "row", "col"))
        y, xl = aux // 2, aux % 2
        z, core = row // 2, row % 2
        self.aux, self.row, self.col = aux, row, col
        self.bit = {
            "xa": (xl + col) % 2, "xb": col,
            "ya": (y + y // 2) % 2, "yb": y // 2,
            "za": (z + z // 2) % 2, "zb": z // 2,
            "cc": core,
        }
        self.partner = {
            "xa": (aux + 1 - 2 * xl, row, col),
            "xb": (aux + 1 - 2 * xl, row, 1 - col),
            "ya": (aux + 2 - 4 * (y % 2), row, col),
            "yb": (2 * (3 - y) + xl, row, col),
            "za": (aux, row + 2 - 4 * (z % 2), col),
            "zb": (aux, 2 * (3 - z) + core, col),
            "cc": (aux, row + 1 - 2 * core, col),
        }

    def greet(self, dims, swap=False):
        barrier = pltpu.get_barrier_semaphore()
        for d in dims:
            pl.semaphore_signal(barrier, inc=1, device_id=self.partner[d], device_id_type=MESH)
        if not swap:
            pl.semaphore_wait(barrier, len(dims))
            return

        @pl.when(self.aux != self.row)
        def _():
            pl.semaphore_signal(
                barrier, inc=1, device_id=(self.row, self.aux, self.col), device_id_type=MESH
            )
            pl.semaphore_wait(barrier, len(dims) + 1)

        @pl.when(self.aux == self.row)
        def _():
            pl.semaphore_wait(barrier, len(dims))


def xy_bits(aux, col):
    y, xl = aux // 2, aux % 2
    return ((xl + col) % 2, col, (y + y // 2) % 2, y // 2)


def row_bits(row):
    z, core = row // 2, row % 2
    return ((z + z // 2) % 2, z // 2, core)


class Sems:
    def __init__(self, send, recv):
        self.send, self.recv, self.n = send, recv, 0

    def take(self):
        n = self.n
        self.n += 1
        assert self.n <= self.send.shape[0]
        return self.send.at[n], self.recv.at[n]


def scatter_stream(place, work, axes, order, tail, recvs, sems):
    done = []
    for step, d in enumerate(order):
        def index(bit_of_d):
            return tuple(
                place.bit[a] if a in done else (bit_of_d if a == d else slice(None)) for a in axes
            ) + tail
        mine, theirs = index(place.bit[d]), index(1 - place.bit[d])
        s, r = sems.take()
        copy = pltpu.make_async_remote_copy(
            src_ref=work.at[theirs], dst_ref=recvs[step], send_sem=s, recv_sem=r,
            device_id=place.partner[d], device_id_type=MESH,
        )
        copy.start()
        yield
        copy.wait()
        work[mine] = work[mine] + recvs[step][...]
        done.append(d)


def gather_stream(place, full, axes, order, tail, sems):
    done = []
    for d in order:
        sl = tuple(slice(None) if a in done else place.bit[a] for a in axes) + tail
        s, r = sems.take()
        copy = pltpu.make_async_remote_copy(
            src_ref=full.at[sl], dst_ref=full.at[sl], send_sem=s, recv_sem=r,
            device_id=place.partner[d], device_id_type=MESH,
        )
        copy.start()
        yield
        copy.wait()
        done.append(d)


def drive(streams):
    streams = list(streams)
    while streams:
        alive = []
        for g in streams:
            try:
                next(g)
                alive.append(g)
            except StopIteration:
                pass
        streams = alive


def rotate(dims, k):
    return tuple(dims[k:]) + tuple(dims[:k])


XY_ORDERS = [("xa", "ya", "xb", "yb"), ("xb", "yb", "xa", "ya"),
             ("ya", "xa", "yb", "xb"), ("yb", "xb", "ya", "xa")]
ROW_ORDERS = [("cc", "za", "zb"), ("cc", "zb", "za")]


def recv_shapes(n, block):
    return [pltpu.VMEM((2,) * (n - 1 - t) + block, F32) for t in range(n)]


def dma(n):
    return pltpu.SemaphoreType.DMA((n,))


ANY = pl.BlockSpec(memory_space=pl.ANY)
VM = pl.BlockSpec(memory_space=pltpu.VMEM)


def call(kernel, outs, in_specs, scratch, cid, *args):
    return pl.pallas_call(
        kernel,
        out_shape=outs,
        in_specs=in_specs,
        out_specs=jax.tree.map(lambda _: VM, outs),
        scratch_shapes=scratch,
        compiler_params=pltpu.CompilerParams(
            collective_id=cid, has_side_effects=True, vmem_limit_bytes=VMEM_LIMIT
        ),
    )(*args)


def split(x):
    hi = x.astype(BF16)
    return hi, (x - hi.astype(F32)).astype(BF16)


def start_all(streams):
    for g in streams:
        next(g)
    return streams


def nt(a, b):
    return lax.dot_general(a, b, (((1,), (1,)), ((), ())), preferred_element_type=F32)


def nn(a, b):
    return jnp.dot(a, b, preferred_element_type=F32)


class Bag:
    def __init__(self):
        self.names, self.shapes = [], []

    def add(self, name, shape):
        self.names.append(name)
        self.shapes.append(shape)

    def recvs(self, name, n, block):
        for t, s in enumerate(recv_shapes(n, block)):
            self.add((name, t), s)

    def bind(self, refs):
        return dict(zip(self.names, refs))


LIMIT = 16383.0


def pack(parts):
    peak = jnp.max(jnp.abs(parts[0]), axis=0)
    for v in parts[1:]:
        peak = jnp.maximum(peak, jnp.max(jnp.abs(v), axis=0))
    peak = jnp.maximum(peak, 1e-30)
    n = [jnp.round(v * (LIMIT / peak)) for v in parts]
    h3, h4 = jnp.floor(n[3] * (1 / 32)), jnp.floor(n[4] * (1 / 32))
    words = [n[0] * 1024 + h3, n[1] * 1024 + h4,
             n[2] * 1024 + ((n[3] - 32 * h3) * 32 + (n[4] - 32 * h4) - 512)]
    if len(parts) == 8:
        h = jnp.floor(n[7] * (1 / 128))
        words += [n[5] * 256 + h, n[6] * 256 + (n[7] - 128 * h)]
    return peak * (1 / LIMIT), words


def unpack(scale, words):
    top = [jnp.floor((w + 512) * (1 / 1024)) for w in words[:3]]
    h3, h4, rest = (w - 1024 * t for w, t in zip(words, top))
    rest = rest + 512
    l3 = jnp.floor(rest * (1 / 32))
    n = top + [h3 * 32 + l3, h4 * 32 + (rest - 32 * l3)]
    if len(words) == 5:
        n5 = jnp.floor((words[3] + 128) * (1 / 256))
        n6 = jnp.floor(words[4] * (1 / 256))
        n += [n5, n6, (words[3] - 256 * n5) * 128 + (words[4] - 256 * n6)]
    return [v * scale for v in n]


def pack_into(ref, block):
    k = block.shape[-1] // 128
    block = block.reshape(-1, 8, block.shape[-1])
    m = block.shape[0]
    scale, words = pack([block[..., 128 * i: 128 * i + 128] for i in range(k)])
    ref[0] = scale
    for j, w in enumerate(words):
        ref[1 + j * m: 1 + (j + 1) * m] = w


def unpack_from(wire, m):
    words = [wire[1 + j * m: 1 + (j + 1) * m] for j in range((wire.shape[0] - 1) // m)]
    return unpack(wire[0], words)


PIECES = 4
R = 128 // PIECES
Q = R // 2
G_CUTS = ((0, 16), (16, 8), (24, 8), (32, 8))
G_ORDERS = [("za", "zb") + o[::-1] + ("cc",) for o in XY_ORDERS] + [XY_ORDERS[0] + ("za", "zb", "cc")]
Z_ORDERS = (("za", "zb"), ("zb", "za"))
SCHEDULE = [
    0, 4, 1, 3, 4, 0, 2, 6, 6, 1, 6, 6, 3, 6, 0, 2, 1, 3, 0, 2, 1, 3, 0, 2,
    1, 3, 0, 2, 1, 4, 3, 0, 2, 1, 3, 0, 4, 2, 1, 3, 0, 5, 2, 1, 3, 4, 2, 0,
    1, 3, 2, 0, 5, 1, 3, 2, 0, 1, 3, 2, 0, 1, 3, 2, 0, 1, 5, 3, 2, 7, 8, 0,
    5, 10, 1, 9, 3, 2, 7, 0, 8, 1, 10, 3, 9, 2, 0, 7, 1, 8, 0, 3, 10, 1, 2, 9,
    3, 2, 12, 12, 12, 7, 8, 9, 12, 10, 11, 11, 11, 12, 11, 12, 11, 12, 12, 11, 12, 11, 12, 12,
]


def grad_cuts(p):
    return [((slice(None), pl.ds(128 * s, 128)), XY_ORDERS[s if s < 4 else p]) for s in range(5)]


def scratch():
    bag, vm = Bag(), pltpu.VMEM
    bag.add("b", vm((2, 2, 768, 512), BF16))
    bag.add("c", vm((768, 1024), F32))
    bag.add("cg", vm((384, 1024), F32))
    bag.add("hc", vm((768, 384), F32))
    bag.add("ct", vm((2, PIECES, 2, 4, R, 768), BF16))
    bag.add("hch", vm((768, 384), BF16))
    bag.add("hcl", vm((768, 384), BF16))
    bag.add("cv", vm((2, 384, 256), F32))
    bag.add("cvh", vm((384, 5120), BF16))
    bag.add("cvl", vm((384, 5120), BF16))
    bag.add("ev", vm((2, 8, 640), F32))
    bag.add("eo", vm((128, 8), F32))
    for p in range(PIECES):
        bag.add(("xs", p), vm((4, R, 1024), F32))
        bag.add(("xr", p), vm((4, R, 1024), F32))
        bag.add(("xw", p), vm((2, 2, R, 1024), F32))
        bag.add(("xf", p), vm((2, 2, R, 1024), F32))
        bag.add(("yw", p), vm((2, 2, 2, 2, R, 384), F32))
        bag.add(("yb", p), vm((R, 384), F32))
        bag.add(("gw", p), vm((2, 2, 2, 2, Q, 640), F32))
        for s in range(2):
            for t, tiles in enumerate((4, 2)):
                bag.add(("xout", p, s, t), vm((5 * tiles + 1, 8, 128), F32))
                bag.add(("xin", p, s, t), vm((5 * tiles + 1, 8, 128), F32))
            bag.add(("xg", p, s), vm((2, 2, 11, 8, 128), F32))
        for s in range(4):
            bag.recvs(("yrec", p, s), 4, (R // 4, 384))
        for s in range(5):
            bag.recvs(("grec", p, s), 4, (Q, 128))
    for s in range(2):
        bag.recvs(("hrec", s), 3, (64, 384))
    bag.add("hw", vm((2, 2, 2, 128, 384), F32))
    bag.add("kc", vm((2, 2, 2, 2, PIECES, 7, 8, 128), F32))
    bag.add("own", vm((PIECES, Q, 640), F32))
    bag.add("kg", vm((2, 2, 2, PIECES, 2, Q, 384), F32))
    bag.add("win", vm((PIECES, Q, 384), F32))
    bag.add("gs", vm((2, 2, 2, 2, 40, 128), F32))
    for s, (_, n) in enumerate(G_CUTS):
        bag.recvs(("gsrec", s), 4, (n, 128))
    bag.add("gfull", vm((2,) * 7 + (40, 128), F32))
    bag.add("wfull", vm((2, 2, 2, 384, 128), F32))
    bag.add("ghi", vm((1024, 1024), BF16))
    bag.add("glo", vm((1024, 1024), BF16))
    bag.add("t", vm((2, 1024, 256), BF16))
    bag.add("acc", vm((2, 1024, 128), F32))
    bag.add("local", dma(12))
    bag.add("send", dma(320))
    bag.add("recv", dma(320))
    return bag


def kernel(bag, entries, b_in, h_in, c_in, cv_in, ev_in, eo_in, out, *refs):
    m = bag.bind(refs)
    place = Place()
    sems = Sems(m["send"], m["recv"])
    core, col = place.row % 2, place.col
    other = 1 - core
    y, z = place.aux // 2, place.row // 2
    across = (place.aux, place.row, 1 - col)
    swapped = (2 * z + place.aux % 2, 2 * y + core, col)
    xmine = tuple(place.bit[d] for d in XY)
    rmine = tuple(place.bit[d] for d in ROW)
    zmine = rmine[:2]

    def remote(src, dst, device):
        s, r = sems.take()
        return pltpu.make_async_remote_copy(
            src_ref=src, dst_ref=dst, send_sem=s, recv_sem=r,
            device_id=device, device_id_type=MESH)

    def load_c(k, zz):
        sl = pl.ds(pl.multiple_of(128 * (2 * zz + k), 128), 128)
        which = zz if k is core else 4 + zz
        return pltpu.make_async_copy(c_in.at[:, sl], m["c"].at[:, sl], m["local"].at[which])

    load_b = pltpu.make_async_copy(b_in, m["b"].at[0], m["local"].at[8])
    load_h = pltpu.make_async_copy(h_in, m["hc"], m["local"].at[9])

    def load_cv(k):
        return pltpu.make_async_copy(
            cv_in.at[:, pl.ds(256 * k, 256)], m["cv"].at[k % 2], m["local"].at[10 + k % 2])

    for zz in range(4):
        load_c(other, zz).start()
    load_b.start()
    for zz in range(4):
        load_c(core, zz).start()
    barrier = pltpu.get_barrier_semaphore()
    dims = XY + ROW
    for d in dims:
        pl.semaphore_signal(barrier, inc=1, device_id=place.partner[d], device_id_type=MESH)
    pl.semaphore_signal(barrier, inc=1, device_id=across, device_id_type=MESH)

    @pl.when(y != z)
    def _():
        pl.semaphore_signal(barrier, inc=1, device_id=swapped, device_id_type=MESH)

    def turn_c(k, zz):
        load_c(k, zz).wait()
        sl = pl.ds(pl.multiple_of(128 * (2 * zz + k), 128), 128)
        hi, lo = split(m["c"][:, sl].T)
        m["ct"][k, :, 0, zz] = hi.reshape(PIECES, R, 768)
        m["ct"][k, :, 1, zz] = lo.reshape(PIECES, R, 768)

    def x_part(p, k, out_ref):
        both = m["ct"][k, p].reshape(8 * R, 768)
        for q in range(2):
            acc = nn(both, m["b"][0, q])
            out_ref[..., pl.ds(512 * q, 512)] = (acc[:4 * R] + acc[4 * R:]).reshape(
                out_ref.shape[:-1] + (512,))

    for zz in range(4):
        turn_c(other, zz)
    load_b.wait()
    x_part(0, other, m["xs", 0])

    @pl.when(y != z)
    def _():
        pl.semaphore_wait(barrier, len(dims) + 2)

    @pl.when(y == z)
    def _():
        pl.semaphore_wait(barrier, len(dims) + 1)

    xc = [remote(m["xs", p], m["xr", p], place.partner["cc"]) for p in range(PIECES)]
    xc[0].start()
    load_h.start()
    load_cv(0).start()
    load_cv(1).start()
    for zz in range(4):
        turn_c(core, zz)
    b_copy = remote(m["b"].at[0], m["b"].at[1], place.partner["cc"])
    ev_copy = remote(m["ev"].at[0], m["ev"].at[1], across)
    for p in range(PIECES):
        x_part(p, core, m["xw", p])
        if p + 1 < PIECES:
            x_part(p + 1, other, m["xs", p + 1])
            xc[p + 1].start()
    b_copy.start()

    tasks, finished, have_b = {}, set(), []

    def advance(n):
        if n in tasks:
            try:
                next(tasks[n])
            except StopIteration:
                del tasks[n]
                finished.add(n)

    def complete(n):
        while n in tasks:
            advance(n)

    def launch(n, g):
        tasks[n] = g
        advance(n)

    def steps(streams, n):
        for _ in range(n - 1):
            yield
            for g in streams:
                next(g)
        yield
        drive(streams)

    def x_scatter(p, s):
        work, rows, done = m["xw", p], pl.ds(16 * s, 16), []
        for t, d in enumerate(Z_ORDERS[s]):
            def index(bit):
                return tuple(place.bit[a] if a in done else (bit if a == d else slice(None))
                             for a in ("za", "zb")) + (rows,)
            mine, theirs = index(place.bit[d]), index(1 - place.bit[d])
            pack_into(m["xout", p, s, t], work[theirs])
            copy = remote(m["xout", p, s, t], m["xin", p, s, t], place.partner[d])
            copy.start()
            yield
            copy.wait()
            for k, v in enumerate(unpack_from(m["xin", p, s, t][...], (4, 2)[t])):
                at = mine + (pl.ds(128 * k, 128),)
                work[at] = work[at] + v.reshape((2, 16, 128) if t == 0 else (16, 128))
            done.append(d)

    def piece(p):
        yield
        xc[p].wait()
        m["xw", p][...] = m["xw", p][...] + m["xr", p][...].reshape(2, 2, R, 1024)
        streams = start_all([x_scatter(p, s) for s in range(2)])
        yield from steps(streams, 2)
        for s in range(2):
            pack_into(m["xg", p, s].at[zmine], m["xw", p][zmine + (pl.ds(16 * s, 16),)])
        streams = start_all([
            gather_stream(place, m["xg", p, s], ("za", "zb"), Z_ORDERS[s][::-1], (), sems)
            for s in range(2)])
        yield from steps(streams, 2)
        for s in range(2):
            for i in range(4):
                for k, v in enumerate(unpack_from(m["xg", p, s][i // 2, i % 2], 2)):
                    m["xf", p][i // 2, i % 2, pl.ds(16 * s, 16), pl.ds(128 * k, 128)] = (
                        v.reshape(16, 128))
        if not have_b:
            b_copy.wait()
            have_b.append(p)
        hi, lo = split(m["xf", p][...].reshape(4 * R, 1024))
        both = jnp.concatenate([hi, lo], axis=0)
        for side in range(2):
            xlo = core if side == 0 else other
            for half in range(2):
                rows = pl.ds(384 * half, 384)
                acc = nt(both[:, :512], m["b"][side, 0, rows])
                acc += nt(both[:, 512:], m["b"][side, 1, rows])
                acc = acc[:4 * R] + acc[4 * R:]
                for zz in range(4):
                    m["yw", p][(xlo + half) % 2, half, (zz + zz // 2) % 2, zz // 2] = (
                        acc[R * zz: R * zz + R])
        streams = start_all([
            scatter_stream(place, m["yw", p], XY, XY_ORDERS[s], (pl.ds(R // 4 * s, R // 4),),
                           [m[("yrec", p, s), t] for t in range(4)], sems) for s in range(4)])
        yield from steps(streams, 4)
        swap = remote(m["yw", p].at[xmine], m["yb", p], swapped)

        @pl.when(y != z)
        def _():
            swap.start()

        @pl.when(y == z)
        def _():
            m["yb", p][...] = m["yw", p][xmine]

        yield
        complete(4)
        complete(6)

        @pl.when(y != z)
        def _():
            swap.wait()

        image = m["hw"][rmine + (pl.ds(R * p, R),)] - m["yb", p][...]
        hi, lo = split(image)
        both = jnp.concatenate([hi, lo], axis=0)
        for aux in range(8):
            sl = pl.ds(640 * aux, 640)
            acc = nn(both, m["cvh"][:, sl])
            acc = acc[:R] + acc[R:] + nn(hi, m["cvl"][:, sl])
            for c in range(2):
                m["gw", p][xy_bits(aux, c)] = acc[Q * c: Q * c + Q]
        streams = start_all([
            scatter_stream(place, m["gw", p], XY, order, tail,
                           [m[("grec", p, s), t] for t in range(4)], sems)
            for s, (tail, order) in enumerate(grad_cuts(p))])
        yield from steps(streams, 4)
        ev = m["ev"][0, 0:1] + m["ev"][1, 0:1]
        eo = m["eo"][pl.ds(R * p + Q * col, Q), 0:1]
        m["own"][p] = m["gw", p][xmine] / (ev - eo)
        mine = pl.ds(pl.multiple_of(256 * col, 128), 384)
        theirs = pl.ds(pl.multiple_of(256 - 256 * col, 128), 384)
        m["kg"][rmine + (p, col)] = m["own"][p, :, mine]
        m["win"][p] = m["own"][p, :, theirs]
        window = remote(m["win"].at[p], m["kg"].at[rmine + (p, col)], across)
        window.start()
        launch(7 + p, gather_piece(p))
        yield
        window.wait()
        streams = start_all([
            gather_stream(place, m["kg"], ROW, Z_ORDERS[s] + ("cc",), (p, s), sems)
            for s in range(2)])
        yield from steps(streams, 3)

    def gather_piece(p):
        pack_into(m["kc"].at[xmine + (p,)], m["own"][p])
        yield from steps(start_all([
            gather_stream(place, m["kc"], XY, XY_ORDERS[p][::-1], (p,), sems)]), 4)

    def h_task():
        yield
        load_h.wait()
        hi, lo = split(m["hc"][...])
        m["hch"][...] = hi
        m["hcl"][...] = lo
        for r in range(8):
            chi = m["ct"][r % 2, :, 0, r // 2].reshape(128, 768)
            clo = m["ct"][r % 2, :, 1, r // 2].reshape(128, 768)
            m["hw"][row_bits(r)] = (
                nn(chi, m["hch"][...]) + nn(clo, m["hch"][...]) + nn(chi, m["hcl"][...]))
            if r == 3:
                yield
        yield from steps(start_all([
            scatter_stream(place, m["hw"], ROW, ROW_ORDERS[s], (pl.ds(64 * s, 64),),
                           [m[("hrec", s), t] for t in range(3)], sems) for s in range(2)]), 3)

    def c_rows():
        source = row_bits(place.aux)
        yield

        @pl.when(place.aux == place.row)
        def _():
            m["cg"][...] = m["c"][pl.ds(pl.multiple_of(384 * col, 384), 384)]

        differs = {d: (place.bit[d] - source[ROW.index(d)]) * (place.bit[d] - source[ROW.index(d)])
                   for d in ROW}
        for k in range(3):
            copies = []
            for s in range(2):
                order = Z_ORDERS[s] + ("cc",)
                later = sum((differs[d] for d in order[k + 1:]), 0)
                at = m["cg"].at[pl.ds(192 * s, 192)]
                copy = remote(at, at, place.partner[order[k]])
                sends = later + differs[order[k]] == 0
                takes = later + (1 - differs[order[k]]) == 0
                copies.append((copy, sends, takes))

                @pl.when(sends)
                def _():
                    copy.start()

            yield
            for copy, sends, takes in copies:
                @pl.when(sends)
                def _():
                    copy.wait_send()

                @pl.when(takes)
                def _():
                    copy.wait_recv()

    def cv_task():
        m["ev"][0] = jnp.zeros((8, 640), F32)
        value = jnp.broadcast_to(ev_in[...], (8, 320))

        @pl.when(col == 0)
        def _():
            m["ev"][0, :, :320] = value

        @pl.when(col == 1)
        def _():
            m["ev"][0, :, 320:] = value

        ev_copy.start()
        m["eo"][...] = jnp.broadcast_to(eo_in[...], (8, 128)).T
        for k in range(20):
            if k % 4 == 0:
                yield
            load_cv(k).wait()
            hi, lo = split(m["cv"][k % 2])
            m["cvh"][:, pl.ds(256 * k, 256)] = hi
            m["cvl"][:, pl.ds(256 * k, 256)] = lo
            if k + 2 < 20:
                load_cv(k + 2).start()
        ev_copy.wait()

    def w_task():
        w = 0.0
        for aux in range(8):
            if aux % 2 == 0:
                yield
            rows = []
            for p in range(PIECES):
                for c in range(2):
                    parts = unpack_from(m["kc"][xy_bits(aux, c) + (p,)], 2)
                    rows.append(jnp.concatenate([v.reshape(Q, 128) for v in parts], axis=1))
            kh, kl = split(jnp.concatenate(rows, axis=0))
            ch, cl = m["cvh"][:, pl.ds(640 * aux, 640)], m["cvl"][:, pl.ds(640 * aux, 640)]
            both = nt(ch, jnp.concatenate([kh, kl], axis=0))
            w = w + both[:, :128] + both[:, 128:] + nt(cl, kh)
        m["wfull"][rmine] = w
        yield from steps(start_all([
            gather_stream(place, m["wfull"], ROW, Z_ORDERS[s] + ("cc",),
                          (pl.ds(192 * s, 192),), sems) for s in range(2)]), 3)

    def place_blocks(r):
        chunks = [m["gfull"][(i // 8, (i // 4) % 2, (i // 2) % 2, i % 2) + row_bits(r)]
                  for i in range(16)]
        column = jnp.concatenate(chunks, axis=0)
        for k in range(5):
            block = column[128 * k: 128 * k + 128]
            i = (r + k) % 8
            hi, lo = split(block)
            m["ghi"][pl.ds(128 * i, 128), pl.ds(128 * r, 128)] = hi
            m["glo"][pl.ds(128 * i, 128), pl.ds(128 * r, 128)] = lo
            if 0 < k < 4:
                hi, lo = split(block.T)
                m["ghi"][pl.ds(128 * r, 128), pl.ds(128 * i, 128)] = hi
                m["glo"][pl.ds(128 * r, 128), pl.ds(128 * i, 128)] = lo
        return column[:128]

    def g_task():
        lanes = lax.broadcasted_iota(jnp.int32, (128, 384), 1)
        rhs = m["kg"][rmine].reshape(128, 384)
        rh, rl = split(jnp.where(lanes >= 128 * col, rhs, 0.0))
        accs = []
        for k in range(5):
            lh, ll = split(m["kg"][row_bits((place.row + k) % 8)].reshape(128, 384))
            accs.append(nt(lh, rh) + nt(lh, rl) + nt(ll, rh))
        acc = jnp.concatenate(accs, axis=0)
        for k in range(16):
            m["gs"][k // 8, (k // 4) % 2, (k // 2) % 2, k % 2] = acc[40 * k: 40 * k + 40]
        yield from steps(start_all([
            scatter_stream(place, m["gs"], XY, XY_ORDERS[s], (pl.ds(*cut),),
                           [m[("gsrec", s), t] for t in range(4)], sems)
            for s, cut in enumerate(G_CUTS)]), 4)
        m["gfull"][xmine + rmine] = m["gs"][xmine]
        yield from steps(start_all([
            gather_stream(place, m["gfull"], XY + ROW, G_ORDERS[s], (pl.ds(8 * s, 8),), sems)
            for s in range(5)]), 7)

    for p in range(PIECES):
        launch(p, piece(p))
    launch(4, h_task())
    launch(5, c_rows())
    launch(6, cv_task())

    def follow():
        if 12 not in tasks and 12 not in finished and finished.issuperset(range(PIECES)):
            launch(12, g_task())
        if 11 not in tasks and 11 not in finished and finished.issuperset(range(7, 7 + PIECES)):
            launch(11, w_task())

    for n in SCHEDULE:
        advance(n)
        follow()
    while tasks:
        for n in sorted(tasks):
            advance(n)
        follow()

    ghi, glo, t, acc_ref = m["ghi"], m["glo"], m["t"], m["acc"]
    r128 = lax.broadcasted_iota(jnp.int32, (128, 128), 0)
    l128 = lax.broadcasted_iota(jnp.int32, (128, 128), 1)
    total = jnp.zeros((128, 128), F32)
    for r in range(8):
        total = total + jnp.where(r128 == l128, place_blocks(r), 0.0)
    meansq = jnp.sum(total, axis=(0, 1), keepdims=True) / entries
    s1 = ROTATION_SCALE / jnp.sqrt(meansq + 1e-06)
    s2 = s1 * s1
    at = pl.ds(pl.multiple_of(128 * place.row, 128), 128)
    t[0, :, :128] = ghi[:, at]
    t[0, :, 128:] = glo[:, at]
    rows8 = lax.broadcasted_iota(jnp.int32, (1024, 128), 0)
    lanes8 = lax.broadcasted_iota(jnp.int32, (1024, 128), 1)
    g1 = (ghi[:, at].astype(F32) + glo[:, at].astype(F32)) * s2
    eye = jnp.where(rows8 == lanes8 + 128 * place.row, 1.0, 0.0)
    acc_ref[0] = eye - g1 * 0.5
    acc_ref[1] = eye - g1 * (1.0 / 6.0)
    coeff = [(1.0 / 24.0, 1.0 / 120.0), (-1.0 / 720.0, -1.0 / 5040.0), (1.0 / 40320.0, 0.0)]
    for k, (ce, cs) in enumerate(coeff):
        now, later = k % 2, (k + 1) % 2
        scale = s2 * s2 if k == 0 else s2

        @pl.loop(0, 4)
        def _(i):
            rs = pl.ds(pl.multiple_of(i * 256, 256), 256)
            high = nn(ghi[rs], t[now])
            power = (high[:, :128] + high[:, 128:] + nn(glo[rs], t[now, :, :128])) * scale
            if k < 2:
                hi, lo = split(power)
                t[later, rs, :128] = hi
                t[later, rs, 128:] = lo
                acc_ref[1, rs] = acc_ref[1, rs] + power * cs
            acc_ref[0, rs] = acc_ref[0, rs] + power * ce

    e_hi, e_lo = split(acc_ref[0])
    c_hi, c_lo = split(m["cg"][...])
    both = nn(c_hi, jnp.concatenate([e_hi, e_lo], axis=1))
    result = both[:, :128] + both[:, 128:] + nn(c_lo, e_hi)
    s_hi, s_lo = split(acc_ref[1] * s1)
    w_all = jnp.concatenate([m["wfull"][row_bits(r)] for r in range(8)], axis=1)
    w_hi, w_lo = split(w_all)
    both = nn(w_hi, jnp.concatenate([s_hi, s_lo], axis=1))
    out[...] = result + both[:, :128] + both[:, 128:] + nn(w_lo, s_hi)


def on_device(b_tensor, hcore, c_occ, c_virt, eps_occ, eps_virt):
    entries = float(c_virt.shape[1] * c_occ.shape[1])
    bag = scratch()
    return call(functools.partial(kernel, bag, entries), jax.ShapeDtypeStruct((384, 128), F32),
                [ANY, ANY, ANY, ANY, VM, VM], bag.shapes, 0,
                b_tensor, hcore, c_occ, c_virt, eps_virt[None, :], eps_occ[None, :])


def solution(mesh):
    placed = (
        P("aux", "row", "col"),
        P("row", ("aux", "col")),
        P("row", None),
        P(("aux", "col"), None),
        P("row"),
        P(("aux", "col")),
    )
    return jax.shard_map(
        on_device, mesh=mesh, in_specs=placed, out_specs=P(("aux", "col"), "row"), check_vma=False
    )
```

```python
import functools

import jax
import jax.numpy as jnp
from jax import lax
from jax.experimental import pallas as pl
from jax.experimental.pallas import tpu as pltpu
from jax.sharding import PartitionSpec as P

ROTATION_SCALE = 0.03
MESH = pl.DeviceIdType.MESH
F32 = jnp.float32
BF16 = jnp.bfloat16
XY = ("xa", "xb", "ya", "yb")
ROW = ("za", "zb", "cc")
VMEM_LIMIT = 62 * 1024 * 1024


class Place:
    def __init__(self):
        aux, row, col = (lax.axis_index(n) for n in ("aux", "row", "col"))
        y, xl = aux // 2, aux % 2
        z, core = row // 2, row % 2
        self.aux, self.row, self.col = aux, row, col
        self.bit = {
            "xa": (xl + col) % 2, "xb": col,
            "ya": (y + y // 2) % 2, "yb": y // 2,
            "za": (z + z // 2) % 2, "zb": z // 2,
            "cc": core,
        }
        self.partner = {
            "xa": (aux + 1 - 2 * xl, row, col),
            "xb": (aux + 1 - 2 * xl, row, 1 - col),
            "ya": (aux + 2 - 4 * (y % 2), row, col),
            "yb": (2 * (3 - y) + xl, row, col),
            "za": (aux, row + 2 - 4 * (z % 2), col),
            "zb": (aux, 2 * (3 - z) + core, col),
            "cc": (aux, row + 1 - 2 * core, col),
        }

    def greet(self, dims, swap=False):
        barrier = pltpu.get_barrier_semaphore()
        for d in dims:
            pl.semaphore_signal(barrier, inc=1, device_id=self.partner[d], device_id_type=MESH)
        if not swap:
            pl.semaphore_wait(barrier, len(dims))
            return

        @pl.when(self.aux != self.row)
        def _():
            pl.semaphore_signal(
                barrier, inc=1, device_id=(self.row, self.aux, self.col), device_id_type=MESH
            )
            pl.semaphore_wait(barrier, len(dims) + 1)

        @pl.when(self.aux == self.row)
        def _():
            pl.semaphore_wait(barrier, len(dims))


def xy_bits(aux, col):
    y, xl = aux // 2, aux % 2
    return ((xl + col) % 2, col, (y + y // 2) % 2, y // 2)


def row_bits(row):
    z, core = row // 2, row % 2
    return ((z + z // 2) % 2, z // 2, core)


class Sems:
    def __init__(self, send, recv):
        self.send, self.recv, self.n = send, recv, 0

    def take(self):
        n = self.n
        self.n += 1
        assert self.n <= self.send.shape[0]
        return self.send.at[n], self.recv.at[n]


def scatter_stream(place, work, axes, order, tail, recvs, sems):
    done = []
    for step, d in enumerate(order):
        def index(bit_of_d):
            return tuple(
                place.bit[a] if a in done else (bit_of_d if a == d else slice(None)) for a in axes
            ) + tail
        mine, theirs = index(place.bit[d]), index(1 - place.bit[d])
        s, r = sems.take()
        copy = pltpu.make_async_remote_copy(
            src_ref=work.at[theirs], dst_ref=recvs[step], send_sem=s, recv_sem=r,
            device_id=place.partner[d], device_id_type=MESH,
        )
        copy.start()
        yield
        copy.wait()
        work[mine] = work[mine] + recvs[step][...]
        done.append(d)


def gather_stream(place, full, axes, order, tail, sems):
    done = []
    for d in order:
        sl = tuple(slice(None) if a in done else place.bit[a] for a in axes) + tail
        s, r = sems.take()
        copy = pltpu.make_async_remote_copy(
            src_ref=full.at[sl], dst_ref=full.at[sl], send_sem=s, recv_sem=r,
            device_id=place.partner[d], device_id_type=MESH,
        )
        copy.start()
        yield
        copy.wait()
        done.append(d)


def drive(streams):
    streams = list(streams)
    while streams:
        alive = []
        for g in streams:
            try:
                next(g)
                alive.append(g)
            except StopIteration:
                pass
        streams = alive


def rotate(dims, k):
    return tuple(dims[k:]) + tuple(dims[:k])


XY_ORDERS = [("xa", "ya", "xb", "yb"), ("xb", "yb", "xa", "ya"),
             ("ya", "xa", "yb", "xb"), ("yb", "xb", "ya", "xa")]
ROW_ORDERS = [("cc", "za", "zb"), ("cc", "zb", "za")]


def recv_shapes(n, block):
    return [pltpu.VMEM((2,) * (n - 1 - t) + block, F32) for t in range(n)]


def dma(n):
    return pltpu.SemaphoreType.DMA((n,))


ANY = pl.BlockSpec(memory_space=pl.ANY)
VM = pl.BlockSpec(memory_space=pltpu.VMEM)


def call(kernel, outs, in_specs, scratch, cid, *args):
    return pl.pallas_call(
        kernel,
        out_shape=outs,
        in_specs=in_specs,
        out_specs=jax.tree.map(lambda _: VM, outs),
        scratch_shapes=scratch,
        compiler_params=pltpu.CompilerParams(
            collective_id=cid, has_side_effects=True, vmem_limit_bytes=VMEM_LIMIT
        ),
    )(*args)


def split(x):
    hi = x.astype(BF16)
    return hi, (x - hi.astype(F32)).astype(BF16)


def start_all(streams):
    for g in streams:
        next(g)
    return streams


def nt(a, b):
    return lax.dot_general(a, b, (((1,), (1,)), ((), ())), preferred_element_type=F32)


def nn(a, b):
    return jnp.dot(a, b, preferred_element_type=F32)


class Bag:
    def __init__(self):
        self.names, self.shapes = [], []

    def add(self, name, shape):
        self.names.append(name)
        self.shapes.append(shape)

    def recvs(self, name, n, block):
        for t, s in enumerate(recv_shapes(n, block)):
            self.add((name, t), s)

    def bind(self, refs):
        return dict(zip(self.names, refs))


LIMIT = 16383.0


def pack(parts):
    peak = jnp.max(jnp.abs(parts[0]), axis=0)
    for v in parts[1:]:
        peak = jnp.maximum(peak, jnp.max(jnp.abs(v), axis=0))
    peak = jnp.maximum(peak, 1e-30)
    n = [jnp.round(v * (LIMIT / peak)) for v in parts]
    words = []
    if len(n) >= 5:
        h3, h4 = jnp.floor(n[3] * (1 / 32)), jnp.floor(n[4] * (1 / 32))
        words += [n[0] * 1024 + h3, n[1] * 1024 + h4,
                  n[2] * 1024 + ((n[3] - 32 * h3) * 32 + (n[4] - 32 * h4) - 512)]
        n = n[5:]
    if n:
        h = jnp.floor(n[2] * (1 / 128))
        words += [n[0] * 256 + h, n[1] * 256 + (n[2] - 128 * h)]
    return peak * (1 / LIMIT), words


def unpack(scale, words):
    n = []
    if len(words) >= 3:
        n = [jnp.floor((w + 512) * (1 / 1024)) for w in words[:3]]
        h3, h4, rest = (w - 1024 * t for w, t in zip(words, n))
        rest = rest + 512
        l3 = jnp.floor(rest * (1 / 32))
        n += [h3 * 32 + l3, h4 * 32 + (rest - 32 * l3)]
        words = words[3:]
    if words:
        n5 = jnp.floor((words[0] + 128) * (1 / 256))
        n6 = jnp.floor(words[1] * (1 / 256))
        n += [n5, n6, (words[0] - 256 * n5) * 128 + (words[1] - 256 * n6)]
    return [v * scale for v in n]


def pack_into(ref, block):
    k = block.shape[-1] // 128
    block = block.reshape(-1, 8, block.shape[-1])
    m = block.shape[0]
    scale, words = pack([block[..., 128 * i: 128 * i + 128] for i in range(k)])
    ref[0] = scale
    for j, w in enumerate(words):
        ref[1 + j * m: 1 + (j + 1) * m] = w


def unpack_from(wire, m):
    words = [wire[1 + j * m: 1 + (j + 1) * m] for j in range((wire.shape[0] - 1) // m)]
    return unpack(wire[0], words)


PIECES = 4
R = 128 // PIECES
Q = R // 2
Z_ORDERS = (("za", "zb"), ("zb", "za"))
SCHEDULE = [
    0, 1, 2, 6, 6, 6, 0, 6, 6, 3, 1, 2, 0, 3, 1, 2, 0, 3, 4, 1, 2, 4, 0, 3,
    4, 1, 2, 0, 3, 1, 4, 5, 2, 0, 4, 3, 1, 0, 2, 3, 1, 5, 0, 2, 3, 1, 0, 2,
    3, 0, 1, 5, 7, 2, 3, 8, 5, 7, 1, 0, 9, 2, 0, 10, 3, 8, 9, 7, 1, 10, 1, 2,
    8, 2, 9, 3, 3, 10, 12, 12, 7, 8, 9, 10, 11, 11, 11, 11, 12, 11, 11, 12, 11, 12,
]


def scratch():
    bag, vm = Bag(), pltpu.VMEM
    bag.add("b", vm((2, 2, 768, 512), BF16))
    bag.add("c", vm((768, 1024), F32))
    bag.add("cg", vm((384, 1024), F32))
    bag.add("hc", vm((768, 384), F32))
    bag.add("ct", vm((2, PIECES, 2, 4, R, 768), BF16))
    bag.add("hch", vm((768, 384), BF16))
    bag.add("hcl", vm((768, 384), BF16))
    bag.add("cv", vm((2, 384, 256), F32))
    bag.add("cvh", vm((384, 5120), BF16))
    bag.add("cvl", vm((384, 5120), BF16))
    bag.add("ev", vm((2, 8, 640), F32))
    bag.add("eo", vm((128, 8), F32))
    for p in range(PIECES):
        bag.add(("xs", p), vm((4, R, 1024), F32))
        bag.add(("xr", p), vm((4, R, 1024), F32))
        bag.add(("xw", p), vm((2, 2, R, 1024), F32))
        bag.add(("xf", p), vm((2, 2, R, 1024), F32))
        bag.add(("yw", p), vm((4, 4, R, 384), F32))
        bag.add(("yb", p), vm((R, 384), F32))
        bag.add(("gw", p), vm((4, 4, Q, 640), F32))
        for s in range(2):
            for t, tiles in enumerate((4, 2)):
                bag.add(("xout", p, s, t), vm((5 * tiles + 1, 8, 128), F32))
                bag.add(("xin", p, s, t), vm((5 * tiles + 1, 8, 128), F32))
            bag.add(("xg", p, s), vm((2, 2, 11, 8, 128), F32))
        for s in range(2):
            for name, rows, lanes, words in (("y", R // 2, 384, 2), ("g", Q // 2, 640, 3)):
                packed = (3, words * rows // 2 + 1, 8, 128)
                bag.add((name + "out", p, s), vm(packed, F32))
                bag.add((name + "in", p, s), vm(packed, F32))
                bag.add((name + "raw", p, s), vm((3, rows, lanes), F32))
    for s in range(2):
        bag.recvs(("hrec", s), 3, (64, 384))
    bag.add("hw", vm((2, 2, 2, 128, 384), F32))
    bag.add("kc", vm((2, 2, 2, 2, PIECES, 7, 8, 128), F32))
    bag.add("own", vm((PIECES, Q, 640), F32))
    bag.add("kg", vm((2, 2, 2, PIECES, 2, Q, 384), F32))
    bag.add("win", vm((PIECES, Q, 384), F32))
    bag.add("gs", vm((2, 4, 80, 128), F32))
    bag.add("gs1", vm((2, 3, 80, 128), F32))
    bag.add("gs2", vm((2, 3, 80, 128), F32))
    bag.add("gfull", vm((2, 4, 4, 2, 80, 128), F32))
    bag.add("wfull", vm((2, 2, 2, 384, 128), F32))
    bag.add("ghi", vm((1024, 1024), BF16))
    bag.add("glo", vm((1024, 1024), BF16))
    bag.add("t", vm((2, 1024, 256), BF16))
    bag.add("acc", vm((2, 1024, 128), F32))
    bag.add("local", dma(12))
    bag.add("send", dma(320))
    bag.add("recv", dma(320))
    return bag


def kernel(bag, entries, b_in, h_in, c_in, cv_in, ev_in, eo_in, out, *refs):
    m = bag.bind(refs)
    place = Place()
    sems = Sems(m["send"], m["recv"])
    core, col = place.row % 2, place.col
    other = 1 - core
    y, z = place.aux // 2, place.row // 2
    across = (place.aux, place.row, 1 - col)
    swapped = (2 * z + place.aux % 2, 2 * y + core, col)
    xmine = tuple(place.bit[d] for d in XY)
    rmine = tuple(place.bit[d] for d in ROW)
    zmine = rmine[:2]
    at = {"x": 2 * col + place.aux % 2, "y": y, "z": z}
    ring = {}
    for d in (1, 2, 3):
        xd, yd, zd = ((at[a] + d) % 4 for a in "xyz")
        ring["x", d] = (2 * y + xd % 2, place.row, xd // 2)
        ring["y", d] = (2 * yd + place.aux % 2, place.row, col)
        ring["z", d] = (place.aux, 2 * zd + core, col)

    def remote(src, dst, device):
        s, r = sems.take()
        return pltpu.make_async_remote_copy(
            src_ref=src, dst_ref=dst, send_sem=s, recv_sem=r,
            device_id=device, device_id_type=MESH)

    def load_c(k, zz):
        sl = pl.ds(pl.multiple_of(128 * (2 * zz + k), 128), 128)
        which = zz if k is core else 4 + zz
        return pltpu.make_async_copy(c_in.at[:, sl], m["c"].at[:, sl], m["local"].at[which])

    load_b = pltpu.make_async_copy(b_in, m["b"].at[0], m["local"].at[8])
    load_h = pltpu.make_async_copy(h_in, m["hc"], m["local"].at[9])

    def load_cv(k):
        return pltpu.make_async_copy(
            cv_in.at[:, pl.ds(256 * k, 256)], m["cv"].at[k % 2], m["local"].at[10 + k % 2])

    for zz in range(4):
        load_c(other, zz).start()
    load_b.start()
    for zz in range(4):
        load_c(core, zz).start()
    barrier = pltpu.get_barrier_semaphore()
    dims = XY + ROW
    greeted = [place.partner[d] for d in dims] + [across, ring["y", 2], ring["z", 2]]
    for device in greeted:
        pl.semaphore_signal(barrier, inc=1, device_id=device, device_id_type=MESH)

    @pl.when(y != z)
    def _():
        pl.semaphore_signal(barrier, inc=1, device_id=swapped, device_id_type=MESH)

    def turn_c(k, zz):
        load_c(k, zz).wait()
        sl = pl.ds(pl.multiple_of(128 * (2 * zz + k), 128), 128)
        hi, lo = split(m["c"][:, sl].T)
        m["ct"][k, :, 0, zz] = hi.reshape(PIECES, R, 768)
        m["ct"][k, :, 1, zz] = lo.reshape(PIECES, R, 768)

    def x_part(p, k, out_ref):
        both = m["ct"][k, p].reshape(8 * R, 768)
        for q in range(2):
            acc = nn(both, m["b"][0, q])
            out_ref[..., pl.ds(512 * q, 512)] = (acc[:4 * R] + acc[4 * R:]).reshape(
                out_ref.shape[:-1] + (512,))

    for zz in range(4):
        turn_c(other, zz)
    load_b.wait()
    x_part(0, other, m["xs", 0])

    @pl.when(y != z)
    def _():
        pl.semaphore_wait(barrier, len(greeted) + 1)

    @pl.when(y == z)
    def _():
        pl.semaphore_wait(barrier, len(greeted))

    xc = [remote(m["xs", p], m["xr", p], place.partner["cc"]) for p in range(PIECES)]
    xc[0].start()
    load_h.start()
    load_cv(0).start()
    load_cv(1).start()
    for zz in range(4):
        turn_c(core, zz)
    b_copy = remote(m["b"].at[0], m["b"].at[1], place.partner["cc"])
    ev_copy = remote(m["ev"].at[0], m["ev"].at[1], across)
    for p in range(PIECES):
        x_part(p, core, m["xw", p])
        if p + 1 < PIECES:
            x_part(p + 1, other, m["xs", p + 1])
            xc[p + 1].start()
    b_copy.start()

    tasks, finished, have_b = {}, set(), []

    def advance(n):
        if n in tasks:
            try:
                next(tasks[n])
            except StopIteration:
                del tasks[n]
                finished.add(n)

    def complete(n):
        while n in tasks:
            advance(n)

    def launch(n, g):
        tasks[n] = g
        advance(n)

    def steps(streams, n):
        for _ in range(n - 1):
            yield
            for g in streams:
                next(g)
        yield
        drive(streams)

    def x_scatter(p, s):
        work, rows, done = m["xw", p], pl.ds(16 * s, 16), []
        for t, d in enumerate(Z_ORDERS[s]):
            def index(bit):
                return tuple(place.bit[a] if a in done else (bit if a == d else slice(None))
                             for a in ("za", "zb")) + (rows,)
            mine, theirs = index(place.bit[d]), index(1 - place.bit[d])
            pack_into(m["xout", p, s, t], work[theirs])
            copy = remote(m["xout", p, s, t], m["xin", p, s, t], place.partner[d])
            copy.start()
            yield
            copy.wait()
            for k, v in enumerate(unpack_from(m["xin", p, s, t][...], (4, 2)[t])):
                spot = mine + (pl.ds(128 * k, 128),)
                work[spot] = work[spot] + v.reshape((2, 16, 128) if t == 0 else (16, 128))
            done.append(d)

    def two_rings(work, s, rows, out, wire, raw):
        first, second = ("x", "y") if s == 0 else ("y", "x")
        lanes = work.shape[-1]
        tiles = (rows.size * 4) // 8

        def index(i, j):
            return ((i, j) if s == 0 else (j, i)) + (rows,)

        copies = []
        for d in (1, 2, 3):
            pack_into(out.at[d - 1], work[index((at[first] + d) % 4, slice(None))])
            copies.append(remote(out.at[d - 1], wire.at[d - 1], ring[first, d]))
            copies[-1].start()
        yield
        mine = index(at[first], slice(None))
        for c in copies:
            c.wait()
        got = [unpack_from(wire[d], tiles) for d in range(3)]
        for k in range(lanes // 128):
            place_k = mine + (pl.ds(128 * k, 128),)
            v = (got[0][k] + got[1][k]) + got[2][k]
            work[place_k] = work[place_k] + v.reshape(4, rows.size, 128)
        copies = []
        for d in (1, 2, 3):
            copies.append(remote(work.at[index(at[first], (at[second] + d) % 4)],
                                 raw.at[d - 1], ring[second, d]))
            copies[-1].start()
        yield
        for c in copies:
            c.wait()
        mine = index(at[first], at[second])
        work[mine] = (work[mine] + raw[0]) + (raw[1] + raw[2])

    def ring_gather(full, index, axis):
        copies = [remote(full.at[index], full.at[index], ring[axis, d]) for d in (1, 2, 3)]
        for c in copies:
            c.start()
        return copies

    def wait_all(copies):
        for c in copies:
            c.wait()

    def piece(p):
        yield
        xc[p].wait()
        m["xw", p][...] = m["xw", p][...] + m["xr", p][...].reshape(2, 2, R, 1024)
        streams = start_all([x_scatter(p, s) for s in range(2)])
        yield from steps(streams, 2)
        for s in range(2):
            pack_into(m["xg", p, s].at[zmine], m["xw", p][zmine + (pl.ds(16 * s, 16),)])
        streams = start_all([
            gather_stream(place, m["xg", p, s], ("za", "zb"), Z_ORDERS[s][::-1], (), sems)
            for s in range(2)])
        yield from steps(streams, 2)
        for s in range(2):
            for i in range(4):
                for k, v in enumerate(unpack_from(m["xg", p, s][i // 2, i % 2], 2)):
                    m["xf", p][i // 2, i % 2, pl.ds(16 * s, 16), pl.ds(128 * k, 128)] = (
                        v.reshape(16, 128))
        if not have_b:
            b_copy.wait()
            have_b.append(p)
        hi, lo = split(m["xf", p][...].reshape(4 * R, 1024))
        both = jnp.concatenate([hi, lo], axis=0)
        for side in range(2):
            xlo = core if side == 0 else other
            for half in range(2):
                rows = pl.ds(384 * half, 384)
                acc = nt(both[:, :512], m["b"][side, 0, rows])
                acc += nt(both[:, 512:], m["b"][side, 1, rows])
                acc = acc[:4 * R] + acc[4 * R:]
                for zz in range(4):
                    m["yw", p][2 * half + xlo, zz] = acc[R * zz: R * zz + R]
        streams = start_all([
            two_rings(m["yw", p], s, pl.ds(R // 2 * s, R // 2),
                      m["yout", p, s], m["yin", p, s], m["yraw", p, s]) for s in range(2)])
        yield from steps(streams, 2)
        swap = remote(m["yw", p].at[at["x"], y], m["yb", p], swapped)

        @pl.when(y != z)
        def _():
            swap.start()

        @pl.when(y == z)
        def _():
            m["yb", p][...] = m["yw", p][at["x"], y]

        yield
        complete(4)
        complete(6)

        @pl.when(y != z)
        def _():
            swap.wait()

        image = m["hw"][rmine + (pl.ds(R * p, R),)] - m["yb", p][...]
        hi, lo = split(image)
        both = jnp.concatenate([hi, lo], axis=0)
        for aux in range(8):
            sl = pl.ds(640 * aux, 640)
            acc = nn(both, m["cvh"][:, sl])
            acc = acc[:R] + acc[R:] + nn(hi, m["cvl"][:, sl])
            for c in range(2):
                m["gw", p][2 * c + aux % 2, aux // 2] = acc[Q * c: Q * c + Q]
        streams = start_all([
            two_rings(m["gw", p], s, pl.ds(Q // 2 * s, Q // 2),
                      m["gout", p, s], m["gin", p, s], m["graw", p, s]) for s in range(2)])
        yield from steps(streams, 2)
        ev = m["ev"][0, 0:1] + m["ev"][1, 0:1]
        eo = m["eo"][pl.ds(R * p + Q * col, Q), 0:1]
        m["own"][p] = m["gw", p][at["x"], y] / (ev - eo)
        mine = pl.ds(pl.multiple_of(256 * col, 128), 384)
        theirs = pl.ds(pl.multiple_of(256 - 256 * col, 128), 384)
        m["kg"][rmine + (p, col)] = m["own"][p, :, mine]
        m["win"][p] = m["own"][p, :, theirs]
        window = remote(m["win"].at[p], m["kg"].at[rmine + (p, col)], across)
        window.start()
        launch(7 + p, gather_piece(p))
        yield
        window.wait()
        copies = ring_gather(m["kg"], rmine + (p,), "z")
        yield
        wait_all(copies)
        block = m["kg"].at[:, :, core, p]
        copy = remote(block, block, place.partner["cc"])
        copy.start()
        yield
        copy.wait()

    def gather_piece(p):
        pack_into(m["kc"].at[xmine + (p,)], m["own"][p])
        yield from steps(start_all([
            gather_stream(place, m["kc"], XY, XY_ORDERS[p][::-1], (p,), sems)]), 4)

    def h_task():
        yield
        load_h.wait()
        hi, lo = split(m["hc"][...])
        m["hch"][...] = hi
        m["hcl"][...] = lo
        for r in range(8):
            chi = m["ct"][r % 2, :, 0, r // 2].reshape(128, 768)
            clo = m["ct"][r % 2, :, 1, r // 2].reshape(128, 768)
            m["hw"][row_bits(r)] = (
                nn(chi, m["hch"][...]) + nn(clo, m["hch"][...]) + nn(chi, m["hcl"][...]))
            if r == 3:
                yield
        yield from steps(start_all([
            scatter_stream(place, m["hw"], ROW, ROW_ORDERS[s], (pl.ds(64 * s, 64),),
                           [m[("hrec", s), t] for t in range(3)], sems) for s in range(2)]), 3)

    def c_rows():
        source = row_bits(place.aux)
        yield

        @pl.when(place.aux == place.row)
        def _():
            m["cg"][...] = m["c"][pl.ds(pl.multiple_of(384 * col, 384), 384)]

        differs = {d: (place.bit[d] - source[ROW.index(d)]) * (place.bit[d] - source[ROW.index(d)])
                   for d in ROW}
        for k in range(3):
            copies = []
            for s in range(2):
                order = Z_ORDERS[s] + ("cc",)
                later = sum((differs[d] for d in order[k + 1:]), 0)
                half = m["cg"].at[pl.ds(192 * s, 192)]
                copy = remote(half, half, place.partner[order[k]])
                sends = later + differs[order[k]] == 0
                takes = later + (1 - differs[order[k]]) == 0
                copies.append((copy, sends, takes))

                @pl.when(sends)
                def _():
                    copy.start()

            yield
            for copy, sends, takes in copies:
                @pl.when(sends)
                def _():
                    copy.wait_send()

                @pl.when(takes)
                def _():
                    copy.wait_recv()

    def cv_task():
        m["ev"][0] = jnp.zeros((8, 640), F32)
        value = jnp.broadcast_to(ev_in[...], (8, 320))

        @pl.when(col == 0)
        def _():
            m["ev"][0, :, :320] = value

        @pl.when(col == 1)
        def _():
            m["ev"][0, :, 320:] = value

        ev_copy.start()
        m["eo"][...] = jnp.broadcast_to(eo_in[...], (8, 128)).T
        for k in range(20):
            if k % 4 == 0:
                yield
            load_cv(k).wait()
            hi, lo = split(m["cv"][k % 2])
            m["cvh"][:, pl.ds(256 * k, 256)] = hi
            m["cvl"][:, pl.ds(256 * k, 256)] = lo
            if k + 2 < 20:
                load_cv(k + 2).start()
        ev_copy.wait()

    def w_task():
        w = 0.0
        for aux in range(8):
            if aux % 2 == 0:
                yield
            rows = []
            for p in range(PIECES):
                for c in range(2):
                    parts = unpack_from(m["kc"][xy_bits(aux, c) + (p,)], 2)
                    rows.append(jnp.concatenate([v.reshape(Q, 128) for v in parts], axis=1))
            kh, kl = split(jnp.concatenate(rows, axis=0))
            ch, cl = m["cvh"][:, pl.ds(640 * aux, 640)], m["cvl"][:, pl.ds(640 * aux, 640)]
            both = nt(ch, jnp.concatenate([kh, kl], axis=0))
            w = w + both[:, :128] + both[:, 128:] + nt(cl, kh)
        m["wfull"][rmine] = w
        yield from steps(start_all([
            gather_stream(place, m["wfull"], ROW, Z_ORDERS[s] + ("cc",),
                          (pl.ds(192 * s, 192),), sems) for s in range(2)]), 3)

    def place_blocks(r):
        column = m["gfull"][:, :, r // 2, r % 2].reshape(640, 128)
        for k in range(5):
            block = column[128 * k: 128 * k + 128]
            i = (r + k) % 8
            hi, lo = split(block)
            m["ghi"][pl.ds(128 * i, 128), pl.ds(128 * r, 128)] = hi
            m["glo"][pl.ds(128 * i, 128), pl.ds(128 * r, 128)] = lo
            if 0 < k < 4:
                hi, lo = split(block.T)
                m["ghi"][pl.ds(128 * r, 128), pl.ds(128 * i, 128)] = hi
                m["glo"][pl.ds(128 * r, 128), pl.ds(128 * i, 128)] = lo
        return column[:128]

    def g_task():
        lanes = lax.broadcasted_iota(jnp.int32, (128, 384), 1)
        rhs = m["kg"][rmine].reshape(128, 384)
        rh, rl = split(jnp.where(lanes >= 128 * col, rhs, 0.0))
        accs = []
        for k in range(5):
            lh, ll = split(m["kg"][row_bits((place.row + k) % 8)].reshape(128, 384))
            accs.append(nt(lh, rh) + nt(lh, rl) + nt(ll, rh))
        acc = jnp.concatenate(accs, axis=0)
        m["gs"][...] = acc.reshape(2, 4, 80, 128)
        firsts, seconds = ("x", "y"), ("y", "x")
        copies = []
        for s, axis in enumerate(firsts):
            for d in (1, 2, 3):
                copies.append(remote(m["gs"].at[s, (at[axis] + d) % 4], m["gs1"].at[s, d - 1],
                                     ring[axis, d]))
                copies[-1].start()
        yield
        wait_all(copies)
        copies = []
        for s, axis in enumerate(firsts):
            mine = (s, at[axis])
            m["gs"][mine] = ((m["gs"][mine] + m["gs1"][s, 0])
                             + (m["gs1"][s, 1] + m["gs1"][s, 2]))
            for d in (1, 2, 3):
                copies.append(remote(m["gs"].at[mine], m["gs2"].at[s, d - 1],
                                     ring[seconds[s], d]))
                copies[-1].start()
        yield
        wait_all(copies)
        copies = []
        for s, axis in enumerate(firsts):
            total = ((m["gs"][s, at[axis]] + m["gs2"][s, 0])
                     + (m["gs2"][s, 1] + m["gs2"][s, 2]))
            m["gfull"][s, at[axis], z, core] = total
            copies += ring_gather(m["gfull"], (s, at[axis], z, core), "z")
        yield
        wait_all(copies)
        copies = []
        for s, axis in enumerate(firsts):
            copies += ring_gather(m["gfull"], (s, at[axis], slice(None), core), axis)
        yield
        wait_all(copies)
        block = m["gfull"].at[:, :, :, core]
        copy = remote(block, block, place.partner["cc"])
        copy.start()
        yield
        copy.wait()

    for p in range(PIECES):
        launch(p, piece(p))
    launch(4, h_task())
    launch(5, c_rows())
    launch(6, cv_task())

    def follow():
        if 12 not in tasks and 12 not in finished and finished.issuperset(range(PIECES)):
            launch(12, g_task())
        if 11 not in tasks and 11 not in finished and finished.issuperset(range(7, 7 + PIECES)):
            launch(11, w_task())

    for n in SCHEDULE:
        advance(n)
        follow()
    while tasks:
        for n in sorted(tasks):
            advance(n)
        follow()

    ghi, glo, t, acc_ref = m["ghi"], m["glo"], m["t"], m["acc"]
    r128 = lax.broadcasted_iota(jnp.int32, (128, 128), 0)
    l128 = lax.broadcasted_iota(jnp.int32, (128, 128), 1)
    total = jnp.zeros((128, 128), F32)
    for r in range(8):
        total = total + jnp.where(r128 == l128, place_blocks(r), 0.0)
    meansq = jnp.sum(total, axis=(0, 1), keepdims=True) / entries
    s1 = ROTATION_SCALE / jnp.sqrt(meansq + 1e-06)
    s2 = s1 * s1
    here = pl.ds(pl.multiple_of(128 * place.row, 128), 128)
    t[0, :, :128] = ghi[:, here]
    t[0, :, 128:] = glo[:, here]
    rows8 = lax.broadcasted_iota(jnp.int32, (1024, 128), 0)
    lanes8 = lax.broadcasted_iota(jnp.int32, (1024, 128), 1)
    g1 = (ghi[:, here].astype(F32) + glo[:, here].astype(F32)) * s2
    eye = jnp.where(rows8 == lanes8 + 128 * place.row, 1.0, 0.0)
    acc_ref[0] = eye - g1 * 0.5
    acc_ref[1] = eye - g1 * (1.0 / 6.0)
    coeff = [(1.0 / 24.0, 1.0 / 120.0), (-1.0 / 720.0, -1.0 / 5040.0), (1.0 / 40320.0, 0.0)]
    for k, (ce, cs) in enumerate(coeff):
        now, later = k % 2, (k + 1) % 2
        scale = s2 * s2 if k == 0 else s2

        @pl.loop(0, 4)
        def _(i):
            rs = pl.ds(pl.multiple_of(i * 256, 256), 256)
            high = nn(ghi[rs], t[now])
            power = (high[:, :128] + high[:, 128:] + nn(glo[rs], t[now, :, :128])) * scale
            if k < 2:
                hi, lo = split(power)
                t[later, rs, :128] = hi
                t[later, rs, 128:] = lo
                acc_ref[1, rs] = acc_ref[1, rs] + power * cs
            acc_ref[0, rs] = acc_ref[0, rs] + power * ce

    e_hi, e_lo = split(acc_ref[0])
    c_hi, c_lo = split(m["cg"][...])
    both = nn(c_hi, jnp.concatenate([e_hi, e_lo], axis=1))
    result = both[:, :128] + both[:, 128:] + nn(c_lo, e_hi)
    s_hi, s_lo = split(acc_ref[1] * s1)
    w_all = jnp.concatenate([m["wfull"][row_bits(r)] for r in range(8)], axis=1)
    w_hi, w_lo = split(w_all)
    both = nn(w_hi, jnp.concatenate([s_hi, s_lo], axis=1))
    out[...] = result + both[:, :128] + both[:, 128:] + nn(w_lo, s_hi)


def on_device(b_tensor, hcore, c_occ, c_virt, eps_occ, eps_virt):
    entries = float(c_virt.shape[1] * c_occ.shape[1])
    bag = scratch()
    return call(functools.partial(kernel, bag, entries), jax.ShapeDtypeStruct((384, 128), F32),
                [ANY, ANY, ANY, ANY, VM, VM], bag.shapes, 0,
                b_tensor, hcore, c_occ, c_virt, eps_virt[None, :], eps_occ[None, :])


def solution(mesh):
    placed = (
        P("aux", "row", "col"),
        P("row", ("aux", "col")),
        P("row", None),
        P(("aux", "col"), None),
        P("row"),
        P(("aux", "col")),
    )
    return jax.shard_map(
        on_device, mesh=mesh, in_specs=placed, out_specs=P(("aux", "col"), "row"), check_vma=False
    )
```

```python
import functools

import jax
import jax.numpy as jnp
from jax import lax
from jax.experimental import pallas as pl
from jax.experimental.pallas import tpu as pltpu
from jax.sharding import PartitionSpec as P

ROTATION_SCALE = 0.03
MESH = pl.DeviceIdType.MESH
F32 = jnp.float32
BF16 = jnp.bfloat16
XY = ("xa", "xb", "ya", "yb")
ROW = ("za", "zb", "cc")
VMEM_LIMIT = 62 * 1024 * 1024


class Place:
    def __init__(self):
        aux, row, col = (lax.axis_index(n) for n in ("aux", "row", "col"))
        y, xl = aux // 2, aux % 2
        z, core = row // 2, row % 2
        self.aux, self.row, self.col = aux, row, col
        self.bit = {
            "xa": (xl + col) % 2, "xb": col,
            "ya": (y + y // 2) % 2, "yb": y // 2,
            "za": (z + z // 2) % 2, "zb": z // 2,
            "cc": core,
        }
        self.partner = {
            "xa": (aux + 1 - 2 * xl, row, col),
            "xb": (aux + 1 - 2 * xl, row, 1 - col),
            "ya": (aux + 2 - 4 * (y % 2), row, col),
            "yb": (2 * (3 - y) + xl, row, col),
            "za": (aux, row + 2 - 4 * (z % 2), col),
            "zb": (aux, 2 * (3 - z) + core, col),
            "cc": (aux, row + 1 - 2 * core, col),
        }

    def greet(self, dims, swap=False):
        barrier = pltpu.get_barrier_semaphore()
        for d in dims:
            pl.semaphore_signal(barrier, inc=1, device_id=self.partner[d], device_id_type=MESH)
        if not swap:
            pl.semaphore_wait(barrier, len(dims))
            return

        @pl.when(self.aux != self.row)
        def _():
            pl.semaphore_signal(
                barrier, inc=1, device_id=(self.row, self.aux, self.col), device_id_type=MESH
            )
            pl.semaphore_wait(barrier, len(dims) + 1)

        @pl.when(self.aux == self.row)
        def _():
            pl.semaphore_wait(barrier, len(dims))


def xy_bits(aux, col):
    y, xl = aux // 2, aux % 2
    return ((xl + col) % 2, col, (y + y // 2) % 2, y // 2)


def row_bits(row):
    z, core = row // 2, row % 2
    return ((z + z // 2) % 2, z // 2, core)


class Sems:
    def __init__(self, send, recv):
        self.send, self.recv, self.n = send, recv, 0

    def take(self):
        n = self.n
        self.n += 1
        assert self.n <= self.send.shape[0]
        return self.send.at[n], self.recv.at[n]


def scatter_stream(place, work, axes, order, tail, recvs, sems):
    done = []
    for step, d in enumerate(order):
        def index(bit_of_d):
            return tuple(
                place.bit[a] if a in done else (bit_of_d if a == d else slice(None)) for a in axes
            ) + tail
        mine, theirs = index(place.bit[d]), index(1 - place.bit[d])
        s, r = sems.take()
        copy = pltpu.make_async_remote_copy(
            src_ref=work.at[theirs], dst_ref=recvs[step], send_sem=s, recv_sem=r,
            device_id=place.partner[d], device_id_type=MESH,
        )
        copy.start()
        yield
        copy.wait()
        work[mine] = work[mine] + recvs[step][...]
        done.append(d)


def gather_stream(place, full, axes, order, tail, sems):
    done = []
    for d in order:
        sl = tuple(slice(None) if a in done else place.bit[a] for a in axes) + tail
        s, r = sems.take()
        copy = pltpu.make_async_remote_copy(
            src_ref=full.at[sl], dst_ref=full.at[sl], send_sem=s, recv_sem=r,
            device_id=place.partner[d], device_id_type=MESH,
        )
        copy.start()
        yield
        copy.wait()
        done.append(d)


def drive(streams):
    streams = list(streams)
    while streams:
        alive = []
        for g in streams:
            try:
                next(g)
                alive.append(g)
            except StopIteration:
                pass
        streams = alive


def rotate(dims, k):
    return tuple(dims[k:]) + tuple(dims[:k])


XY_ORDERS = [("xa", "ya", "xb", "yb"), ("xb", "yb", "xa", "ya"),
             ("ya", "xa", "yb", "xb"), ("yb", "xb", "ya", "xa")]
ROW_ORDERS = [("cc", "za", "zb"), ("cc", "zb", "za")]


def recv_shapes(n, block):
    return [pltpu.VMEM((2,) * (n - 1 - t) + block, F32) for t in range(n)]


def dma(n):
    return pltpu.SemaphoreType.DMA((n,))


ANY = pl.BlockSpec(memory_space=pl.ANY)
VM = pl.BlockSpec(memory_space=pltpu.VMEM)


def call(kernel, outs, in_specs, scratch, cid, *args):
    return pl.pallas_call(
        kernel,
        out_shape=outs,
        in_specs=in_specs,
        out_specs=jax.tree.map(lambda _: VM, outs),
        scratch_shapes=scratch,
        compiler_params=pltpu.CompilerParams(
            collective_id=cid, has_side_effects=True, vmem_limit_bytes=VMEM_LIMIT
        ),
    )(*args)


def split(x):
    hi = x.astype(BF16)
    return hi, (x - hi.astype(F32)).astype(BF16)


def start_all(streams):
    for g in streams:
        next(g)
    return streams


def nt(a, b):
    return lax.dot_general(a, b, (((1,), (1,)), ((), ())), preferred_element_type=F32)


def nn(a, b):
    return jnp.dot(a, b, preferred_element_type=F32)


class Bag:
    def __init__(self):
        self.names, self.shapes = [], []

    def add(self, name, shape):
        self.names.append(name)
        self.shapes.append(shape)

    def recvs(self, name, n, block):
        for t, s in enumerate(recv_shapes(n, block)):
            self.add((name, t), s)

    def bind(self, refs):
        return dict(zip(self.names, refs))


LIMIT = 16383.0


def pack(parts):
    peak = jnp.max(jnp.abs(parts[0]), axis=0)
    for v in parts[1:]:
        peak = jnp.maximum(peak, jnp.max(jnp.abs(v), axis=0))
    peak = jnp.maximum(peak, 1e-30)
    n = [jnp.round(v * (LIMIT / peak)) for v in parts]
    words = []
    if len(n) >= 5:
        h3, h4 = jnp.floor(n[3] * (1 / 32)), jnp.floor(n[4] * (1 / 32))
        words += [n[0] * 1024 + h3, n[1] * 1024 + h4,
                  n[2] * 1024 + ((n[3] - 32 * h3) * 32 + (n[4] - 32 * h4) - 512)]
        n = n[5:]
    if n:
        h = jnp.floor(n[2] * (1 / 128))
        words += [n[0] * 256 + h, n[1] * 256 + (n[2] - 128 * h)]
    return peak * (1 / LIMIT), words


def unpack(scale, words):
    n = []
    if len(words) >= 3:
        n = [jnp.floor((w + 512) * (1 / 1024)) for w in words[:3]]
        h3, h4, rest = (w - 1024 * t for w, t in zip(words, n))
        rest = rest + 512
        l3 = jnp.floor(rest * (1 / 32))
        n += [h3 * 32 + l3, h4 * 32 + (rest - 32 * l3)]
        words = words[3:]
    if words:
        n5 = jnp.floor((words[0] + 128) * (1 / 256))
        n6 = jnp.floor(words[1] * (1 / 256))
        n += [n5, n6, (words[0] - 256 * n5) * 128 + (words[1] - 256 * n6)]
    return [v * scale for v in n]


def pack_into(ref, block):
    k = block.shape[-1] // 128
    block = block.reshape(-1, 8, block.shape[-1])
    m = block.shape[0]
    scale, words = pack([block[..., 128 * i: 128 * i + 128] for i in range(k)])
    ref[0] = scale
    for j, w in enumerate(words):
        ref[1 + j * m: 1 + (j + 1) * m] = w


def unpack_from(wire, m):
    words = [wire[1 + j * m: 1 + (j + 1) * m] for j in range((wire.shape[0] - 1) // m)]
    return unpack(wire[0], words)


PIECES = 4
R = 128 // PIECES
Q = R // 2
Z_ORDERS = (("za", "zb"), ("zb", "za"))
SCHEDULE = [
    0, 2, 1, 0, 3, 2, 1, 0, 3, 2, 4, 0, 1, 3, 4, 2, 0, 1, 3, 4, 2, 6, 1, 0,
    3, 4, 5, 6, 6, 6, 6, 2, 1, 0, 4, 3, 2, 0, 1, 3, 5, 2, 1, 0, 3, 2, 1, 5,
    0, 3, 5, 2, 0, 1, 3, 2, 1, 0, 0, 3, 7, 9, 8, 10, 2, 2, 1, 7, 9, 8, 10, 1,
    3, 3, 9, 7, 8, 10, 12, 7, 9, 8, 10, 11, 11, 11, 12, 11, 12, 11, 11, 12, 11, 12,
]


def scratch():
    bag, vm = Bag(), pltpu.VMEM
    bag.add("b", vm((2, 2, 768, 512), BF16))
    bag.add("c", vm((768, 1024), F32))
    bag.add("cg", vm((384, 1024), F32))
    bag.add("hc", vm((768, 384), F32))
    bag.add("ct", vm((2, PIECES, 2, 4, R, 768), BF16))
    bag.add("hch", vm((768, 384), BF16))
    bag.add("hcl", vm((768, 384), BF16))
    bag.add("cv", vm((2, 384, 256), F32))
    bag.add("cvh", vm((384, 5120), BF16))
    bag.add("cvl", vm((384, 5120), BF16))
    bag.add("ev", vm((2, 8, 640), F32))
    bag.add("eo", vm((128, 8), F32))
    for p in range(PIECES):
        bag.add(("xs", p), vm((4, R, 1024), F32))
        bag.add(("xr", p), vm((4, R, 1024), F32))
        bag.add(("xw", p), vm((2, 2, R, 1024), F32))
        bag.add(("xf", p), vm((2, 2, R, 1024), F32))
        bag.add(("yw", p), vm((4, 4, R, 384), F32))
        bag.add(("yb", p), vm((R, 384), F32))
        bag.add(("gw", p), vm((4, 4, Q, 640), F32))
        for s in range(2):
            for t, tiles in enumerate((4, 2)):
                bag.add(("xout", p, s, t), vm((5 * tiles + 1, 8, 128), F32))
                bag.add(("xin", p, s, t), vm((5 * tiles + 1, 8, 128), F32))
            bag.add(("xg", p, s), vm((2, 2, 11, 8, 128), F32))
        for s in range(2):
            for name, rows, lanes, words in (("y", R // 2, 384, 2), ("g", Q // 2, 640, 3)):
                packed = (3, words * rows // 2 + 1, 8, 128)
                bag.add((name + "out", p, s), vm(packed, F32))
                bag.add((name + "in", p, s), vm(packed, F32))
                bag.add((name + "raw", p, s), vm((3, rows, lanes), F32))
    for s in range(2):
        bag.recvs(("hrec", s), 3, (64, 384))
    bag.add("hw", vm((2, 2, 2, 128, 384), F32))
    bag.add("kc", vm((2, 2, 2, 2, PIECES, 7, 8, 128), F32))
    bag.add("own", vm((PIECES, Q, 640), F32))
    bag.add("kg", vm((2, 2, 2, PIECES, 2, Q, 384), F32))
    bag.add("win", vm((PIECES, Q, 384), F32))
    bag.add("gs", vm((2, 4, 80, 128), F32))
    bag.add("gs1", vm((2, 3, 80, 128), F32))
    bag.add("gs2", vm((2, 3, 80, 128), F32))
    bag.add("gfull", vm((2, 4, 4, 2, 7, 8, 128), F32))
    bag.add("wfull", vm((2, 2, 2, 384, 128), F32))
    bag.add("ghi", vm((1024, 1024), BF16))
    bag.add("glo", vm((1024, 1024), BF16))
    bag.add("t", vm((2, 1024, 256), BF16))
    bag.add("acc", vm((2, 1024, 128), F32))
    bag.add("local", dma(12))
    bag.add("send", dma(320))
    bag.add("recv", dma(320))
    return bag


def kernel(bag, entries, b_in, h_in, c_in, cv_in, ev_in, eo_in, out, *refs):
    m = bag.bind(refs)
    place = Place()
    sems = Sems(m["send"], m["recv"])
    core, col = place.row % 2, place.col
    other = 1 - core
    y, z = place.aux // 2, place.row // 2
    across = (place.aux, place.row, 1 - col)
    swapped = (2 * z + place.aux % 2, 2 * y + core, col)
    xmine = tuple(place.bit[d] for d in XY)
    rmine = tuple(place.bit[d] for d in ROW)
    zmine = rmine[:2]
    at = {"x": 2 * col + place.aux % 2, "y": y, "z": z}
    ring = {}
    for d in (1, 2, 3):
        xd, yd, zd = ((at[a] + d) % 4 for a in "xyz")
        ring["x", d] = (2 * y + xd % 2, place.row, xd // 2)
        ring["y", d] = (2 * yd + place.aux % 2, place.row, col)
        ring["z", d] = (place.aux, 2 * zd + core, col)

    def remote(src, dst, device):
        s, r = sems.take()
        return pltpu.make_async_remote_copy(
            src_ref=src, dst_ref=dst, send_sem=s, recv_sem=r,
            device_id=device, device_id_type=MESH)

    def load_c(k, zz):
        sl = pl.ds(pl.multiple_of(128 * (2 * zz + k), 128), 128)
        which = zz if k is core else 4 + zz
        return pltpu.make_async_copy(c_in.at[:, sl], m["c"].at[:, sl], m["local"].at[which])

    load_b = pltpu.make_async_copy(b_in, m["b"].at[0], m["local"].at[8])
    load_h = pltpu.make_async_copy(h_in, m["hc"], m["local"].at[9])

    def load_cv(k):
        return pltpu.make_async_copy(
            cv_in.at[:, pl.ds(256 * k, 256)], m["cv"].at[k % 2], m["local"].at[10 + k % 2])

    for zz in range(4):
        load_c(other, zz).start()
    load_b.start()
    for zz in range(4):
        load_c(core, zz).start()
    barrier = pltpu.get_barrier_semaphore()
    dims = XY + ROW
    greeted = [place.partner[d] for d in dims] + [across, ring["y", 2], ring["z", 2]]
    for device in greeted:
        pl.semaphore_signal(barrier, inc=1, device_id=device, device_id_type=MESH)

    @pl.when(y != z)
    def _():
        pl.semaphore_signal(barrier, inc=1, device_id=swapped, device_id_type=MESH)

    def turn_c(k, zz):
        load_c(k, zz).wait()
        sl = pl.ds(pl.multiple_of(128 * (2 * zz + k), 128), 128)
        hi, lo = split(m["c"][:, sl].T)
        m["ct"][k, :, 0, zz] = hi.reshape(PIECES, R, 768)
        m["ct"][k, :, 1, zz] = lo.reshape(PIECES, R, 768)

    def x_part(p, k, out_ref):
        both = m["ct"][k, p].reshape(8 * R, 768)
        for q in range(2):
            acc = nn(both, m["b"][0, q])
            out_ref[..., pl.ds(512 * q, 512)] = (acc[:4 * R] + acc[4 * R:]).reshape(
                out_ref.shape[:-1] + (512,))

    for zz in range(4):
        turn_c(other, zz)
    load_b.wait()
    x_part(0, other, m["xs", 0])

    @pl.when(y != z)
    def _():
        pl.semaphore_wait(barrier, len(greeted) + 1)

    @pl.when(y == z)
    def _():
        pl.semaphore_wait(barrier, len(greeted))

    xc = [remote(m["xs", p], m["xr", p], place.partner["cc"]) for p in range(PIECES)]
    xc[0].start()
    load_h.start()
    load_cv(0).start()
    load_cv(1).start()
    for zz in range(4):
        turn_c(core, zz)
    b_copy = remote(m["b"].at[0], m["b"].at[1], place.partner["cc"])
    ev_copy = remote(m["ev"].at[0], m["ev"].at[1], across)
    for p in range(PIECES):
        x_part(p, core, m["xw", p])
        if p + 1 < PIECES:
            x_part(p + 1, other, m["xs", p + 1])
            xc[p + 1].start()
    b_copy.start()

    tasks, finished, have_b = {}, set(), []

    def advance(n):
        if n in tasks:
            try:
                next(tasks[n])
            except StopIteration:
                del tasks[n]
                finished.add(n)

    def complete(n):
        while n in tasks:
            advance(n)

    def launch(n, g):
        tasks[n] = g
        advance(n)

    def steps(streams, n):
        for _ in range(n - 1):
            yield
            for g in streams:
                next(g)
        yield
        drive(streams)

    def x_scatter(p, s):
        work, rows, done = m["xw", p], pl.ds(16 * s, 16), []
        for t, d in enumerate(Z_ORDERS[s]):
            def index(bit):
                return tuple(place.bit[a] if a in done else (bit if a == d else slice(None))
                             for a in ("za", "zb")) + (rows,)
            mine, theirs = index(place.bit[d]), index(1 - place.bit[d])
            pack_into(m["xout", p, s, t], work[theirs])
            copy = remote(m["xout", p, s, t], m["xin", p, s, t], place.partner[d])
            copy.start()
            yield
            copy.wait()
            for k, v in enumerate(unpack_from(m["xin", p, s, t][...], (4, 2)[t])):
                spot = mine + (pl.ds(128 * k, 128),)
                work[spot] = work[spot] + v.reshape((2, 16, 128) if t == 0 else (16, 128))
            done.append(d)

    def two_rings(work, s, rows, out, wire, raw):
        first, second = ("x", "y") if s == 0 else ("y", "x")
        lanes = work.shape[-1]
        tiles = (rows.size * 4) // 8

        def index(i, j):
            return ((i, j) if s == 0 else (j, i)) + (rows,)

        copies = []
        for d in (1, 2, 3):
            pack_into(out.at[d - 1], work[index((at[first] + d) % 4, slice(None))])
            copies.append(remote(out.at[d - 1], wire.at[d - 1], ring[first, d]))
            copies[-1].start()
        yield
        mine = index(at[first], slice(None))
        for c in copies:
            c.wait()
        got = [unpack_from(wire[d], tiles) for d in range(3)]
        for k in range(lanes // 128):
            place_k = mine + (pl.ds(128 * k, 128),)
            v = (got[0][k] + got[1][k]) + got[2][k]
            work[place_k] = work[place_k] + v.reshape(4, rows.size, 128)
        copies = []
        for d in (1, 2, 3):
            copies.append(remote(work.at[index(at[first], (at[second] + d) % 4)],
                                 raw.at[d - 1], ring[second, d]))
            copies[-1].start()
        yield
        for c in copies:
            c.wait()
        mine = index(at[first], at[second])
        work[mine] = (work[mine] + raw[0]) + (raw[1] + raw[2])

    def ring_gather(full, index, axis):
        copies = [remote(full.at[index], full.at[index], ring[axis, d]) for d in (1, 2, 3)]
        for c in copies:
            c.start()
        return copies

    def wait_all(copies):
        for c in copies:
            c.wait()

    def piece(p):
        yield
        xc[p].wait()
        m["xw", p][...] = m["xw", p][...] + m["xr", p][...].reshape(2, 2, R, 1024)
        streams = start_all([x_scatter(p, s) for s in range(2)])
        yield from steps(streams, 2)
        for s in range(2):
            pack_into(m["xg", p, s].at[zmine], m["xw", p][zmine + (pl.ds(16 * s, 16),)])
        streams = start_all([
            gather_stream(place, m["xg", p, s], ("za", "zb"), Z_ORDERS[s][::-1], (), sems)
            for s in range(2)])
        yield from steps(streams, 2)
        for s in range(2):
            for i in range(4):
                for k, v in enumerate(unpack_from(m["xg", p, s][i // 2, i % 2], 2)):
                    m["xf", p][i // 2, i % 2, pl.ds(16 * s, 16), pl.ds(128 * k, 128)] = (
                        v.reshape(16, 128))
        if not have_b:
            b_copy.wait()
            have_b.append(p)
        hi, lo = split(m["xf", p][...].reshape(4 * R, 1024))
        both = jnp.concatenate([hi, lo], axis=0)
        for side in range(2):
            xlo = core if side == 0 else other
            for half in range(2):
                rows = pl.ds(384 * half, 384)
                acc = nt(both[:, :512], m["b"][side, 0, rows])
                acc += nt(both[:, 512:], m["b"][side, 1, rows])
                acc = acc[:4 * R] + acc[4 * R:]
                for zz in range(4):
                    m["yw", p][2 * half + xlo, zz] = acc[R * zz: R * zz + R]
        streams = start_all([
            two_rings(m["yw", p], s, pl.ds(R // 2 * s, R // 2),
                      m["yout", p, s], m["yin", p, s], m["yraw", p, s]) for s in range(2)])
        yield from steps(streams, 2)
        swap = remote(m["yw", p].at[at["x"], y], m["yb", p], swapped)

        @pl.when(y != z)
        def _():
            swap.start()

        @pl.when(y == z)
        def _():
            m["yb", p][...] = m["yw", p][at["x"], y]

        yield
        complete(4)
        complete(6)

        @pl.when(y != z)
        def _():
            swap.wait()

        image = m["hw"][rmine + (pl.ds(R * p, R),)] - m["yb", p][...]
        hi, lo = split(image)
        both = jnp.concatenate([hi, lo], axis=0)
        for aux in range(8):
            sl = pl.ds(640 * aux, 640)
            acc = nn(both, m["cvh"][:, sl])
            acc = acc[:R] + acc[R:] + nn(hi, m["cvl"][:, sl])
            for c in range(2):
                m["gw", p][2 * c + aux % 2, aux // 2] = acc[Q * c: Q * c + Q]
        streams = start_all([
            two_rings(m["gw", p], s, pl.ds(Q // 2 * s, Q // 2),
                      m["gout", p, s], m["gin", p, s], m["graw", p, s]) for s in range(2)])
        yield from steps(streams, 2)
        ev = m["ev"][0, 0:1] + m["ev"][1, 0:1]
        eo = m["eo"][pl.ds(R * p + Q * col, Q), 0:1]
        m["own"][p] = m["gw", p][at["x"], y] / (ev - eo)
        mine = pl.ds(pl.multiple_of(256 * col, 128), 384)
        theirs = pl.ds(pl.multiple_of(256 - 256 * col, 128), 384)
        m["kg"][rmine + (p, col)] = m["own"][p, :, mine]
        m["win"][p] = m["own"][p, :, theirs]
        window = remote(m["win"].at[p], m["kg"].at[rmine + (p, col)], across)
        window.start()
        launch(7 + p, gather_piece(p))
        yield
        window.wait()
        copies = ring_gather(m["kg"], rmine + (p,), "z")
        yield
        wait_all(copies)
        block = m["kg"].at[:, :, core, p]
        copy = remote(block, block, place.partner["cc"])
        copy.start()
        yield
        copy.wait()

    def gather_piece(p):
        pack_into(m["kc"].at[xmine + (p,)], m["own"][p])
        yield from steps(start_all([
            gather_stream(place, m["kc"], XY, XY_ORDERS[p][::-1], (p,), sems)]), 4)

    def h_task():
        yield
        load_h.wait()
        hi, lo = split(m["hc"][...])
        m["hch"][...] = hi
        m["hcl"][...] = lo
        for r in range(8):
            chi = m["ct"][r % 2, :, 0, r // 2].reshape(128, 768)
            clo = m["ct"][r % 2, :, 1, r // 2].reshape(128, 768)
            m["hw"][row_bits(r)] = (
                nn(chi, m["hch"][...]) + nn(clo, m["hch"][...]) + nn(chi, m["hcl"][...]))
            if r == 3:
                yield
        yield from steps(start_all([
            scatter_stream(place, m["hw"], ROW, ROW_ORDERS[s], (pl.ds(64 * s, 64),),
                           [m[("hrec", s), t] for t in range(3)], sems) for s in range(2)]), 3)

    def c_rows():
        source = row_bits(place.aux)
        yield

        @pl.when(place.aux == place.row)
        def _():
            m["cg"][...] = m["c"][pl.ds(pl.multiple_of(384 * col, 384), 384)]

        differs = {d: (place.bit[d] - source[ROW.index(d)]) * (place.bit[d] - source[ROW.index(d)])
                   for d in ROW}
        for k in range(3):
            copies = []
            for s in range(2):
                order = Z_ORDERS[s] + ("cc",)
                later = sum((differs[d] for d in order[k + 1:]), 0)
                half = m["cg"].at[pl.ds(192 * s, 192)]
                copy = remote(half, half, place.partner[order[k]])
                sends = later + differs[order[k]] == 0
                takes = later + (1 - differs[order[k]]) == 0
                copies.append((copy, sends, takes))

                @pl.when(sends)
                def _():
                    copy.start()

            yield
            for copy, sends, takes in copies:
                @pl.when(sends)
                def _():
                    copy.wait_send()

                @pl.when(takes)
                def _():
                    copy.wait_recv()

    def cv_task():
        m["ev"][0] = jnp.zeros((8, 640), F32)
        value = jnp.broadcast_to(ev_in[...][None, :], (8, 320))

        @pl.when(col == 0)
        def _():
            m["ev"][0, :, :320] = value

        @pl.when(col == 1)
        def _():
            m["ev"][0, :, 320:] = value

        ev_copy.start()
        m["eo"][...] = jnp.broadcast_to(eo_in[...], (8, 128)).T
        for k in range(20):
            if k % 4 == 0:
                yield
            load_cv(k).wait()
            hi, lo = split(m["cv"][k % 2])
            m["cvh"][:, pl.ds(256 * k, 256)] = hi
            m["cvl"][:, pl.ds(256 * k, 256)] = lo
            if k + 2 < 20:
                load_cv(k + 2).start()
        ev_copy.wait()

    def w_task():
        w = 0.0
        for aux in range(8):
            if aux % 2 == 0:
                yield
            rows = []
            for p in range(PIECES):
                for c in range(2):
                    parts = unpack_from(m["kc"][xy_bits(aux, c) + (p,)], 2)
                    rows.append(jnp.concatenate([v.reshape(Q, 128) for v in parts], axis=1))
            kh, kl = split(jnp.concatenate(rows, axis=0))
            ch, cl = m["cvh"][:, pl.ds(640 * aux, 640)], m["cvl"][:, pl.ds(640 * aux, 640)]
            both = nt(ch, jnp.concatenate([kh, kl], axis=0))
            w = w + both[:, :128] + both[:, 128:] + nt(cl, kh)
        m["wfull"][rmine] = w
        yield from steps(start_all([
            gather_stream(place, m["wfull"], ROW, Z_ORDERS[s] + ("cc",),
                          (pl.ds(192 * s, 192),), sems) for s in range(2)]), 3)

    def place_blocks(r):
        column = jnp.concatenate(
            [v.reshape(16, 128) for s in range(2) for i in range(4)
             for v in unpack_from(m["gfull"][s, i, r // 2, r % 2], 2)], axis=0)
        for k in range(5):
            block = column[128 * k: 128 * k + 128]
            i = (r + k) % 8
            hi, lo = split(block)
            m["ghi"][pl.ds(128 * i, 128), pl.ds(128 * r, 128)] = hi
            m["glo"][pl.ds(128 * i, 128), pl.ds(128 * r, 128)] = lo
            if 0 < k < 4:
                hi, lo = split(block.T)
                m["ghi"][pl.ds(128 * r, 128), pl.ds(128 * i, 128)] = hi
                m["glo"][pl.ds(128 * r, 128), pl.ds(128 * i, 128)] = lo
        return column[:128]

    def g_task():
        lanes = lax.broadcasted_iota(jnp.int32, (128, 384), 1)
        rhs = m["kg"][rmine].reshape(128, 384)
        rh, rl = split(jnp.where(lanes >= 128 * col, rhs, 0.0))
        accs = []
        for k in range(5):
            lh, ll = split(m["kg"][row_bits((place.row + k) % 8)].reshape(128, 384))
            accs.append(nt(lh, rh) + nt(lh, rl) + nt(ll, rh))
        acc = jnp.concatenate(accs, axis=0)
        m["gs"][...] = acc.reshape(2, 4, 80, 128)
        firsts, seconds = ("x", "y"), ("y", "x")
        copies = []
        for s, axis in enumerate(firsts):
            for d in (1, 2, 3):
                copies.append(remote(m["gs"].at[s, (at[axis] + d) % 4], m["gs1"].at[s, d - 1],
                                     ring[axis, d]))
                copies[-1].start()
        yield
        wait_all(copies)
        copies = []
        for s, axis in enumerate(firsts):
            mine = (s, at[axis])
            m["gs"][mine] = ((m["gs"][mine] + m["gs1"][s, 0])
                             + (m["gs1"][s, 1] + m["gs1"][s, 2]))
            for d in (1, 2, 3):
                copies.append(remote(m["gs"].at[mine], m["gs2"].at[s, d - 1],
                                     ring[seconds[s], d]))
                copies[-1].start()
        yield
        wait_all(copies)
        copies = []
        for s, axis in enumerate(firsts):
            total = ((m["gs"][s, at[axis]] + m["gs2"][s, 0])
                     + (m["gs2"][s, 1] + m["gs2"][s, 2]))
            scale, words = pack([total[16 * i: 16 * i + 16].reshape(2, 8, 128) for i in range(5)])
            mine = m["gfull"].at[s, at[axis], z, core]
            mine[0] = scale
            for i, w in enumerate(words):
                mine[1 + 2 * i: 3 + 2 * i] = w
            copies += ring_gather(m["gfull"], (s, at[axis], z, core), "z")
        yield
        wait_all(copies)
        copies = []
        for s, axis in enumerate(firsts):
            copies += ring_gather(m["gfull"], (s, at[axis], slice(None), core), axis)
        yield
        wait_all(copies)
        block = m["gfull"].at[:, :, :, core]
        copy = remote(block, block, place.partner["cc"])
        copy.start()
        yield
        copy.wait()

    for p in range(PIECES):
        launch(p, piece(p))
    launch(4, h_task())
    launch(5, c_rows())
    launch(6, cv_task())

    def follow():
        if 12 not in tasks and 12 not in finished and finished.issuperset(range(PIECES)):
            launch(12, g_task())
        if 11 not in tasks and 11 not in finished and finished.issuperset(range(7, 7 + PIECES)):
            launch(11, w_task())

    for n in SCHEDULE:
        advance(n)
        follow()
    while tasks:
        for n in sorted(tasks):
            advance(n)
        follow()

    ghi, glo, t, acc_ref = m["ghi"], m["glo"], m["t"], m["acc"]
    r128 = lax.broadcasted_iota(jnp.int32, (128, 128), 0)
    l128 = lax.broadcasted_iota(jnp.int32, (128, 128), 1)
    total = jnp.zeros((128, 128), F32)
    for r in range(8):
        total = total + jnp.where(r128 == l128, place_blocks(r), 0.0)
    meansq = jnp.sum(total, axis=(0, 1), keepdims=True) / entries
    s1 = ROTATION_SCALE / jnp.sqrt(meansq + 1e-06)
    s2 = s1 * s1
    here = pl.ds(pl.multiple_of(128 * place.row, 128), 128)
    t[0, :, :128] = ghi[:, here]
    t[0, :, 128:] = glo[:, here]
    rows8 = lax.broadcasted_iota(jnp.int32, (1024, 128), 0)
    lanes8 = lax.broadcasted_iota(jnp.int32, (1024, 128), 1)
    g1 = (ghi[:, here].astype(F32) + glo[:, here].astype(F32)) * s2
    eye = jnp.where(rows8 == lanes8 + 128 * place.row, 1.0, 0.0)
    acc_ref[0] = eye - g1 * 0.5
    acc_ref[1] = eye - g1 * (1.0 / 6.0)
    coeff = [(1.0 / 24.0, 1.0 / 120.0), (-1.0 / 720.0, -1.0 / 5040.0), (1.0 / 40320.0, 0.0)]
    for k, (ce, cs) in enumerate(coeff):
        now, later = k % 2, (k + 1) % 2
        scale = s2 * s2 if k == 0 else s2

        @pl.loop(0, 4)
        def _(i):
            rs = pl.ds(pl.multiple_of(i * 256, 256), 256)
            high = nn(ghi[rs], t[now])
            power = (high[:, :128] + high[:, 128:] + nn(glo[rs], t[now, :, :128])) * scale
            if k < 2:
                hi, lo = split(power)
                t[later, rs, :128] = hi
                t[later, rs, 128:] = lo
                acc_ref[1, rs] = acc_ref[1, rs] + power * cs
            acc_ref[0, rs] = acc_ref[0, rs] + power * ce

    e_hi, e_lo = split(acc_ref[0])
    c_hi, c_lo = split(m["cg"][...])
    both = nn(c_hi, jnp.concatenate([e_hi, e_lo], axis=1))
    result = both[:, :128] + both[:, 128:] + nn(c_lo, e_hi)
    s_hi, s_lo = split(acc_ref[1] * s1)
    w_all = jnp.concatenate([m["wfull"][row_bits(r)] for r in range(8)], axis=1)
    w_hi, w_lo = split(w_all)
    both = nn(w_hi, jnp.concatenate([s_hi, s_lo], axis=1))
    out[...] = result + both[:, :128] + both[:, 128:] + nn(w_lo, s_hi)


def on_device(b_tensor, hcore, c_occ, c_virt, eps_occ, eps_virt):
    entries = float(c_virt.shape[1] * c_occ.shape[1])
    bag = scratch()
    return call(functools.partial(kernel, bag, entries), jax.ShapeDtypeStruct((384, 128), F32),
                [ANY, ANY, ANY, ANY, VM, VM], bag.shapes, 0,
                b_tensor, hcore, c_occ, c_virt, eps_virt, eps_occ[None, :])


def solution(mesh):
    placed = (
        P("aux", "row", "col"),
        P("row", ("aux", "col")),
        P("row", None),
        P(("aux", "col"), None),
        P("row"),
        P(("aux", "col")),
    )
    return jax.shard_map(
        on_device, mesh=mesh, in_specs=placed, out_specs=P(("aux", "col"), "row"), check_vma=False
    )
```

```python
import functools

import jax
import jax.numpy as jnp
from jax import lax
from jax.experimental import pallas as pl
from jax.experimental.pallas import tpu as pltpu
from jax.sharding import PartitionSpec as P

ROTATION_SCALE = 0.03
MESH = pl.DeviceIdType.MESH
F32 = jnp.float32
BF16 = jnp.bfloat16
XY = ("xa", "xb", "ya", "yb")
ROW = ("za", "zb", "cc")
VMEM_LIMIT = 62 * 1024 * 1024


class Place:
    def __init__(self):
        aux, row, col = (lax.axis_index(n) for n in ("aux", "row", "col"))
        y, xl = aux // 2, aux % 2
        z, core = row // 2, row % 2
        self.aux, self.row, self.col = aux, row, col
        self.bit = {
            "xa": (xl + col) % 2, "xb": col,
            "ya": (y + y // 2) % 2, "yb": y // 2,
            "za": (z + z // 2) % 2, "zb": z // 2,
            "cc": core,
        }
        self.partner = {
            "xa": (aux + 1 - 2 * xl, row, col),
            "xb": (aux + 1 - 2 * xl, row, 1 - col),
            "ya": (aux + 2 - 4 * (y % 2), row, col),
            "yb": (2 * (3 - y) + xl, row, col),
            "za": (aux, row + 2 - 4 * (z % 2), col),
            "zb": (aux, 2 * (3 - z) + core, col),
            "cc": (aux, row + 1 - 2 * core, col),
        }

    def greet(self, dims, swap=False):
        barrier = pltpu.get_barrier_semaphore()
        for d in dims:
            pl.semaphore_signal(barrier, inc=1, device_id=self.partner[d], device_id_type=MESH)
        if not swap:
            pl.semaphore_wait(barrier, len(dims))
            return

        @pl.when(self.aux != self.row)
        def _():
            pl.semaphore_signal(
                barrier, inc=1, device_id=(self.row, self.aux, self.col), device_id_type=MESH
            )
            pl.semaphore_wait(barrier, len(dims) + 1)

        @pl.when(self.aux == self.row)
        def _():
            pl.semaphore_wait(barrier, len(dims))


def xy_bits(aux, col):
    y, xl = aux // 2, aux % 2
    return ((xl + col) % 2, col, (y + y // 2) % 2, y // 2)


def row_bits(row):
    z, core = row // 2, row % 2
    return ((z + z // 2) % 2, z // 2, core)


class Sems:
    def __init__(self, send, recv):
        self.send, self.recv, self.n = send, recv, 0

    def take(self):
        n = self.n
        self.n += 1
        assert self.n <= self.send.shape[0]
        return self.send.at[n], self.recv.at[n]


def scatter_stream(place, work, axes, order, tail, recvs, sems):
    done = []
    for step, d in enumerate(order):
        def index(bit_of_d):
            return tuple(
                place.bit[a] if a in done else (bit_of_d if a == d else slice(None)) for a in axes
            ) + tail
        mine, theirs = index(place.bit[d]), index(1 - place.bit[d])
        s, r = sems.take()
        copy = pltpu.make_async_remote_copy(
            src_ref=work.at[theirs], dst_ref=recvs[step], send_sem=s, recv_sem=r,
            device_id=place.partner[d], device_id_type=MESH,
        )
        copy.start()
        yield
        copy.wait()
        work[mine] = work[mine] + recvs[step][...]
        done.append(d)


def gather_stream(place, full, axes, order, tail, sems):
    done = []
    for d in order:
        sl = tuple(slice(None) if a in done else place.bit[a] for a in axes) + tail
        s, r = sems.take()
        copy = pltpu.make_async_remote_copy(
            src_ref=full.at[sl], dst_ref=full.at[sl], send_sem=s, recv_sem=r,
            device_id=place.partner[d], device_id_type=MESH,
        )
        copy.start()
        yield
        copy.wait()
        done.append(d)


def drive(streams):
    streams = list(streams)
    while streams:
        alive = []
        for g in streams:
            try:
                next(g)
                alive.append(g)
            except StopIteration:
                pass
        streams = alive


def rotate(dims, k):
    return tuple(dims[k:]) + tuple(dims[:k])


XY_ORDERS = [("xa", "ya", "xb", "yb"), ("xb", "yb", "xa", "ya"),
             ("ya", "xa", "yb", "xb"), ("yb", "xb", "ya", "xa")]
ROW_ORDERS = [("cc", "za", "zb"), ("cc", "zb", "za")]


def recv_shapes(n, block):
    return [pltpu.VMEM((2,) * (n - 1 - t) + block, F32) for t in range(n)]


def dma(n):
    return pltpu.SemaphoreType.DMA((n,))


ANY = pl.BlockSpec(memory_space=pl.ANY)
VM = pl.BlockSpec(memory_space=pltpu.VMEM)


def call(kernel, outs, in_specs, scratch, cid, *args):
    return pl.pallas_call(
        kernel,
        out_shape=outs,
        in_specs=in_specs,
        out_specs=jax.tree.map(lambda _: VM, outs),
        scratch_shapes=scratch,
        compiler_params=pltpu.CompilerParams(
            collective_id=cid, has_side_effects=True, vmem_limit_bytes=VMEM_LIMIT
        ),
    )(*args)


def split(x):
    hi = x.astype(BF16)
    return hi, (x - hi.astype(F32)).astype(BF16)


def start_all(streams):
    for g in streams:
        next(g)
    return streams


def nt(a, b):
    return lax.dot_general(a, b, (((1,), (1,)), ((), ())), preferred_element_type=F32)


def nn(a, b):
    return jnp.dot(a, b, preferred_element_type=F32)


class Bag:
    def __init__(self):
        self.names, self.shapes = [], []

    def add(self, name, shape):
        self.names.append(name)
        self.shapes.append(shape)

    def recvs(self, name, n, block):
        for t, s in enumerate(recv_shapes(n, block)):
            self.add((name, t), s)

    def bind(self, refs):
        return dict(zip(self.names, refs))


LIMIT = 16383.0


def pack(parts):
    peak = jnp.max(jnp.abs(parts[0]), axis=0)
    for v in parts[1:]:
        peak = jnp.maximum(peak, jnp.max(jnp.abs(v), axis=0))
    peak = jnp.maximum(peak, 1e-30)
    n = [jnp.round(v * (LIMIT / peak)) for v in parts]
    words = []
    if len(n) >= 5:
        h3, h4 = jnp.floor(n[3] * (1 / 32)), jnp.floor(n[4] * (1 / 32))
        words += [n[0] * 1024 + h3, n[1] * 1024 + h4,
                  n[2] * 1024 + ((n[3] - 32 * h3) * 32 + (n[4] - 32 * h4) - 512)]
        n = n[5:]
    if n:
        h = jnp.floor(n[2] * (1 / 128))
        words += [n[0] * 256 + h, n[1] * 256 + (n[2] - 128 * h)]
    return peak * (1 / LIMIT), words


def unpack(scale, words):
    n = []
    if len(words) >= 3:
        n = [jnp.floor((w + 512) * (1 / 1024)) for w in words[:3]]
        h3, h4, rest = (w - 1024 * t for w, t in zip(words, n))
        rest = rest + 512
        l3 = jnp.floor(rest * (1 / 32))
        n += [h3 * 32 + l3, h4 * 32 + (rest - 32 * l3)]
        words = words[3:]
    if words:
        n5 = jnp.floor((words[0] + 128) * (1 / 256))
        n6 = jnp.floor(words[1] * (1 / 256))
        n += [n5, n6, (words[0] - 256 * n5) * 128 + (words[1] - 256 * n6)]
    return [v * scale for v in n]


def pack_into(ref, block):
    k = block.shape[-1] // 128
    block = block.reshape(-1, 8, block.shape[-1])
    m = block.shape[0]
    scale, words = pack([block[..., 128 * i: 128 * i + 128] for i in range(k)])
    ref[0] = scale
    for j, w in enumerate(words):
        ref[1 + j * m: 1 + (j + 1) * m] = w


def unpack_from(wire, m):
    words = [wire[1 + j * m: 1 + (j + 1) * m] for j in range((wire.shape[0] - 1) // m)]
    return unpack(wire[0], words)


PIECES = 4
R = 128 // PIECES
Q = R // 2
Z_ORDERS = (("za", "zb"), ("zb", "za"))
SCHEDULE = [
    1, 0, 4, 4, 1, 2, 0, 3, 1, 2, 0, 3, 1, 2, 0, 3, 1, 2, 0, 3, 4, 2, 1, 3,
    0, 4, 2, 5, 1, 6, 6, 6, 4, 6, 6, 3, 0, 1, 2, 3, 0, 5, 2, 1, 3, 0, 2, 1,
    5, 3, 0, 1, 2, 5, 3, 0, 2, 1, 1, 3, 0, 0, 2, 2, 8, 9, 7, 10, 3, 3, 8, 9,
    7, 10, 12, 8, 9, 7, 10, 12, 12, 9, 8, 7, 10, 11, 11, 11, 11, 11, 12, 12, 12, 11, 12, 12,
    11,
]


def scratch():
    bag, vm = Bag(), pltpu.VMEM
    bag.add("b", vm((2, 2, 768, 512), BF16))
    bag.add("c", vm((768, 1024), F32))
    bag.add("cg", vm((384, 1024), F32))
    bag.add("hc", vm((768, 384), F32))
    bag.add("ct", vm((2, PIECES, 2, 4, R, 768), BF16))
    bag.add("hch", vm((768, 384), BF16))
    bag.add("hcl", vm((768, 384), BF16))
    bag.add("cv", vm((2, 384, 256), F32))
    bag.add("cvh", vm((384, 5120), BF16))
    bag.add("cvl", vm((384, 5120), BF16))
    bag.add("ev", vm((2, 8, 640), F32))
    bag.add("eo", vm((128, 8), F32))
    for p in range(PIECES):
        bag.add(("xs", p), vm((4, R, 1024), F32))
        bag.add(("xr", p), vm((4, R, 1024), F32))
        bag.add(("xw", p), vm((2, 2, R, 1024), F32))
        bag.add(("xf", p), vm((2, 2, R, 1024), F32))
        bag.add(("yw", p), vm((4, 4, R, 384), F32))
        bag.add(("yb", p), vm((R, 384), F32))
        bag.add(("gw", p), vm((4, 4, Q, 640), F32))
        for s in range(2):
            for t, tiles in enumerate((4, 2)):
                bag.add(("xout", p, s, t), vm((5 * tiles + 1, 8, 128), F32))
                bag.add(("xin", p, s, t), vm((5 * tiles + 1, 8, 128), F32))
            bag.add(("xg", p, s), vm((2, 2, 11, 8, 128), F32))
        for s in range(2):
            for name, rows, lanes, words in (("y", R // 2, 384, 2), ("g", Q // 2, 640, 3)):
                packed = (3, words * rows // 2 + 1, 8, 128)
                bag.add((name + "out", p, s), vm(packed, F32))
                bag.add((name + "in", p, s), vm(packed, F32))
                bag.add((name + "raw", p, s), vm((3, rows, lanes), F32))
    for s in range(2):
        bag.recvs(("hrec", s), 3, (64, 384))
    bag.add("hw", vm((2, 2, 2, 128, 384), F32))
    bag.add("kc", vm((2, 2, 2, 2, PIECES, 7, 8, 128), F32))
    bag.add("own", vm((PIECES, Q, 640), F32))
    bag.add("kg", vm((2, 2, 2, PIECES, 2, Q, 384), F32))
    bag.add("win", vm((PIECES, Q, 384), F32))
    bag.add("gs", vm((2, 4, 80, 128), F32))
    bag.add("gs1", vm((2, 3, 80, 128), F32))
    bag.add("gs2", vm((2, 3, 80, 128), F32))
    bag.add("gfull", vm((2, 4, 4, 2, 7, 8, 128), F32))
    bag.add("wfull", vm((2, 2, 2, 384, 128), F32))
    bag.add("ghi", vm((1024, 1024), BF16))
    bag.add("glo", vm((1024, 1024), BF16))
    bag.add("t", vm((2, 1024, 256), BF16))
    bag.add("acc", vm((2, 1024, 128), F32))
    bag.add("local", dma(12))
    bag.add("send", dma(320))
    bag.add("recv", dma(320))
    return bag


def kernel(bag, entries, b_in, h_in, c_in, cv_in, ev_in, eo_in, out, *refs):
    m = bag.bind(refs)
    place = Place()
    sems = Sems(m["send"], m["recv"])
    core, col = place.row % 2, place.col
    other = 1 - core
    y, z = place.aux // 2, place.row // 2
    across = (place.aux, place.row, 1 - col)
    swapped = (2 * z + place.aux % 2, 2 * y + core, col)
    xmine = tuple(place.bit[d] for d in XY)
    rmine = tuple(place.bit[d] for d in ROW)
    zmine = rmine[:2]
    at = {"x": 2 * col + place.aux % 2, "y": y, "z": z}
    ring = {}
    for d in (1, 2, 3):
        xd, yd, zd = ((at[a] + d) % 4 for a in "xyz")
        ring["x", d] = (2 * y + xd % 2, place.row, xd // 2)
        ring["y", d] = (2 * yd + place.aux % 2, place.row, col)
        ring["z", d] = (place.aux, 2 * zd + core, col)

    def remote(src, dst, device):
        s, r = sems.take()
        return pltpu.make_async_remote_copy(
            src_ref=src, dst_ref=dst, send_sem=s, recv_sem=r,
            device_id=device, device_id_type=MESH)

    def load_c(k, zz):
        sl = pl.ds(pl.multiple_of(128 * (2 * zz + k), 128), 128)
        which = zz if k is core else 4 + zz
        return pltpu.make_async_copy(c_in.at[:, sl], m["c"].at[:, sl], m["local"].at[which])

    load_b = pltpu.make_async_copy(b_in, m["b"].at[0], m["local"].at[8])
    load_h = pltpu.make_async_copy(h_in, m["hc"], m["local"].at[9])

    def load_cv(k):
        return pltpu.make_async_copy(
            cv_in.at[:, pl.ds(256 * k, 256)], m["cv"].at[k % 2], m["local"].at[10 + k % 2])

    for zz in range(4):
        load_c(other, zz).start()
    load_b.start()
    for zz in range(4):
        load_c(core, zz).start()
    barrier = pltpu.get_barrier_semaphore()
    dims = XY + ROW
    greeted = [place.partner[d] for d in dims] + [across, ring["y", 2], ring["z", 2]]
    for device in greeted:
        pl.semaphore_signal(barrier, inc=1, device_id=device, device_id_type=MESH)

    @pl.when(y != z)
    def _():
        pl.semaphore_signal(barrier, inc=1, device_id=swapped, device_id_type=MESH)

    def turn_c(k, zz):
        load_c(k, zz).wait()
        sl = pl.ds(pl.multiple_of(128 * (2 * zz + k), 128), 128)
        hi, lo = split(m["c"][:, sl].T)
        m["ct"][k, :, 0, zz] = hi.reshape(PIECES, R, 768)
        m["ct"][k, :, 1, zz] = lo.reshape(PIECES, R, 768)

    def x_part(p, k, out_ref):
        both = m["ct"][k, p].reshape(8 * R, 768)
        for q in range(2):
            acc = nn(both, m["b"][0, q])
            out_ref[..., pl.ds(512 * q, 512)] = (acc[:4 * R] + acc[4 * R:]).reshape(
                out_ref.shape[:-1] + (512,))

    for zz in range(4):
        turn_c(other, zz)
    load_b.wait()
    x_part(0, other, m["xs", 0])

    @pl.when(y != z)
    def _():
        pl.semaphore_wait(barrier, len(greeted) + 1)

    @pl.when(y == z)
    def _():
        pl.semaphore_wait(barrier, len(greeted))

    xc = [remote(m["xs", p], m["xr", p], place.partner["cc"]) for p in range(PIECES)]
    xc[0].start()
    load_h.start()
    load_cv(0).start()
    load_cv(1).start()
    for zz in range(4):
        turn_c(core, zz)
    b_copy = remote(m["b"].at[0], m["b"].at[1], place.partner["cc"])
    ev_copy = remote(m["ev"].at[0], m["ev"].at[1], across)
    for p in range(PIECES):
        x_part(p, core, m["xw", p])
        if p + 1 < PIECES:
            x_part(p + 1, other, m["xs", p + 1])
            xc[p + 1].start()
    b_copy.start()

    tasks, finished, have_b, scales = {}, set(), [], []

    def advance(n):
        if n in tasks:
            try:
                next(tasks[n])
            except StopIteration:
                del tasks[n]
                finished.add(n)

    def complete(n):
        while n in tasks:
            advance(n)

    def launch(n, g):
        tasks[n] = g
        advance(n)

    def steps(streams, n):
        for _ in range(n - 1):
            yield
            for g in streams:
                next(g)
        yield
        drive(streams)

    def x_scatter(p, s):
        work, rows, done = m["xw", p], pl.ds(16 * s, 16), []
        for t, d in enumerate(Z_ORDERS[s]):
            def index(bit):
                return tuple(place.bit[a] if a in done else (bit if a == d else slice(None))
                             for a in ("za", "zb")) + (rows,)
            mine, theirs = index(place.bit[d]), index(1 - place.bit[d])
            pack_into(m["xout", p, s, t], work[theirs])
            copy = remote(m["xout", p, s, t], m["xin", p, s, t], place.partner[d])
            copy.start()
            yield
            copy.wait()
            for k, v in enumerate(unpack_from(m["xin", p, s, t][...], (4, 2)[t])):
                spot = mine + (pl.ds(128 * k, 128),)
                work[spot] = work[spot] + v.reshape((2, 16, 128) if t == 0 else (16, 128))
            done.append(d)

    def two_rings(work, s, rows, out, wire, raw):
        first, second = ("x", "y") if s == 0 else ("y", "x")
        lanes = work.shape[-1]
        tiles = (rows.size * 4) // 8

        def index(i, j):
            return ((i, j) if s == 0 else (j, i)) + (rows,)

        copies = []
        for d in (1, 2, 3):
            pack_into(out.at[d - 1], work[index((at[first] + d) % 4, slice(None))])
            copies.append(remote(out.at[d - 1], wire.at[d - 1], ring[first, d]))
            copies[-1].start()
        yield
        mine = index(at[first], slice(None))
        for c in copies:
            c.wait()
        got = [unpack_from(wire[d], tiles) for d in range(3)]
        for k in range(lanes // 128):
            place_k = mine + (pl.ds(128 * k, 128),)
            v = (got[0][k] + got[1][k]) + got[2][k]
            work[place_k] = work[place_k] + v.reshape(4, rows.size, 128)
        copies = []
        for d in (1, 2, 3):
            copies.append(remote(work.at[index(at[first], (at[second] + d) % 4)],
                                 raw.at[d - 1], ring[second, d]))
            copies[-1].start()
        yield
        for c in copies:
            c.wait()
        mine = index(at[first], at[second])
        work[mine] = (work[mine] + raw[0]) + (raw[1] + raw[2])

    def ring_gather(full, index, axis):
        copies = [remote(full.at[index], full.at[index], ring[axis, d]) for d in (1, 2, 3)]
        for c in copies:
            c.start()
        return copies

    def wait_all(copies):
        for c in copies:
            c.wait()

    def piece(p):
        yield
        xc[p].wait()
        m["xw", p][...] = m["xw", p][...] + m["xr", p][...].reshape(2, 2, R, 1024)
        streams = start_all([x_scatter(p, s) for s in range(2)])
        yield from steps(streams, 2)
        for s in range(2):
            pack_into(m["xg", p, s].at[zmine], m["xw", p][zmine + (pl.ds(16 * s, 16),)])
        streams = start_all([
            gather_stream(place, m["xg", p, s], ("za", "zb"), Z_ORDERS[s][::-1], (), sems)
            for s in range(2)])
        yield from steps(streams, 2)
        for s in range(2):
            for i in range(4):
                for k, v in enumerate(unpack_from(m["xg", p, s][i // 2, i % 2], 2)):
                    m["xf", p][i // 2, i % 2, pl.ds(16 * s, 16), pl.ds(128 * k, 128)] = (
                        v.reshape(16, 128))
        if not have_b:
            b_copy.wait()
            have_b.append(p)
        hi, lo = split(m["xf", p][...].reshape(4 * R, 1024))
        both = jnp.concatenate([hi, lo], axis=0)
        for side in range(2):
            xlo = core if side == 0 else other
            for half in range(2):
                rows = pl.ds(384 * half, 384)
                acc = nt(both[:, :512], m["b"][side, 0, rows])
                acc += nt(both[:, 512:], m["b"][side, 1, rows])
                acc = acc[:4 * R] + acc[4 * R:]
                for zz in range(4):
                    m["yw", p][2 * half + xlo, zz] = acc[R * zz: R * zz + R]
        streams = start_all([
            two_rings(m["yw", p], s, pl.ds(R // 2 * s, R // 2),
                      m["yout", p, s], m["yin", p, s], m["yraw", p, s]) for s in range(2)])
        yield from steps(streams, 2)
        swap = remote(m["yw", p].at[at["x"], y], m["yb", p], swapped)

        @pl.when(y != z)
        def _():
            swap.start()

        @pl.when(y == z)
        def _():
            m["yb", p][...] = m["yw", p][at["x"], y]

        yield
        complete(4)
        complete(6)

        @pl.when(y != z)
        def _():
            swap.wait()

        image = m["hw"][rmine + (pl.ds(R * p, R),)] - m["yb", p][...]
        hi, lo = split(image)
        both = jnp.concatenate([hi, lo], axis=0)
        for aux in range(8):
            sl = pl.ds(640 * aux, 640)
            acc = nn(both, m["cvh"][:, sl])
            acc = acc[:R] + acc[R:] + nn(hi, m["cvl"][:, sl])
            for c in range(2):
                m["gw", p][2 * c + aux % 2, aux // 2] = acc[Q * c: Q * c + Q]
        streams = start_all([
            two_rings(m["gw", p], s, pl.ds(Q // 2 * s, Q // 2),
                      m["gout", p, s], m["gin", p, s], m["graw", p, s]) for s in range(2)])
        yield from steps(streams, 2)
        ev = m["ev"][0, 0:1] + m["ev"][1, 0:1]
        eo = m["eo"][pl.ds(R * p + Q * col, Q), 0:1]
        m["own"][p] = m["gw", p][at["x"], y] / (ev - eo)
        mine = pl.ds(pl.multiple_of(256 * col, 128), 384)
        theirs = pl.ds(pl.multiple_of(256 - 256 * col, 128), 384)
        m["kg"][rmine + (p, col)] = m["own"][p, :, mine]
        m["win"][p] = m["own"][p, :, theirs]
        window = remote(m["win"].at[p], m["kg"].at[rmine + (p, col)], across)
        window.start()
        launch(7 + p, gather_piece(p))
        yield
        window.wait()
        copies = ring_gather(m["kg"], rmine + (p,), "z")
        yield
        wait_all(copies)
        block = m["kg"].at[:, :, core, p]
        copy = remote(block, block, place.partner["cc"])
        copy.start()
        yield
        copy.wait()

    def gather_piece(p):
        pack_into(m["kc"].at[xmine + (p,)], m["own"][p])
        yield from steps(start_all([
            gather_stream(place, m["kc"], XY, XY_ORDERS[p][::-1], (p,), sems)]), 4)

    def h_task():
        yield
        load_h.wait()
        hi, lo = split(m["hc"][...])
        m["hch"][...] = hi
        m["hcl"][...] = lo
        for r in range(8):
            chi = m["ct"][r % 2, :, 0, r // 2].reshape(128, 768)
            clo = m["ct"][r % 2, :, 1, r // 2].reshape(128, 768)
            m["hw"][row_bits(r)] = (
                nn(chi, m["hch"][...]) + nn(clo, m["hch"][...]) + nn(chi, m["hcl"][...]))
            if r == 3:
                yield
        yield from steps(start_all([
            scatter_stream(place, m["hw"], ROW, ROW_ORDERS[s], (pl.ds(64 * s, 64),),
                           [m[("hrec", s), t] for t in range(3)], sems) for s in range(2)]), 3)

    def c_rows():
        source = row_bits(place.aux)
        yield

        @pl.when(place.aux == place.row)
        def _():
            m["cg"][...] = m["c"][pl.ds(pl.multiple_of(384 * col, 384), 384)]

        differs = {d: (place.bit[d] - source[ROW.index(d)]) * (place.bit[d] - source[ROW.index(d)])
                   for d in ROW}
        for k in range(3):
            copies = []
            for s in range(2):
                order = Z_ORDERS[s] + ("cc",)
                later = sum((differs[d] for d in order[k + 1:]), 0)
                half = m["cg"].at[pl.ds(192 * s, 192)]
                copy = remote(half, half, place.partner[order[k]])
                sends = later + differs[order[k]] == 0
                takes = later + (1 - differs[order[k]]) == 0
                copies.append((copy, sends, takes))

                @pl.when(sends)
                def _():
                    copy.start()

            yield
            for copy, sends, takes in copies:
                @pl.when(sends)
                def _():
                    copy.wait_send()

                @pl.when(takes)
                def _():
                    copy.wait_recv()

    def cv_task():
        m["ev"][0] = jnp.zeros((8, 640), F32)
        value = jnp.broadcast_to(ev_in[...][None, :], (8, 320))

        @pl.when(col == 0)
        def _():
            m["ev"][0, :, :320] = value

        @pl.when(col == 1)
        def _():
            m["ev"][0, :, 320:] = value

        ev_copy.start()
        m["eo"][...] = jnp.broadcast_to(eo_in[...], (8, 128)).T
        for k in range(20):
            if k % 4 == 0:
                yield
            load_cv(k).wait()
            hi, lo = split(m["cv"][k % 2])
            m["cvh"][:, pl.ds(256 * k, 256)] = hi
            m["cvl"][:, pl.ds(256 * k, 256)] = lo
            if k + 2 < 20:
                load_cv(k + 2).start()
        ev_copy.wait()

    def w_task():
        w = 0.0
        for aux in range(8):
            if aux % 2 == 0:
                yield
            rows = []
            for p in range(PIECES):
                for c in range(2):
                    parts = unpack_from(m["kc"][xy_bits(aux, c) + (p,)], 2)
                    rows.append(jnp.concatenate([v.reshape(Q, 128) for v in parts], axis=1))
            kh, kl = split(jnp.concatenate(rows, axis=0))
            ch, cl = m["cvh"][:, pl.ds(640 * aux, 640)], m["cvl"][:, pl.ds(640 * aux, 640)]
            both = nt(ch, jnp.concatenate([kh, kl], axis=0))
            w = w + both[:, :128] + both[:, 128:] + nt(cl, kh)
        m["wfull"][rmine] = w
        yield from steps(start_all([
            gather_stream(place, m["wfull"], ROW, Z_ORDERS[s] + ("cc",),
                          (pl.ds(192 * s, 192),), sems) for s in range(2)]), 3)

    def place_blocks(r):
        column = jnp.concatenate(
            [v.reshape(16, 128) for s in range(2) for i in range(4)
             for v in unpack_from(m["gfull"][s, i, r // 2, r % 2], 2)], axis=0)
        for k in range(5):
            block = column[128 * k: 128 * k + 128]
            i = (r + k) % 8
            hi, lo = split(block)
            m["ghi"][pl.ds(128 * i, 128), pl.ds(128 * r, 128)] = hi
            m["glo"][pl.ds(128 * i, 128), pl.ds(128 * r, 128)] = lo
            if 0 < k < 4:
                hi, lo = split(block.T)
                m["ghi"][pl.ds(128 * r, 128), pl.ds(128 * i, 128)] = hi
                m["glo"][pl.ds(128 * r, 128), pl.ds(128 * i, 128)] = lo
        return column[:128]

    def g_task():
        lanes = lax.broadcasted_iota(jnp.int32, (128, 384), 1)
        rhs = m["kg"][rmine].reshape(128, 384)
        rh, rl = split(jnp.where(lanes >= 128 * col, rhs, 0.0))
        accs = []
        for k in range(5):
            lh, ll = split(m["kg"][row_bits((place.row + k) % 8)].reshape(128, 384))
            accs.append(nt(lh, rh) + nt(lh, rl) + nt(ll, rh))
        acc = jnp.concatenate(accs, axis=0)
        m["gs"][...] = acc.reshape(2, 4, 80, 128)
        firsts, seconds = ("x", "y"), ("y", "x")
        copies = []
        for s, axis in enumerate(firsts):
            for d in (1, 2, 3):
                copies.append(remote(m["gs"].at[s, (at[axis] + d) % 4], m["gs1"].at[s, d - 1],
                                     ring[axis, d]))
                copies[-1].start()
        yield
        wait_all(copies)
        copies = []
        for s, axis in enumerate(firsts):
            mine = (s, at[axis])
            m["gs"][mine] = ((m["gs"][mine] + m["gs1"][s, 0])
                             + (m["gs1"][s, 1] + m["gs1"][s, 2]))
            for d in (1, 2, 3):
                copies.append(remote(m["gs"].at[mine], m["gs2"].at[s, d - 1],
                                     ring[seconds[s], d]))
                copies[-1].start()
        yield
        wait_all(copies)
        copies = []
        for s, axis in enumerate(firsts):
            total = ((m["gs"][s, at[axis]] + m["gs2"][s, 0])
                     + (m["gs2"][s, 1] + m["gs2"][s, 2]))
            scale, words = pack([total[16 * i: 16 * i + 16].reshape(2, 8, 128) for i in range(5)])
            mine = m["gfull"].at[s, at[axis], z, core]
            mine[0] = scale
            for i, w in enumerate(words):
                mine[1 + 2 * i: 3 + 2 * i] = w
            copies += ring_gather(m["gfull"], (s, at[axis], z, core), "z")
        yield
        wait_all(copies)
        copies = []
        for s, axis in enumerate(firsts):
            copies += ring_gather(m["gfull"], (s, at[axis], slice(None), core), axis)
        yield
        wait_all(copies)
        block = m["gfull"].at[:, :, :, core]
        copy = remote(block, block, place.partner["cc"])
        copy.start()
        yield
        copy.wait()
        ghi, glo, t, acc_ref = m["ghi"], m["glo"], m["t"], m["acc"]
        r128 = lax.broadcasted_iota(jnp.int32, (128, 128), 0)
        l128 = lax.broadcasted_iota(jnp.int32, (128, 128), 1)
        total = jnp.zeros((128, 128), F32)
        for r in range(8):
            total = total + jnp.where(r128 == l128, place_blocks(r), 0.0)
        meansq = jnp.sum(total, axis=(0, 1), keepdims=True) / entries
        s1 = ROTATION_SCALE / jnp.sqrt(meansq + 1e-06)
        s2 = s1 * s1
        here = pl.ds(pl.multiple_of(128 * place.row, 128), 128)
        t[0, :, :128] = ghi[:, here]
        t[0, :, 128:] = glo[:, here]
        rows8 = lax.broadcasted_iota(jnp.int32, (1024, 128), 0)
        lanes8 = lax.broadcasted_iota(jnp.int32, (1024, 128), 1)
        g1 = (ghi[:, here].astype(F32) + glo[:, here].astype(F32)) * s2
        eye = jnp.where(rows8 == lanes8 + 128 * place.row, 1.0, 0.0)
        acc_ref[0] = eye - g1 * 0.5
        acc_ref[1] = eye - g1 * (1.0 / 6.0)
        yield
        coeff = [(1.0 / 24.0, 1.0 / 120.0), (-1.0 / 720.0, -1.0 / 5040.0), (1.0 / 40320.0, 0.0)]
        for k, (ce, cs) in enumerate(coeff):
            now, later = k % 2, (k + 1) % 2
            scale = s2 * s2 if k == 0 else s2

            @pl.loop(0, 4)
            def _(i):
                rs = pl.ds(pl.multiple_of(i * 256, 256), 256)
                high = nn(ghi[rs], t[now])
                power = (high[:, :128] + high[:, 128:] + nn(glo[rs], t[now, :, :128])) * scale
                if k < 2:
                    hi, lo = split(power)
                    t[later, rs, :128] = hi
                    t[later, rs, 128:] = lo
                    acc_ref[1, rs] = acc_ref[1, rs] + power * cs
                acc_ref[0, rs] = acc_ref[0, rs] + power * ce

            if k < 2:
                yield
        scales.append(s1)

    for p in range(PIECES):
        launch(p, piece(p))
    launch(4, h_task())
    launch(5, c_rows())
    launch(6, cv_task())

    def follow():
        if 12 not in tasks and 12 not in finished and finished.issuperset(range(PIECES)):
            launch(12, g_task())
        if 11 not in tasks and 11 not in finished and finished.issuperset(range(7, 7 + PIECES)):
            launch(11, w_task())

    for n in SCHEDULE:
        advance(n)
        follow()
    while tasks:
        for n in sorted(tasks):
            advance(n)
        follow()

    acc_ref = m["acc"]
    e_hi, e_lo = split(acc_ref[0])
    c_hi, c_lo = split(m["cg"][...])
    both = nn(c_hi, jnp.concatenate([e_hi, e_lo], axis=1))
    result = both[:, :128] + both[:, 128:] + nn(c_lo, e_hi)
    s_hi, s_lo = split(acc_ref[1] * scales[0])
    w_all = jnp.concatenate([m["wfull"][row_bits(r)] for r in range(8)], axis=1)
    w_hi, w_lo = split(w_all)
    both = nn(w_hi, jnp.concatenate([s_hi, s_lo], axis=1))
    out[...] = result + both[:, :128] + both[:, 128:] + nn(w_lo, s_hi)


def on_device(b_tensor, hcore, c_occ, c_virt, eps_occ, eps_virt):
    entries = float(c_virt.shape[1] * c_occ.shape[1])
    bag = scratch()
    return call(functools.partial(kernel, bag, entries), jax.ShapeDtypeStruct((384, 128), F32),
                [ANY, ANY, ANY, ANY, VM, VM], bag.shapes, 0,
                b_tensor, hcore, c_occ, c_virt, eps_virt, eps_occ[None, :])


def solution(mesh):
    placed = (
        P("aux", "row", "col"),
        P("row", ("aux", "col")),
        P("row", None),
        P(("aux", "col"), None),
        P("row"),
        P(("aux", "col")),
    )
    return jax.shard_map(
        on_device, mesh=mesh, in_specs=placed, out_specs=P(("aux", "col"), "row"), check_vma=False
    )
```
